128 devices in a mesh: cache: 16 (over x, z), cls: 8 (over y, core).
Axes of the slice: x: 4, y: 4, z: 4, core: 2. Of those that a mesh axis runs over, the one named last changes fastest.
Arguments:
- queries: bfloat16 [4096, 1024], P(('cache', 'cls')), may hold values from -14 to 14
- cache_keys: bfloat16 [163840, 1024], P('cache'), may hold values from -6 to 6
- labels: int32 [163840], P('cache'), may hold values from 0 to 10239, as said below
- prototypes: bfloat16 [10240, 1024], P('cls'), may hold values from -1 to 1
Outputs:
- log_probs: float32 [4096, 10240], P('cache', 'cls')
The draws below stay inside these ranges and needn't reach their ends.
Inputs may be any that keep to these rules, and one draw needn't show every extreme that they name: Split the classes into 16 aligned blocks of 640; the 10240 cached shapes of one index of cache hold at most 1280 labels of one block, and one block, drawn from the seed, holds exactly 1280 labels of every index of cache.
All inputs are finite; a program needn't handle non-finite values.
Results may differ from the reference program's by a relative error of at most 0.0009.
The reference program's roundings to bfloat16 on the way count: a program that leaves them out, or rounds other values in their place, can miss the bound.
Values may be sent and summed in bfloat16 or wider, within the bound.
No kernel may reach another device: no remote copies, remote signals or barrier semaphores. Data moves between devices by JAX's collectives and lax.ppermute only.
A program may use at most 192 MiB of HBM per device.

```python
import jax
import jax.numpy as jnp
from jax import lax

D = 1024
CACHE_DEV = 10240
C = 10240
NC = 163840
NQ = 4096
CB = 640
CAP = 1280
N_CACHE = 16


def draw_queries(key, part):
    base_key = jax.random.fold_in(key, 1)
    values = jnp.clip(jax.random.normal(base_key, (NQ, D), jnp.float32), -6.0, 6.0)
    return values.astype(jnp.bfloat16)


def draw_prototypes(key, part):
    base_key = jax.random.fold_in(key, 2)
    values = 0.035 * jnp.clip(jax.random.normal(base_key, (C, D), jnp.float32), -6.0, 6.0)
    return values.astype(jnp.bfloat16)


def draw_labels(key, part):
    blocks = NC // CACHE_DEV
    remaining = CACHE_DEV - CAP
    busiest = jax.random.randint(jax.random.fold_in(key, 11), (), 0, blocks)
    shard_keys = jax.random.split(jax.random.fold_in(key, 12), blocks)

    def one_shard(shard_key):
        key_one, key_two, key_three, key_four = jax.random.split(shard_key, 4)
        ordering = jax.random.permutation(key_one, blocks)
        where_busy = jnp.argmax((ordering == busiest).astype(jnp.int32))
        ordering = ordering.at[where_busy].set(ordering[0]).at[0].set(busiest)
        weights = jax.random.randint(key_two, (blocks,), 32, 64).at[0].set(0)
        shares = remaining * weights // jnp.maximum(jnp.sum(weights), 1)
        missing = remaining - jnp.sum(shares)
        rank_ids = jnp.arange(blocks)
        shares = shares + ((rank_ids >= 1) & (rank_ids <= missing)).astype(jnp.int32)
        counts_by_rank = shares.at[0].set(CAP)
        counts = jnp.zeros((blocks,), jnp.int32).at[ordering].set(counts_by_rank)
        bounds = jnp.cumsum(counts)
        row_ids = jnp.arange(CACHE_DEV)
        block_of_row = jnp.sum((row_ids[:, None] >= bounds[None, :]).astype(jnp.int32), axis=1)
        within = jax.random.randint(key_four, (CACHE_DEV,), 0, CB)
        starts = (bounds - counts).astype(jnp.int32)
        within = within.at[starts].set(0, mode='drop')
        within = within.at[(bounds - 1).astype(jnp.int32)].set(CB - 1, mode='drop')
        ordered = (block_of_row * CB + within).astype(jnp.int32)
        shuffle = jax.random.permutation(key_three, CACHE_DEV)
        return ordered[shuffle]
    return jax.vmap(one_shard)(shard_keys).reshape(NC)


def block_scale(stream_key, shape, cuts, least, top_value):
    def one(dim, blocks):
        steps = jax.random.uniform(jax.random.fold_in(jax.random.fold_in(stream_key, 6), dim), (blocks,), jnp.float32, least / len(cuts), top_value / len(cuts))
        return jnp.repeat(jnp.exp(steps), shape[dim] // blocks).reshape((-1,) + (1,) * (len(shape) - dim - 1))

    gain = one(*cuts[0])
    for cut in cuts[1:]:
        gain = gain * one(*cut)
    return gain


def gaussian(stream_key, shape, scale, bound, pieces=(), held_as=jnp.bfloat16):
    loudness = block_scale(stream_key, shape, pieces, -0.22, 0.18) if pieces else 1.0
    array = jax.random.normal(stream_key, shape, jnp.float32) * scale * loudness
    return jnp.minimum(jnp.maximum(array, -bound), bound).astype(held_as)


def setup_inputs(seed: int = 0) -> dict:
    key_of = jax.random.split(jax.random.key(seed), 5)
    return {
        "queries": draw_queries(jax.random.fold_in(key_of[4], 71), 0),
        "cache_keys": gaussian(key_of[1], (NC, D), 1.0, 6.0, ((0, 16),)),
        "labels": draw_labels(jax.random.fold_in(key_of[4], 71), 0),
        "prototypes": draw_prototypes(jax.random.fold_in(key_of[4], 71), 0),
    }


text_scale = 100.0
epsilon = 1e-06

def unit_rows(matrix):
    widened = matrix.astype(jnp.float32)
    return (widened / jnp.sqrt(lax.optimization_barrier(jnp.sum(widened * widened, axis=1, keepdims=True)) + epsilon)).astype(jnp.bfloat16)

def reference(queries, cache_keys, labels, prototypes):
    sharpness = float(D) ** 0.5
    unit_queries = unit_rows(queries)
    key_blocks = unit_rows(cache_keys).reshape(N_CACHE, CACHE_DEV, D)
    label_blocks = labels.reshape(N_CACHE, CACHE_DEV)

    def add_shard(running, inputs):
        key_block, label_block = inputs
        cosine = jnp.dot(key_block, unit_queries.T, preferred_element_type=jnp.float32)
        scores = jnp.exp(sharpness * cosine).astype(jnp.bfloat16)
        scores = lax.optimization_barrier(scores).astype(jnp.float32)
        return (running + jax.ops.segment_sum(scores, label_block, num_segments=C), None)
    cache_logits, unused = lax.scan(add_shard, jnp.zeros((C, NQ), jnp.float32), (key_blocks, label_blocks))
    text_logits = text_scale * jnp.dot(unit_queries, prototypes.T, preferred_element_type=jnp.float32)
    logits = text_logits + cache_logits.T
    highest = lax.optimization_barrier(jnp.max(logits, axis=1, keepdims=True))
    return logits - highest - jnp.log(lax.optimization_barrier(jnp.sum(jnp.exp(logits - highest), axis=1, keepdims=True)))
```

```python
import functools

import jax
import jax.numpy as jnp
from jax import lax
from jax.experimental import pallas as pl
from jax.experimental.pallas import tpu as pltpu
from jax.sharding import PartitionSpec as P

text_scale = 100.0
epsilon = 1e-06
SIDE = 4
CB = 640
CAP = 1280
QT = 256
KT = 256
TAIL = 16
VMEM_LIMIT = 40 * 1024 * 1024


def params():
    return pltpu.CompilerParams(vmem_limit_bytes=VMEM_LIMIT)


def unit_rows(matrix):
    widened = matrix.astype(jnp.float32)
    return (widened / jnp.sqrt(jnp.sum(widened * widened, axis=1, keepdims=True) + epsilon)).astype(
        jnp.bfloat16
    )


def prepare_kernel(rows_ref, labels_ref, unit_ref, hot_ref):
    unit_ref[...] = unit_rows(rows_ref[...])
    classes = lax.broadcasted_iota(jnp.int32, (KT, CB), 1)
    hot_ref[...] = jnp.where(labels_ref[...] == classes, 1.0, 0.0).astype(jnp.bfloat16)


def prepare(rows, labels):
    count, width = rows.shape
    return pl.pallas_call(
        prepare_kernel,
        grid=(count // KT,),
        in_specs=[
            pl.BlockSpec((KT, width), lambda i: (i, 0)),
            pl.BlockSpec((KT, 1), lambda i: (i, 0)),
        ],
        out_specs=[
            pl.BlockSpec((KT, width), lambda i: (i, 0)),
            pl.BlockSpec((KT, CB), lambda i: (i, 0)),
        ],
        out_shape=[
            jax.ShapeDtypeStruct((count, width), jnp.bfloat16),
            jax.ShapeDtypeStruct((count, CB), jnp.bfloat16),
        ],
        compiler_params=params(),
        cost_estimate=pl.CostEstimate(flops=count * width * 4, bytes_accessed=count * width * 6, transcendentals=count),
        name="prepare",
    )(rows, labels)


def diagonal():
    shape = (QT, QT)
    return lax.broadcasted_iota(jnp.int32, shape, 0) == lax.broadcasted_iota(jnp.int32, shape, 1)


def encode(values, message_ref, tile, tail_row):
    largest = jnp.maximum(jnp.max(values, axis=1, keepdims=True), 1e-30)
    exponent = jnp.ceil(jnp.log2(largest) - 14.99)
    codes = (values * jnp.exp2(-exponent) + 0.5).astype(jnp.int32)
    message_ref[pl.ds(tile * QT, QT), :] = codes.astype(jnp.int16)
    along = jnp.sum(jnp.where(diagonal(), exponent, 0.0), axis=0, keepdims=True)
    shape = (TAIL, QT)
    old = message_ref[tail_row : tail_row + TAIL, :QT].astype(jnp.int32)
    new = jnp.broadcast_to(along, shape).astype(jnp.int32)
    at = lax.broadcasted_iota(jnp.int32, shape, 0) == tile
    message_ref[tail_row : tail_row + TAIL, :QT] = jnp.where(at, new, old).astype(jnp.int16)


def clear_tail(message_ref, tail_row):
    message_ref[tail_row : tail_row + TAIL, :] = jnp.zeros((TAIL, CB), jnp.int16)


def decode(message_ref, tile, tail_row):
    shape = (TAIL, QT)
    tail = message_ref[tail_row : tail_row + TAIL, :QT].astype(jnp.float32)
    at = lax.broadcasted_iota(jnp.int32, shape, 0) == tile
    along = jnp.sum(jnp.where(at, tail, 0.0), axis=0, keepdims=True)
    exponent = jnp.sum(jnp.where(diagonal(), along, 0.0), axis=1, keepdims=True)
    codes = message_ref[pl.ds(tile * QT, QT), :].astype(jnp.float32)
    return codes * jnp.exp2(exponent)


HALF = 2 * QT
HALF_MSG = jax.ShapeDtypeStruct((HALF + TAIL, CB), jnp.int16)
TILE_MSG = jax.ShapeDtypeStruct((QT + TAIL, CB), jnp.int16)


def tile_sums(tiles, q_ref, keys_ref, hot_ref, total_ref):
    sharpness = float(q_ref.shape[-1]) ** 0.5
    total_ref[...] = jnp.zeros_like(total_ref)

    def step(t, carry):
        at = pl.ds(t * KT, KT)
        cosine = lax.dot_general(
            q_ref[0], keys_ref[at, :], (((1,), (1,)), ((), ())), preferred_element_type=jnp.float32
        )
        scores = jnp.exp(sharpness * cosine).astype(jnp.bfloat16)
        total_ref[...] += jnp.dot(scores, hot_ref[at, :], preferred_element_type=jnp.float32)
        return carry

    lax.fori_loop(0, tiles, step, 0)


def sums(targets, messages, raws, plan, queries, keys, hots):
    steps, width = len(targets), keys.shape[1]
    out_shape = [HALF_MSG] * messages
    out_specs = [pl.BlockSpec(HALF_MSG.shape, lambda i, p: (0, 0))] * messages
    if raws:
        out_shape.append(jax.ShapeDtypeStruct((raws, QT, CB), jnp.float32))
        out_specs.append(pl.BlockSpec((raws, QT, CB), lambda i, p: (0, 0, 0)))

    def kernel(plan_ref, q_ref, keys_ref, hot_ref, *rest):
        outs, total_ref = rest[:-1], rest[-1]
        step = pl.program_id(0)
        tile_sums(plan_ref[2, step], q_ref, keys_ref, hot_ref, total_ref)
        for index, (out, tile) in enumerate(targets):
            @pl.when(step == index)
            def _(out=out, tile=tile):
                if out < 0:
                    outs[-1][tile] = total_ref[...]
                else:
                    if tile == 0:
                        clear_tail(outs[out], HALF)
                    encode(total_ref[...], outs[out], tile, HALF)

    return pl.pallas_call(
        kernel,
        grid_spec=pltpu.PrefetchScalarGridSpec(
            num_scalar_prefetch=1,
            grid=(steps,),
            in_specs=[
                pl.BlockSpec((1, QT, width), lambda i, p: (p[0, i], 0, 0)),
                pl.BlockSpec((CAP, width), lambda i, p: (p[1, i], 0)),
                pl.BlockSpec((CAP, CB), lambda i, p: (p[1, i], 0)),
            ],
            out_specs=out_specs,
            scratch_shapes=[pltpu.VMEM((QT, CB), jnp.float32)],
        ),
        out_shape=out_shape,
        compiler_params=params(),
        cost_estimate=pl.CostEstimate(
            flops=steps * 2 * QT * CAP * (width + CB),
            bytes_accessed=2 * CAP * (width + CB) * 2,
            transcendentals=steps * QT * CAP,
        ),
        name="sums",
    )(plan, queries, keys, hots)


def forward(raw, arrived):
    count = len(arrived)

    def kernel(raw_ref, *rest):
        for m in range(count):
            source, target = rest[m], rest[count + m]
            clear_tail(target, HALF)

            def body(t, carry, m=m, source=source, target=target):
                encode(raw_ref[2 * m + t] + decode(source, t, HALF), target, t, HALF)
                return carry

            lax.fori_loop(0, 2, body, 0)

    return pl.pallas_call(
        kernel,
        out_shape=[HALF_MSG] * count,
        compiler_params=params(),
        cost_estimate=pl.CostEstimate(flops=10 * count * HALF * CB, bytes_accessed=8 * count * HALF * CB, transcendentals=0),
        name="forward",
    )(raw, *arrived)


def turn(place, raw, first_a, first_b, second_a, second_b):
    def kernel(place_ref, raw_ref, fa, fb, sa, sb, own_ref, plus_ref, far_ref, minus_ref, total_ref):
        for k, out in enumerate((None, plus_ref, far_ref, minus_ref)):
            tile = lax.rem(place_ref[0] + k, SIDE)

            @pl.when(tile < 2)
            def _():
                total_ref[...] = raw_ref[tile] + decode(fa, tile, HALF) + decode(fb, tile, HALF)

            @pl.when(tile >= 2)
            def _():
                total_ref[...] = raw_ref[tile] + decode(sa, tile - 2, HALF) + decode(sb, tile - 2, HALF)

            if out is None:
                own_ref[...] = total_ref[...]
            else:
                clear_tail(out, QT)
                encode(total_ref[...], out, 0, QT)

    vmem = pl.BlockSpec(memory_space=pltpu.VMEM)
    return pl.pallas_call(
        kernel,
        in_specs=[pl.BlockSpec(memory_space=pltpu.SMEM)] + [vmem] * 5,
        out_specs=[vmem] * 4,
        out_shape=[jax.ShapeDtypeStruct((QT, CB), jnp.float32), TILE_MSG, TILE_MSG, TILE_MSG],
        scratch_shapes=[pltpu.VMEM((QT, CB), jnp.float32)],
        compiler_params=params(),
        cost_estimate=pl.CostEstimate(flops=40 * QT * CB, bytes_accessed=40 * QT * CB, transcendentals=0),
        name="turn",
    )(place, raw, first_a, first_b, second_a, second_b)


def close(text, own_a, msgs_a, own_b, msgs_b):
    def kernel(text_ref, *rest):
        own, msgs = rest[0:2], (rest[2:5], rest[5:8])
        logits_ref, stats_ref = rest[8:]
        for block in range(2):
            total = own[block][...]
            for msg in msgs[block]:
                total += decode(msg, 0, QT)
            at = slice(block * CB, block * CB + CB)
            logits_ref[:, at] = text_ref[:, at] + total
        logits = logits_ref[...]
        largest = jnp.max(logits, axis=1, keepdims=True)
        total = jnp.sum(jnp.exp(logits - largest), axis=1, keepdims=True)
        eye = diagonal()
        stats_ref[0:1, :] = jnp.sum(jnp.where(eye, largest, 0.0), axis=0, keepdims=True)
        stats_ref[1:2, :] = jnp.sum(jnp.where(eye, total, 0.0), axis=0, keepdims=True)

    return pl.pallas_call(
        kernel,
        out_shape=[
            jax.ShapeDtypeStruct((QT, 2 * CB), jnp.float32),
            jax.ShapeDtypeStruct((2, QT), jnp.float32),
        ],
        compiler_params=params(),
        cost_estimate=pl.CostEstimate(flops=30 * QT * CB, bytes_accessed=40 * QT * CB, transcendentals=QT * CB),
        name="close",
    )(text, own_a, own_b, *msgs_a, *msgs_b)


def finish(logits, stats):
    def kernel(logits_ref, stats_ref, out_ref):
        largest = jnp.max(stats_ref[:, 0, :], axis=0, keepdims=True)
        total = jnp.sum(stats_ref[:, 1, :] * jnp.exp(stats_ref[:, 0, :] - largest), axis=0, keepdims=True)
        eye = diagonal()
        largest = jnp.sum(jnp.where(eye, largest, 0.0), axis=1, keepdims=True)
        shift = jnp.sum(jnp.where(eye, jnp.log(total), 0.0), axis=1, keepdims=True)
        out_ref[...] = logits_ref[...] - largest - shift

    return pl.pallas_call(
        kernel,
        out_shape=jax.ShapeDtypeStruct(logits.shape, jnp.float32),
        compiler_params=params(),
        name="finish",
    )(logits, stats)


def shifted(dx, dz):
    return [
        (x * SIDE + z, (x + dx) % SIDE * SIDE + (z + dz) % SIDE) for x in range(SIDE) for z in range(SIDE)
    ]


def send(message, dx, dz):
    return lax.ppermute(message, "cache", shifted(dx, dz))


def per_device(queries, cache_keys, labels, prototypes):
    width = queries.shape[1]
    own = lax.axis_index("cache")
    x, z = own // SIDE, own % SIDE
    low = lax.axis_index("cls") * (2 * CB)

    unit_queries = lax.all_gather(unit_rows(queries), ("cache", "cls"), axis=0, tiled=True)

    order = lax.sort(labels * 16384 + lax.iota(jnp.int32, labels.shape[0]), is_stable=False)
    start = jnp.sum((labels < low).astype(jnp.int32))
    middle = jnp.sum((labels < low + CB).astype(jnp.int32))
    stop = jnp.sum((labels < low + 2 * CB).astype(jnp.int32))
    padded = jnp.concatenate([order, jnp.zeros((CAP,), jnp.int32)])
    picked = jnp.concatenate(
        [lax.dynamic_slice(padded, (start,), (CAP,)), lax.dynamic_slice(padded, (middle,), (CAP,))]
    )
    counts = jnp.stack([middle - start, stop - middle])
    place = lax.iota(jnp.int32, 2 * CAP)
    block = place // CAP
    valid = place - block * CAP < jnp.where(block == 0, counts[0], counts[1])
    local = jnp.where(valid, picked // 16384 - low - block * CB, -1)
    rows = jnp.take(cache_keys, picked % 16384, axis=0, mode="clip")
    keys, hots = prepare(rows, local[:, None])
    tiles = (counts + KT - 1) // KT

    q3 = unit_queries.reshape(SIDE * SIDE, QT, width)
    text = text_scale * lax.dot_general(
        lax.dynamic_index_in_dim(q3, own, 0, keepdims=False),
        prototypes,
        (((1,), (1,)), ((), ())),
        preferred_element_type=jnp.float32,
    )

    def steps_a(dx, parts):
        return [(0, (x + dx) % SIDE * SIDE + j) for j in parts]

    def steps_b(dz, parts):
        return [(1, j * SIDE + (z + dz) % SIDE) for j in parts]

    def plan(steps):
        chunks = jnp.stack([chunk for _, chunk in steps])
        blocks = jnp.array([b for b, _ in steps], jnp.int32)
        return jnp.stack([chunks.astype(jnp.int32), blocks, jnp.stack([tiles[b] for b, _ in steps])])

    run = functools.partial(sums, queries=q3, keys=keys, hots=hots)
    low_half, high_half, all_four = (0, 1), (2, 3), (0, 1, 2, 3)

    pa_right, pa_left, pb_right, pb_left = run(
        [(m, t) for m in range(4) for t in range(2)],
        4,
        0,
        plan(steps_a(2, all_four) + steps_b(2, all_four)),
    )
    pa_right, pa_left = send(pa_right, 1, 0), send(pa_left, -1, 0)
    pb_right, pb_left = send(pb_right, 0, 1), send(pb_left, 0, -1)

    qa_right, qa_left, qb_right, qb_left = run(
        [(m, t) for m in range(4) for t in range(2)],
        4,
        0,
        plan(steps_a(1, high_half) + steps_a(3, low_half) + steps_b(1, high_half) + steps_b(3, low_half)),
    )
    qa_right, qa_left = send(qa_right, 1, 0), send(qa_left, -1, 0)
    qb_right, qb_left = send(qb_right, 0, 1), send(qb_left, 0, -1)
    (raw,) = run(
        [(-1, t) for t in range(8)],
        0,
        8,
        plan(steps_a(1, low_half) + steps_a(3, high_half) + steps_b(1, low_half) + steps_b(3, high_half)),
    )
    ra_right, ra_left, rb_right, rb_left = forward(raw, (pa_right, pa_left, pb_right, pb_left))
    ra_right, ra_left = send(ra_right, 1, 0), send(ra_left, -1, 0)
    rb_right, rb_left = send(rb_right, 0, 1), send(rb_left, 0, -1)
    (mine,) = run([(-1, t) for t in range(8)], 0, 8, plan(steps_a(0, all_four) + steps_b(0, all_four)))

    own_a, a_plus, a_far, a_minus = turn(z[None], mine[:4], ra_right, qa_left, qa_right, ra_left)
    own_b, b_plus, b_far, b_minus = turn(x[None], mine[4:], rb_right, qb_left, qb_right, rb_left)
    a_msgs = send(a_plus, 0, 1), send(a_far, 0, 2), send(a_minus, 0, -1)
    b_msgs = send(b_plus, 1, 0), send(b_far, 2, 0), send(b_minus, -1, 0)

    logits, stats = close(text, own_a, a_msgs, own_b, b_msgs)
    return finish(logits, lax.all_gather(stats, "cls"))


def solution(mesh):
    placed = (P(("cache", "cls"), None), P("cache", None), P("cache"), P("cls", None))
    return jax.shard_map(
        per_device, mesh=mesh, in_specs=placed, out_specs=P("cache", "cls"), check_vma=False
    )
```

```python
import jax
import jax.numpy as jnp
from jax import lax
from jax.experimental import pallas as pl
from jax.experimental.pallas import tpu as pltpu
from jax.sharding import PartitionSpec as P

text_scale = 100.0
epsilon = 1e-06
SIDE = 4
CB = 640
CAP = 1280
QT = 256
KT = 256
TAIL = 16
VMEM_LIMIT = 24 * 1024 * 1024


def params():
    return pltpu.CompilerParams(vmem_limit_bytes=VMEM_LIMIT)


def unit_rows(matrix):
    widened = matrix.astype(jnp.float32)
    return (widened / jnp.sqrt(jnp.sum(widened * widened, axis=1, keepdims=True) + epsilon)).astype(
        jnp.bfloat16
    )


def prepare_kernel(rows_ref, labels_ref, unit_ref, hot_ref):
    unit_ref[...] = unit_rows(rows_ref[...])
    classes = lax.broadcasted_iota(jnp.int32, (KT, CB), 1)
    labels = jnp.sum(jnp.where(diagonal(), labels_ref[0], 0), axis=1, keepdims=True)
    hot_ref[...] = jnp.where(labels == classes, 1.0, 0.0).astype(jnp.bfloat16)


def prepare(rows, labels):
    count, width = rows.shape
    return pl.pallas_call(
        prepare_kernel,
        grid=(count // KT,),
        in_specs=[
            pl.BlockSpec((KT, width), lambda i: (i, 0)),
            pl.BlockSpec((1, 1, KT), lambda i: (i, 0, 0)),
        ],
        out_specs=[
            pl.BlockSpec((KT, width), lambda i: (i, 0)),
            pl.BlockSpec((KT, CB), lambda i: (i, 0)),
        ],
        out_shape=[
            jax.ShapeDtypeStruct((count, width), jnp.bfloat16),
            jax.ShapeDtypeStruct((count, CB), jnp.bfloat16),
        ],
        compiler_params=params(),
        cost_estimate=pl.CostEstimate(flops=count * width * 4, bytes_accessed=count * width * 6, transcendentals=count),
        name="prepare",
    )(rows, labels.reshape(count // KT, 1, KT))


def diagonal():
    shape = (QT, QT)
    return lax.broadcasted_iota(jnp.int32, shape, 0) == lax.broadcasted_iota(jnp.int32, shape, 1)


def encode(values, message_ref, tile, tail_row):
    largest = jnp.maximum(jnp.max(values, axis=1, keepdims=True), 1e-30)
    exponent = jnp.ceil(jnp.log2(largest) - 14.99)
    codes = (values * jnp.exp2(-exponent) + 0.5).astype(jnp.int32)
    message_ref[pl.ds(tile * QT, QT), :] = codes.astype(jnp.int16)
    along = jnp.sum(jnp.where(diagonal(), exponent, 0.0), axis=0, keepdims=True)
    shape = (TAIL, QT)
    old = message_ref[tail_row : tail_row + TAIL, :QT].astype(jnp.int32)
    new = jnp.broadcast_to(along, shape).astype(jnp.int32)
    at = lax.broadcasted_iota(jnp.int32, shape, 0) == tile
    message_ref[tail_row : tail_row + TAIL, :QT] = jnp.where(at, new, old).astype(jnp.int16)


def clear_tail(message_ref, tail_row):
    message_ref[tail_row : tail_row + TAIL, :] = jnp.zeros((TAIL, CB), jnp.int16)


def decode(message_ref, tile, tail_row):
    shape = (TAIL, QT)
    tail = message_ref[tail_row : tail_row + TAIL, :QT].astype(jnp.float32)
    at = lax.broadcasted_iota(jnp.int32, shape, 0) == tile
    along = jnp.sum(jnp.where(at, tail, 0.0), axis=0, keepdims=True)
    exponent = jnp.sum(jnp.where(diagonal(), along, 0.0), axis=1, keepdims=True)
    codes = message_ref[pl.ds(tile * QT, QT), :].astype(jnp.float32)
    return codes * jnp.exp2(exponent)


HALF = 2 * QT
HALF_MSG = jax.ShapeDtypeStruct((HALF + TAIL, CB), jnp.int16)
TILE_MSG = jax.ShapeDtypeStruct((QT + TAIL, CB), jnp.int16)


SUPER = SIDE * QT
TILES = CAP // KT


def aligned(value):
    return pl.multiple_of(value, KT)


def super_sums(tiles, wait_keys, wait_hots, q_ref, keys_ref, hot_ref, scores_ref, total_ref):
    width = q_ref.shape[-1]
    sharpness = float(width) ** 0.5
    queries = q_ref[...].reshape(SUPER, width)

    def step(t, carry):
        wait_keys(t)
        keys = keys_ref[pl.ds(aligned(t * KT), KT), :]
        cosine = lax.dot_general(
            queries, keys, (((1,), (1,)), ((), ())), preferred_element_type=jnp.float32
        )
        scores_ref[:, pl.ds(aligned(t * KT), KT)] = jnp.exp(sharpness * cosine).astype(jnp.bfloat16)
        return carry

    lax.fori_loop(0, tiles, step, 0)
    wait_hots()

    @pl.when(tiles == 0)
    def _():
        total_ref[...] = jnp.zeros_like(total_ref)

    for count in range(1, TILES + 1):
        @pl.when(tiles == count)
        def _(count=count):
            total_ref[...] = jnp.dot(
                scores_ref[:, : count * KT],
                hot_ref[: count * KT, :],
                preferred_element_type=jnp.float32,
            )


HALF_RAW = jax.ShapeDtypeStruct((HALF, CB), jnp.float32)


def sums(coded, plan, tiles, queries, keys, hots):
    width = keys.shape[1]

    def kernel(plan_ref, tiles_ref, q_hbm, keys_hbm, hot_hbm, *rest):
        outs, (q_ref, keys_ref, hot_ref, scores_ref, total_ref, q_sems, key_sems, hot_sems) = rest[:4], rest[4:]

        def copy_queries(job, part):
            return pltpu.make_async_copy(
                q_hbm.at[plan_ref[job * SIDE + part]], q_ref.at[job, part], q_sems.at[job, part]
            )

        def copy_keys(job, t):
            return pltpu.make_async_copy(
                keys_hbm.at[pl.ds(aligned(job * CAP + t * KT), KT), :],
                keys_ref.at[job, pl.ds(aligned(t * KT), KT), :],
                key_sems.at[job, t],
            )

        def copy_hots(job):
            return pltpu.make_async_copy(
                hot_hbm.at[pl.ds(aligned(job * CAP), CAP), :], hot_ref.at[job], hot_sems.at[job]
            )

        for job in range(2):
            for part in range(SIDE):
                copy_queries(job, part).start()

            def start(t, carry, job=job):
                copy_keys(job, t).start()
                return carry

            lax.fori_loop(0, tiles_ref[job], start, 0)
            copy_hots(job).start()

        def run(job, carry):
            for part in range(SIDE):
                copy_queries(job, part).wait()
            super_sums(
                tiles_ref[job],
                lambda t: copy_keys(job, t).wait(),
                lambda: copy_hots(job).wait(),
                q_ref.at[job],
                keys_ref.at[job],
                hot_ref.at[job],
                scores_ref,
                total_ref,
            )
            for at in range(4):
                @pl.when(job == at // 2)
                def _(at=at):
                    first = at % 2 * HALF
                    if coded[at]:
                        clear_tail(outs[at], HALF)

                        def body(t, carry):
                            encode(total_ref[pl.ds(aligned(first + t * QT), QT), :], outs[at], t, HALF)
                            return carry

                        lax.fori_loop(0, 2, body, 0)
                    else:
                        outs[at][...] = total_ref[first : first + HALF, :]
            return carry

        lax.fori_loop(0, 2, run, 0)

    vmem, smem = pl.BlockSpec(memory_space=pltpu.VMEM), pl.BlockSpec(memory_space=pltpu.SMEM)
    hbm = pl.BlockSpec(memory_space=pl.ANY)
    return pl.pallas_call(
        kernel,
        in_specs=[smem, smem, hbm, hbm, hbm],
        out_specs=[vmem] * 4,
        out_shape=[HALF_MSG if flag else HALF_RAW for flag in coded],
        scratch_shapes=[
            pltpu.VMEM((2, SIDE, QT, width), jnp.bfloat16),
            pltpu.VMEM((2, CAP, width), jnp.bfloat16),
            pltpu.VMEM((2, CAP, CB), jnp.bfloat16),
            pltpu.VMEM((SUPER, CAP), jnp.bfloat16),
            pltpu.VMEM((SUPER, CB), jnp.float32),
            pltpu.SemaphoreType.DMA((2, SIDE)),
            pltpu.SemaphoreType.DMA((2, TILES)),
            pltpu.SemaphoreType.DMA((2,)),
        ],
        compiler_params=pltpu.CompilerParams(vmem_limit_bytes=58 * 1024 * 1024),
        cost_estimate=pl.CostEstimate(
            flops=2 * 2 * SUPER * CAP * (width + CB),
            bytes_accessed=4 * SUPER * width,
            transcendentals=SUPER * CAP,
        ),
        name="sums",
    )(plan, tiles, queries, keys, hots)


def forward(raws, arrived):
    count = len(arrived)

    def kernel(*refs):
        for own, source, target in zip(refs[:count], refs[count : 2 * count], refs[2 * count :]):
            clear_tail(target, HALF)

            def body(t, carry, own=own, source=source, target=target):
                encode(own[pl.ds(aligned(t * QT), QT), :] + decode(source, t, HALF), target, t, HALF)
                return carry

            lax.fori_loop(0, 2, body, 0)

    return pl.pallas_call(
        kernel,
        out_shape=[HALF_MSG] * count,
        compiler_params=params(),
        cost_estimate=pl.CostEstimate(flops=10 * count * HALF * CB, bytes_accessed=8 * count * HALF * CB, transcendentals=0),
        name="forward",
    )(*raws, *arrived)


def turn(place, first, second, first_a, first_b, second_a, second_b):
    def kernel(place_ref, first_ref, second_ref, fa, fb, sa, sb, own_ref, plus_ref, far_ref, minus_ref, total_ref):
        for k, out in enumerate((None, plus_ref, far_ref, minus_ref)):
            tile = lax.rem(place_ref[0] + k, SIDE)

            @pl.when(tile < 2)
            def _():
                own = first_ref[pl.ds(aligned(tile * QT), QT), :]
                total_ref[...] = own + decode(fa, tile, HALF) + decode(fb, tile, HALF)

            @pl.when(tile >= 2)
            def _():
                own = second_ref[pl.ds(aligned((tile - 2) * QT), QT), :]
                total_ref[...] = own + decode(sa, tile - 2, HALF) + decode(sb, tile - 2, HALF)

            if out is None:
                own_ref[...] = total_ref[...]
            else:
                clear_tail(out, QT)
                encode(total_ref[...], out, 0, QT)

    vmem = pl.BlockSpec(memory_space=pltpu.VMEM)
    return pl.pallas_call(
        kernel,
        in_specs=[pl.BlockSpec(memory_space=pltpu.SMEM)] + [vmem] * 6,
        out_specs=[vmem] * 4,
        out_shape=[jax.ShapeDtypeStruct((QT, CB), jnp.float32), TILE_MSG, TILE_MSG, TILE_MSG],
        scratch_shapes=[pltpu.VMEM((QT, CB), jnp.float32)],
        compiler_params=params(),
        cost_estimate=pl.CostEstimate(flops=40 * QT * CB, bytes_accessed=40 * QT * CB, transcendentals=0),
        name="turn",
    )(place, first, second, first_a, first_b, second_a, second_b)


def close(text, own_a, msgs_a, own_b, msgs_b):
    def kernel(text_ref, *rest):
        own, msgs = rest[0:2], (rest[2:5], rest[5:8])
        logits_ref, stats_ref = rest[8:]
        for block in range(2):
            total = own[block][...]
            for msg in msgs[block]:
                total += decode(msg, 0, QT)
            at = slice(block * CB, block * CB + CB)
            logits_ref[:, at] = text_ref[:, at] + total
        logits = logits_ref[...]
        largest = jnp.max(logits, axis=1, keepdims=True)
        total = jnp.sum(jnp.exp(logits - largest), axis=1, keepdims=True)
        eye = diagonal()
        stats_ref[0:1, :] = jnp.sum(jnp.where(eye, largest, 0.0), axis=0, keepdims=True)
        stats_ref[1:2, :] = jnp.sum(jnp.where(eye, total, 0.0), axis=0, keepdims=True)

    return pl.pallas_call(
        kernel,
        out_shape=[
            jax.ShapeDtypeStruct((QT, 2 * CB), jnp.float32),
            jax.ShapeDtypeStruct((2, QT), jnp.float32),
        ],
        compiler_params=params(),
        cost_estimate=pl.CostEstimate(flops=30 * QT * CB, bytes_accessed=40 * QT * CB, transcendentals=QT * CB),
        name="close",
    )(text, own_a, own_b, *msgs_a, *msgs_b)


def finish(logits, stats):
    def kernel(logits_ref, stats_ref, out_ref):
        largest = jnp.max(stats_ref[:, 0, :], axis=0, keepdims=True)
        total = jnp.sum(stats_ref[:, 1, :] * jnp.exp(stats_ref[:, 0, :] - largest), axis=0, keepdims=True)
        eye = diagonal()
        largest = jnp.sum(jnp.where(eye, largest, 0.0), axis=1, keepdims=True)
        shift = jnp.sum(jnp.where(eye, jnp.log(total), 0.0), axis=1, keepdims=True)
        out_ref[...] = logits_ref[...] - largest - shift

    return pl.pallas_call(
        kernel,
        out_shape=jax.ShapeDtypeStruct(logits.shape, jnp.float32),
        compiler_params=params(),
        name="finish",
    )(logits, stats)


def shifted(dx, dz):
    return [
        (x * SIDE + z, (x + dx) % SIDE * SIDE + (z + dz) % SIDE) for x in range(SIDE) for z in range(SIDE)
    ]


def send(message, dx, dz):
    return lax.ppermute(message, "cache", shifted(dx, dz))


def per_device(queries, cache_keys, labels, prototypes):
    width = queries.shape[1]
    own = lax.axis_index("cache")
    x, z = own // SIDE, own % SIDE
    low = lax.axis_index("cls") * (2 * CB)

    unit_queries = lax.all_gather(unit_rows(queries), ("cache", "cls"), axis=0, tiled=True)

    order = lax.sort(labels * 16384 + lax.iota(jnp.int32, labels.shape[0]), is_stable=False)
    start = jnp.sum((labels < low).astype(jnp.int32))
    middle = jnp.sum((labels < low + CB).astype(jnp.int32))
    stop = jnp.sum((labels < low + 2 * CB).astype(jnp.int32))
    padded = jnp.concatenate([order, jnp.zeros((CAP,), jnp.int32)])
    picked = jnp.concatenate(
        [lax.dynamic_slice(padded, (start,), (CAP,)), lax.dynamic_slice(padded, (middle,), (CAP,))]
    )
    counts = jnp.stack([middle - start, stop - middle])
    place = lax.iota(jnp.int32, 2 * CAP)
    block = place // CAP
    valid = place - block * CAP < jnp.where(block == 0, counts[0], counts[1])
    local = jnp.where(valid, picked // 16384 - low - block * CB, -1)
    rows = jnp.take(cache_keys, picked % 16384, axis=0, mode="clip")
    keys, hots = prepare(rows, local)
    tiles = (counts + KT - 1) // KT

    q3 = unit_queries.reshape(SIDE * SIDE, QT, width)
    text = text_scale * lax.dot_general(
        lax.dynamic_index_in_dim(q3, own, 0, keepdims=False),
        prototypes,
        (((1,), (1,)), ((), ())),
        preferred_element_type=jnp.float32,
    )

    side = lax.iota(jnp.int32, SIDE)

    def run(shift, coded):
        plan = jnp.concatenate([(x + shift) % SIDE * SIDE + side, side * SIDE + (z + shift) % SIDE])
        return sums(coded, plan.astype(jnp.int32), tiles, q3, keys, hots)

    pa_right, pa_left, pb_right, pb_left = run(2, (True, True, True, True))
    pa_right, pa_left = send(pa_right, 1, 0), send(pa_left, -1, 0)
    pb_right, pb_left = send(pb_right, 0, 1), send(pb_left, 0, -1)

    a_right, qa_right, b_right, qb_right = run(1, (False, True, False, True))
    qa_right, qb_right = send(qa_right, 1, 0), send(qb_right, 0, 1)
    qa_left, a_left, qb_left, b_left = run(3, (True, False, True, False))
    qa_left, qb_left = send(qa_left, -1, 0), send(qb_left, 0, -1)
    ra_right, ra_left, rb_right, rb_left = forward(
        (a_right, a_left, b_right, b_left), (pa_right, pa_left, pb_right, pb_left)
    )
    ra_right, ra_left = send(ra_right, 1, 0), send(ra_left, -1, 0)
    rb_right, rb_left = send(rb_right, 0, 1), send(rb_left, 0, -1)
    a_low, a_high, b_low, b_high = run(0, (False, False, False, False))

    own_a, a_plus, a_far, a_minus = turn(z[None], a_low, a_high, ra_right, qa_left, qa_right, ra_left)
    own_b, b_plus, b_far, b_minus = turn(x[None], b_low, b_high, rb_right, qb_left, qb_right, rb_left)
    a_msgs = send(a_plus, 0, 1), send(a_far, 0, 2), send(a_minus, 0, -1)
    b_msgs = send(b_plus, 1, 0), send(b_far, 2, 0), send(b_minus, -1, 0)

    logits, stats = close(text, own_a, a_msgs, own_b, b_msgs)
    return finish(logits, lax.all_gather(stats, "cls"))


def solution(mesh):
    placed = (P(("cache", "cls"), None), P("cache", None), P("cache"), P("cls", None))
    return jax.shard_map(
        per_device, mesh=mesh, in_specs=placed, out_specs=P("cache", "cls"), check_vma=False
    )
```

```python
import jax
import jax.numpy as jnp
from jax import lax
from jax.experimental import pallas as pl
from jax.experimental.pallas import tpu as pltpu
from jax.sharding import PartitionSpec as P

text_scale = 100.0
epsilon = 1e-06
SIDE = 4
CB = 640
CAP = 1280
QT = 256
KT = 256
TAIL = 16
VMEM_LIMIT = 58 * 1024 * 1024


def params():
    return pltpu.CompilerParams(vmem_limit_bytes=VMEM_LIMIT)


def unit_rows(matrix):
    widened = matrix.astype(jnp.float32)
    return (widened / jnp.sqrt(jnp.sum(widened * widened, axis=1, keepdims=True) + epsilon)).astype(
        jnp.bfloat16
    )


def prepare_kernel(rows_ref, labels_ref, unit_ref, hot_ref):
    unit_ref[...] = unit_rows(rows_ref[...])
    classes = lax.broadcasted_iota(jnp.int32, (KT, CB), 1)
    labels = jnp.sum(jnp.where(diagonal(), labels_ref[0], 0), axis=1, keepdims=True)
    hot_ref[...] = jnp.where(labels == classes, 1.0, 0.0).astype(jnp.bfloat16)


def prepare(rows, labels):
    count, width = rows.shape
    return pl.pallas_call(
        prepare_kernel,
        grid=(count // KT,),
        in_specs=[
            pl.BlockSpec((KT, width), lambda i: (i, 0)),
            pl.BlockSpec((1, 1, KT), lambda i: (i, 0, 0)),
        ],
        out_specs=[
            pl.BlockSpec((KT, width), lambda i: (i, 0)),
            pl.BlockSpec((KT, CB), lambda i: (i, 0)),
        ],
        out_shape=[
            jax.ShapeDtypeStruct((count, width), jnp.bfloat16),
            jax.ShapeDtypeStruct((count, CB), jnp.bfloat16),
        ],
        compiler_params=params(),
        cost_estimate=pl.CostEstimate(flops=count * width * 4, bytes_accessed=count * width * 6, transcendentals=count),
        name="prepare",
    )(rows, labels.reshape(count // KT, 1, KT))


def aligned(value, to=QT):
    return pl.multiple_of(value, to)


def diagonal(rows=QT, shift=0):
    shape = (rows, QT)
    return lax.broadcasted_iota(jnp.int32, shape, 0) + shift == lax.broadcasted_iota(jnp.int32, shape, 1)


def encode(values, message_ref, tile, tail_row):
    largest = jnp.maximum(jnp.max(values, axis=1, keepdims=True), 1e-30)
    exponent = jnp.ceil(jnp.log2(largest) - 14.99)
    codes = (values * jnp.exp2(-exponent) + 0.5).astype(jnp.int32)
    message_ref[pl.ds(aligned(tile * QT), QT), :] = codes.astype(jnp.int16)
    along = jnp.sum(jnp.where(diagonal(), exponent, 0.0), axis=0, keepdims=True)
    shape = (TAIL, QT)
    old = message_ref[tail_row : tail_row + TAIL, :QT].astype(jnp.int32)
    new = jnp.broadcast_to(along, shape).astype(jnp.int32)
    at = lax.broadcasted_iota(jnp.int32, shape, 0) == tile
    message_ref[tail_row : tail_row + TAIL, :QT] = jnp.where(at, new, old).astype(jnp.int16)


def clear_tail(message_ref, tail_row):
    message_ref[tail_row : tail_row + TAIL, :] = jnp.zeros((TAIL, CB), jnp.int16)


def decode(message_ref, start, rows, tail_row):
    shape = (TAIL, QT)
    tail = message_ref[tail_row : tail_row + TAIL, :QT].astype(jnp.float32)
    at = lax.broadcasted_iota(jnp.int32, shape, 0) == start // QT
    along = jnp.sum(jnp.where(at, tail, 0.0), axis=0, keepdims=True)
    exponent = jnp.sum(jnp.where(diagonal(rows, start % QT), along, 0.0), axis=1, keepdims=True)
    codes = message_ref[pl.ds(aligned(start, rows), rows), :].astype(jnp.float32)
    return codes * jnp.exp2(exponent)


HQ = QT // 2
HALF = SIDE * HQ
HALF_MSG = jax.ShapeDtypeStruct((HALF + TAIL, CB), jnp.int16)
TILE_MSG = jax.ShapeDtypeStruct((QT + TAIL, CB), jnp.int16)
HALF_RAW = jax.ShapeDtypeStruct((HALF, CB), jnp.float32)
TILES = CAP // KT


def half_sums(tiles, wait_keys, wait_hots, q_ref, keys_ref, hot_ref, scores_ref, total_ref):
    width = q_ref.shape[-1]
    sharpness = float(width) ** 0.5
    queries = q_ref[...].reshape(HALF, width)

    def step(t, carry):
        wait_keys(t)
        keys = keys_ref[pl.ds(aligned(t * KT), KT), :]
        cosine = lax.dot_general(
            queries, keys, (((1,), (1,)), ((), ())), preferred_element_type=jnp.float32
        )
        scores_ref[:, pl.ds(aligned(t * KT), KT)] = jnp.exp(sharpness * cosine).astype(jnp.bfloat16)
        return carry

    lax.fori_loop(0, tiles, step, 0)
    wait_hots()

    @pl.when(tiles == 0)
    def _():
        total_ref[...] = jnp.zeros_like(total_ref)

    for count in range(1, TILES + 1):
        @pl.when(tiles == count)
        def _(count=count):
            total_ref[...] = jnp.dot(
                scores_ref[:, : count * KT],
                hot_ref[: count * KT, :],
                preferred_element_type=jnp.float32,
            )


def sums(shift, coded, facts, queries, keys, hots, arrived=()):
    width = keys.shape[1]
    joined = len(arrived)

    def kernel(facts_ref, q_hbm, keys_hbm, hot_hbm, *rest):
        came, outs, next_ref = rest[:joined], rest[joined : joined + 2], rest[joined + 2]
        scratch = rest[joined + 3 :]
        q_ref, keys_ref, hot_ref, scores_ref, total_ref, came_ref = scratch[:6]
        q_sems, key_sems, hot_sems, came_sems = scratch[6:]
        for at in range(4):
            next_ref[at] = facts_ref[at]
        row = lax.rem(facts_ref[0] + shift, SIDE)
        column = lax.rem(facts_ref[1] + shift, SIDE)

        def copy_queries(job, part):
            chunk = jnp.where(job == 0, row * SIDE + part, part * SIDE + column)
            return pltpu.make_async_copy(q_hbm.at[chunk], q_ref.at[job, part], q_sems.at[job, part])

        def copy_keys(job, t):
            return pltpu.make_async_copy(
                keys_hbm.at[pl.ds(aligned(job * CAP + t * KT), KT), :],
                keys_ref.at[job, pl.ds(aligned(t * KT), KT), :],
                key_sems.at[job, t],
            )

        def copy_hots(job):
            return pltpu.make_async_copy(
                hot_hbm.at[pl.ds(aligned(job * CAP), CAP), :], hot_ref.at[job], hot_sems.at[job]
            )

        def copy_came(job):
            return pltpu.make_async_copy(came[job], came_ref.at[job], came_sems.at[job])

        for job in range(2):
            for part in range(SIDE):
                copy_queries(job, part).start()

            def start(t, carry, job=job):
                copy_keys(job, t).start()
                return carry

            lax.fori_loop(0, facts_ref[2 + job], start, 0)
            copy_hots(job).start()
            if joined:
                copy_came(job).start()

        def run(job, carry):
            for part in range(SIDE):
                copy_queries(job, part).wait()
            half_sums(
                facts_ref[2 + job],
                lambda t: copy_keys(job, t).wait(),
                lambda: copy_hots(job).wait(),
                q_ref.at[job],
                keys_ref.at[job],
                hot_ref.at[job],
                scores_ref,
                total_ref,
            )
            for at in range(2):
                @pl.when(job == at)
                def _(at=at):
                    if joined:
                        copy_came(at).wait()
                    if not coded:
                        outs[at][...] = total_ref[...]
                        return
                    clear_tail(outs[at], HALF)

                    def body(t, carry):
                        values = total_ref[pl.ds(aligned(t * QT), QT), :]
                        if joined:
                            values += decode(came_ref.at[at], t * QT, QT, HALF)
                        encode(values, outs[at], t, HALF)
                        return carry

                    lax.fori_loop(0, HALF // QT, body, 0)
            return carry

        lax.fori_loop(0, 2, run, 0)

    vmem, smem = pl.BlockSpec(memory_space=pltpu.VMEM), pl.BlockSpec(memory_space=pltpu.SMEM)
    anywhere = pl.BlockSpec(memory_space=pl.ANY)
    return pl.pallas_call(
        kernel,
        in_specs=[smem] + [anywhere] * (3 + joined),
        out_specs=[vmem] * 2 + [smem],
        out_shape=[HALF_MSG if coded else HALF_RAW] * 2 + [jax.ShapeDtypeStruct((4,), jnp.int32)],
        scratch_shapes=[
            pltpu.VMEM((2, SIDE, HQ, width), jnp.bfloat16),
            pltpu.VMEM((2, CAP, width), jnp.bfloat16),
            pltpu.VMEM((2, CAP, CB), jnp.bfloat16),
            pltpu.VMEM((HALF, CAP), jnp.bfloat16),
            pltpu.VMEM((HALF, CB), jnp.float32),
            pltpu.VMEM((2,) + HALF_MSG.shape, jnp.int16),
            pltpu.SemaphoreType.DMA((2, SIDE)),
            pltpu.SemaphoreType.DMA((2, TILES)),
            pltpu.SemaphoreType.DMA((2,)),
            pltpu.SemaphoreType.DMA((2,)),
        ],
        compiler_params=params(),
        cost_estimate=pl.CostEstimate(
            flops=2 * 2 * HALF * CAP * (width + CB),
            bytes_accessed=4 * HALF * width,
            transcendentals=HALF * CAP,
        ),
        name="sums",
    )(facts, queries, keys, hots, *arrived)


def turn(place, mine, other, mine_a, mine_b, other_a, other_b):
    def kernel(place_ref, mine_ref, other_ref, ma, mb, oa, ob, own_ref, plus_ref, far_ref, minus_ref, total_ref):
        for k, out in ((2, far_ref), (1, plus_ref), (3, minus_ref), (0, None)):
            start = lax.rem(place_ref[0] + k, SIDE) * HQ
            at = pl.ds(aligned(start, HQ), HQ)
            total_ref[:HQ, :] = mine_ref[at, :] + decode(ma, start, HQ, HALF) + decode(mb, start, HQ, HALF)
            total_ref[HQ:, :] = other_ref[at, :] + decode(oa, start, HQ, HALF) + decode(ob, start, HQ, HALF)
            if out is None:
                own_ref[...] = total_ref[...]
            else:
                clear_tail(out, QT)
                encode(total_ref[...], out, 0, QT)

    vmem = pl.BlockSpec(memory_space=pltpu.VMEM)
    return pl.pallas_call(
        kernel,
        in_specs=[pl.BlockSpec(memory_space=pltpu.SMEM)] + [vmem] * 6,
        out_specs=[vmem] * 4,
        out_shape=[jax.ShapeDtypeStruct((QT, CB), jnp.float32), TILE_MSG, TILE_MSG, TILE_MSG],
        scratch_shapes=[pltpu.VMEM((QT, CB), jnp.float32)],
        compiler_params=params(),
        cost_estimate=pl.CostEstimate(flops=40 * QT * CB, bytes_accessed=40 * QT * CB, transcendentals=0),
        name="turn",
    )(place, mine, other, mine_a, mine_b, other_a, other_b)


def close(core, text, own_a, msgs_a, own_b, msgs_b):
    piece = HQ // SIDE

    def kernel(core_ref, text_ref, *rest):
        own, msgs = rest[0:2], (rest[2:5], rest[5:8])
        logits_ref, stats_ref, total_ref = rest[8:]
        for block in range(2):
            total = own[block][...]
            for msg in msgs[block]:
                total += decode(msg, 0, QT, QT)
            at = slice(block * CB, block * CB + CB)
            total_ref[...] = text_ref[:, at] + total
            for half in range(2):
                place = jnp.where(core_ref[0] == half, 0, piece)
                for y in range(SIDE):
                    source = half * HQ + y * piece
                    target = pl.ds(pl.multiple_of(y * 2 * piece + place, piece), piece)
                    logits_ref[target, at] = total_ref[source : source + piece, :]
        logits = logits_ref[...]
        largest = jnp.max(logits, axis=1, keepdims=True)
        total = jnp.sum(jnp.exp(logits - largest), axis=1, keepdims=True)
        eye = diagonal()
        stats_ref[0:1, :] = jnp.sum(jnp.where(eye, largest, 0.0), axis=0, keepdims=True)
        stats_ref[1:2, :] = jnp.sum(jnp.where(eye, total, 0.0), axis=0, keepdims=True)

    vmem = pl.BlockSpec(memory_space=pltpu.VMEM)
    return pl.pallas_call(
        kernel,
        in_specs=[pl.BlockSpec(memory_space=pltpu.SMEM)] + [vmem] * 9,
        out_specs=[vmem] * 2,
        out_shape=[
            jax.ShapeDtypeStruct((QT, 2 * CB), jnp.float32),
            jax.ShapeDtypeStruct((2, QT), jnp.float32),
        ],
        scratch_shapes=[pltpu.VMEM((QT, CB), jnp.float32)],
        compiler_params=params(),
        cost_estimate=pl.CostEstimate(flops=30 * QT * CB, bytes_accessed=40 * QT * CB, transcendentals=QT * CB),
        name="close",
    )(core, text, own_a, own_b, *msgs_a, *msgs_b)


def finish(logits, stats):
    def kernel(logits_ref, stats_ref, out_ref):
        largest = jnp.max(stats_ref[:, 0, :], axis=0, keepdims=True)
        total = jnp.sum(stats_ref[:, 1, :] * jnp.exp(stats_ref[:, 0, :] - largest), axis=0, keepdims=True)
        eye = diagonal()
        largest = jnp.sum(jnp.where(eye, largest, 0.0), axis=1, keepdims=True)
        shift = jnp.sum(jnp.where(eye, jnp.log(total), 0.0), axis=1, keepdims=True)
        out_ref[...] = logits_ref[...] - largest - shift

    return pl.pallas_call(
        kernel,
        out_shape=jax.ShapeDtypeStruct(logits.shape, jnp.float32),
        compiler_params=params(),
        name="finish",
    )(logits, stats)


def shifted(dx, dz):
    return [
        (x * SIDE + z, (x + dx) % SIDE * SIDE + (z + dz) % SIDE) for x in range(SIDE) for z in range(SIDE)
    ]


def send(message, dx, dz):
    return lax.ppermute(message, "cache", shifted(dx, dz))


def per_device(queries, cache_keys, labels, prototypes):
    width = queries.shape[1]
    own = lax.axis_index("cache")
    x, z = own // SIDE, own % SIDE
    core = lax.axis_index("core")
    low = (lax.axis_index("y") * 2 + core) * (2 * CB)

    gathered = lax.all_gather(unit_rows(queries), ("cache", "y"), axis=0, tiled=True)

    order = lax.sort(labels * 16384 + lax.iota(jnp.int32, labels.shape[0]), is_stable=False)
    start = jnp.sum((labels < low).astype(jnp.int32))
    middle = jnp.sum((labels < low + CB).astype(jnp.int32))
    stop = jnp.sum((labels < low + 2 * CB).astype(jnp.int32))
    padded = jnp.concatenate([order, jnp.zeros((CAP,), jnp.int32)])
    picked = jnp.concatenate(
        [lax.dynamic_slice(padded, (start,), (CAP,)), lax.dynamic_slice(padded, (middle,), (CAP,))]
    )
    counts = jnp.stack([middle - start, stop - middle])
    place = lax.iota(jnp.int32, 2 * CAP)
    block = place // CAP
    valid = place - block * CAP < jnp.where(block == 0, counts[0], counts[1])
    local = jnp.where(valid, picked // 16384 - low - block * CB, -1)
    rows = jnp.take(cache_keys, picked % 16384, axis=0, mode="clip")
    keys, hots = prepare(rows, local)
    tiles = (counts + KT - 1) // KT
    gathered, keys, hots = lax.optimization_barrier((gathered, keys, hots))
    q_mine = gathered.reshape(SIDE * SIDE, HQ, width)
    q_other = lax.ppermute(gathered, "core", [(0, 1), (1, 0)]).reshape(SIDE * SIDE, HQ, width)
    facts = jnp.stack([x, z, tiles[0], tiles[1]]).astype(jnp.int32)

    def run(facts, shift, coded, which, arrived=()):
        first, second, facts = sums(shift, coded, facts, which, keys, hots, arrived)
        return (first, second), facts

    def send_right(pair):
        return send(pair[0], 1, 0), send(pair[1], 0, 1)

    def send_left(pair):
        return send(pair[0], -1, 0), send(pair[1], 0, -1)

    far_right, facts = run(facts, 2, True, q_mine)
    far_right = send_right(far_right)
    far_left, facts = run(facts, 2, True, q_other)
    far_left = send_left(far_left)
    free_right, facts = run(facts, 1, True, q_other)
    free_right = send_right(free_right)
    free_left, facts = run(facts, 3, True, q_mine)
    free_left = send_left(free_left)
    full_right, facts = run(facts, 1, True, q_mine, far_right)
    full_right = send_right(full_right)
    full_left, facts = run(facts, 3, True, q_other, far_left)
    full_left = send_left(full_left)
    mine, facts = run(facts, 0, False, q_mine)
    other, _ = run(facts, 0, False, q_other)

    text = text_scale * lax.dot_general(
        jnp.concatenate(
            [lax.dynamic_index_in_dim(part, own, 0, keepdims=False) for part in (q_mine, q_other)], axis=0
        ),
        prototypes,
        (((1,), (1,)), ((), ())),
        preferred_element_type=jnp.float32,
    )

    own_a, a_plus, a_far, a_minus = turn(
        z[None], mine[0], other[0], full_right[0], free_left[0], free_right[0], full_left[0]
    )
    own_b, b_plus, b_far, b_minus = turn(
        x[None], mine[1], other[1], full_right[1], free_left[1], free_right[1], full_left[1]
    )
    a_msgs = send(a_far, 0, 2), send(a_plus, 0, 1), send(a_minus, 0, -1)
    b_msgs = send(b_far, 2, 0), send(b_plus, 1, 0), send(b_minus, -1, 0)

    logits, stats = close(core[None], text, own_a, a_msgs, own_b, b_msgs)
    return finish(logits, lax.all_gather(stats, ("y", "core")))


def solution(mesh):
    fine = jax.sharding.Mesh(mesh.devices.reshape(SIDE * SIDE, SIDE, 2), ("cache", "y", "core"))
    cls = ("y", "core")
    placed = (P(("cache", "y", "core"), None), P("cache", None), P("cache"), P(cls, None))
    return jax.shard_map(
        per_device, mesh=fine, in_specs=placed, out_specs=P("cache", cls), check_vma=False
    )
```

```python
import jax
import jax.numpy as jnp
from jax import lax
from jax.experimental import pallas as pl
from jax.experimental.pallas import tpu as pltpu
from jax.sharding import PartitionSpec as P

text_scale = 100.0
epsilon = 1e-06
SIDE = 4
CB = 640
CAP = 1280
QT = 256
KT = 256
TAIL = 16


def params(mib=58):
    return pltpu.CompilerParams(vmem_limit_bytes=mib * 1024 * 1024)


def unit_rows(matrix):
    widened = matrix.astype(jnp.float32)
    return (widened / jnp.sqrt(jnp.sum(widened * widened, axis=1, keepdims=True) + epsilon)).astype(
        jnp.bfloat16
    )


def prepare_kernel(rows_ref, labels_ref, unit_ref, hot_ref):
    unit_ref[...] = unit_rows(rows_ref[...])
    classes = lax.broadcasted_iota(jnp.int32, (KT, CB), 1)
    labels = jnp.sum(jnp.where(diagonal(), labels_ref[0], 0), axis=1, keepdims=True)
    hot_ref[...] = jnp.where(labels == classes, 1.0, 0.0).astype(jnp.bfloat16)


def prepare(rows, labels):
    count, width = rows.shape
    return pl.pallas_call(
        prepare_kernel,
        grid=(count // KT,),
        in_specs=[
            pl.BlockSpec((KT, width), lambda i: (i, 0)),
            pl.BlockSpec((1, 1, KT), lambda i: (i, 0, 0)),
        ],
        out_specs=[
            pl.BlockSpec((KT, width), lambda i: (i, 0)),
            pl.BlockSpec((KT, CB), lambda i: (i, 0)),
        ],
        out_shape=[
            jax.ShapeDtypeStruct((count, width), jnp.bfloat16),
            jax.ShapeDtypeStruct((count, CB), jnp.bfloat16),
        ],
        compiler_params=params(),
        cost_estimate=pl.CostEstimate(flops=count * width * 4, bytes_accessed=count * width * 6, transcendentals=count),
        name="prepare",
    )(rows, labels.reshape(count // KT, 1, KT))


def aligned(value):
    return pl.multiple_of(value, QT)


def diagonal():
    shape = (QT, QT)
    return lax.broadcasted_iota(jnp.int32, shape, 0) == lax.broadcasted_iota(jnp.int32, shape, 1)


def encode(values, message_ref, tile, tail_row):
    largest = jnp.maximum(jnp.max(values, axis=1, keepdims=True), 1e-30)
    exponent = jnp.ceil(jnp.log2(largest) - 14.99)
    codes = (values * jnp.exp2(-exponent) + 0.5).astype(jnp.int32)
    message_ref[pl.ds(aligned(tile * QT), QT), :] = codes.astype(jnp.int16)
    along = jnp.sum(jnp.where(diagonal(), exponent, 0.0), axis=0, keepdims=True)
    shape = (TAIL, QT)
    old = message_ref[tail_row : tail_row + TAIL, :QT].astype(jnp.int32)
    new = jnp.broadcast_to(along, shape).astype(jnp.int32)
    at = lax.broadcasted_iota(jnp.int32, shape, 0) == tile
    message_ref[tail_row : tail_row + TAIL, :QT] = jnp.where(at, new, old).astype(jnp.int16)


def clear_tail(message_ref, tail_row):
    message_ref[tail_row : tail_row + TAIL, :] = jnp.zeros((TAIL, CB), jnp.int16)


def decode(message_ref, tile, tail_row):
    shape = (TAIL, QT)
    tail = message_ref[tail_row : tail_row + TAIL, :QT].astype(jnp.float32)
    at = lax.broadcasted_iota(jnp.int32, shape, 0) == tile
    along = jnp.sum(jnp.where(at, tail, 0.0), axis=0, keepdims=True)
    exponent = jnp.sum(jnp.where(diagonal(), along, 0.0), axis=1, keepdims=True)
    codes = message_ref[pl.ds(aligned(tile * QT), QT), :].astype(jnp.float32)
    return codes * jnp.exp2(exponent)


HALF = 2 * QT
HALF_MSG = jax.ShapeDtypeStruct((HALF + TAIL, CB), jnp.int16)
TILE_MSG = jax.ShapeDtypeStruct((QT + TAIL, CB), jnp.int16)
HALF_RAW = jax.ShapeDtypeStruct((HALF, CB), jnp.float32)
TILES = CAP // KT


def half_sums(tiles, wait_keys, wait_hots, q_ref, keys_ref, hot_ref, scores_ref, total_ref):
    width = q_ref.shape[-1]
    sharpness = float(width) ** 0.5
    queries = q_ref[...].reshape(HALF, width)

    def step(t, carry):
        wait_keys(t)
        keys = keys_ref[pl.ds(aligned(t * KT), KT), :]
        cosine = lax.dot_general(
            queries, keys, (((1,), (1,)), ((), ())), preferred_element_type=jnp.float32
        )
        scores_ref[:, pl.ds(aligned(t * KT), KT)] = jnp.exp(sharpness * cosine).astype(jnp.bfloat16)
        return carry

    lax.fori_loop(0, tiles, step, 0)
    wait_hots()

    @pl.when(tiles == 0)
    def _():
        total_ref[...] = jnp.zeros_like(total_ref)

    for count in range(1, TILES + 1):
        @pl.when(tiles == count)
        def _(count=count):
            total_ref[...] = jnp.dot(
                scores_ref[:, : count * KT],
                hot_ref[: count * KT, :],
                preferred_element_type=jnp.float32,
            )


def sums(shifts, halves, coded, facts, queries, keys, hots, arrived=()):
    width = keys.shape[1]
    joined = len(arrived)

    def kernel(facts_ref, q_hbm, keys_hbm, hot_hbm, *rest):
        came, outs, next_ref = rest[:joined], rest[joined : joined + 4], rest[joined + 4]
        scratch = rest[joined + 5 :]
        q_ref, keys_ref, hot_ref, scores_ref, total_ref, came_ref = scratch[:6]
        q_sems, key_sems, hot_sems, came_sems = scratch[6:]
        for at in range(4):
            next_ref[at] = facts_ref[at]

        def copy_queries(job, part):
            block, side = job // 2, job % 2
            away = jnp.where(side == 0, shifts[0], shifts[1])
            inner = jnp.where(side == 0, halves[0], halves[1]) * 2 + part
            outer = lax.rem(facts_ref[block] + away, SIDE)
            chunk = jnp.where(block == 0, outer * SIDE + inner, inner * SIDE + outer)
            return pltpu.make_async_copy(q_hbm.at[chunk], q_ref.at[job, part], q_sems.at[job, part])

        def copy_keys(block, t):
            return pltpu.make_async_copy(
                keys_hbm.at[pl.ds(aligned(block * CAP + t * KT), KT), :],
                keys_ref.at[block, pl.ds(aligned(t * KT), KT), :],
                key_sems.at[block, t],
            )

        def copy_hots(block):
            return pltpu.make_async_copy(
                hot_hbm.at[pl.ds(aligned(block * CAP), CAP), :], hot_ref.at[block], hot_sems.at[block]
            )

        def copy_came(job):
            return pltpu.make_async_copy(came[job], came_ref.at[job], came_sems.at[job])

        def start_queries(job):
            for part in range(2):
                copy_queries(job, part).start()

        for block in range(2):
            start_queries(2 * block)

            def start(t, carry, block=block):
                copy_keys(block, t).start()
                return carry

            lax.fori_loop(0, facts_ref[2 + block], start, 0)
            copy_hots(block).start()
            start_queries(2 * block + 1)
        for job in range(joined):
            copy_came(job).start()

        def run(job, carry):
            block = job // 2
            first = job % 2 == 0
            for part in range(2):
                copy_queries(job, part).wait()

            def wait_keys(t):
                @pl.when(first)
                def _():
                    copy_keys(block, t).wait()

            def wait_hots():
                @pl.when(first)
                def _():
                    copy_hots(block).wait()

            half_sums(
                facts_ref[2 + block],
                wait_keys,
                wait_hots,
                q_ref.at[job],
                keys_ref.at[block],
                hot_ref.at[block],
                scores_ref,
                total_ref,
            )
            for at in range(4):
                @pl.when(job == at)
                def _(at=at):
                    if joined:
                        copy_came(at).wait()
                    if coded:
                        clear_tail(outs[at], HALF)

                    def body(t, carry):
                        rows = pl.ds(aligned(t * QT), QT)
                        values = total_ref[rows, :]
                        if joined:
                            values += decode(came_ref.at[at], t, HALF)
                        if coded:
                            encode(values, outs[at], t, HALF)
                        else:
                            outs[at][rows, :] = values
                        return carry

                    lax.fori_loop(0, HALF // QT, body, 0)
            return carry

        lax.fori_loop(0, 4, run, 0)

    vmem, smem = pl.BlockSpec(memory_space=pltpu.VMEM), pl.BlockSpec(memory_space=pltpu.SMEM)
    anywhere = pl.BlockSpec(memory_space=pl.ANY)
    return pl.pallas_call(
        kernel,
        in_specs=[smem] + [anywhere] * (3 + joined),
        out_specs=[vmem] * 4 + [smem],
        out_shape=[HALF_MSG if coded else HALF_RAW] * 4 + [jax.ShapeDtypeStruct((4,), jnp.int32)],
        scratch_shapes=[
            pltpu.VMEM((4, 2, QT, width), jnp.bfloat16),
            pltpu.VMEM((2, CAP, width), jnp.bfloat16),
            pltpu.VMEM((2, CAP, CB), jnp.bfloat16),
            pltpu.VMEM((HALF, CAP), jnp.bfloat16),
            pltpu.VMEM((HALF, CB), jnp.float32),
            pltpu.VMEM((4,) + HALF_MSG.shape, jnp.int16),
            pltpu.SemaphoreType.DMA((4, 2)),
            pltpu.SemaphoreType.DMA((2, TILES)),
            pltpu.SemaphoreType.DMA((2,)),
            pltpu.SemaphoreType.DMA((4,)),
        ],
        compiler_params=params(),
        cost_estimate=pl.CostEstimate(
            flops=2 * 4 * HALF * CAP * (width + CB),
            bytes_accessed=8 * HALF * width,
            transcendentals=2 * HALF * CAP,
        ),
        name="sums",
    )(facts, queries, keys, hots, *arrived)


def turn(place, low, high, low_came, high_came):
    def kernel(place_ref, low_ref, high_ref, low_msg, high_msg, own_ref, plus_ref, far_ref, minus_ref, total_ref):
        for k, out in ((2, far_ref), (1, plus_ref), (3, minus_ref), (0, None)):
            tile = lax.rem(place_ref[0] + k, SIDE)

            def gather(own, came, at):
                total_ref[...] = own[pl.ds(aligned(at * QT), QT), :] + decode(came, at, HALF)

            @pl.when(tile < 2)
            def _():
                gather(low_ref, low_msg, tile)

            @pl.when(tile >= 2)
            def _():
                gather(high_ref, high_msg, tile - 2)

            if out is None:
                own_ref[...] = total_ref[...]
            else:
                clear_tail(out, QT)
                encode(total_ref[...], out, 0, QT)

    vmem = pl.BlockSpec(memory_space=pltpu.VMEM)
    return pl.pallas_call(
        kernel,
        in_specs=[pl.BlockSpec(memory_space=pltpu.SMEM)] + [vmem] * 4,
        out_specs=[vmem] * 4,
        out_shape=[jax.ShapeDtypeStruct((QT, CB), jnp.float32), TILE_MSG, TILE_MSG, TILE_MSG],
        scratch_shapes=[pltpu.VMEM((QT, CB), jnp.float32)],
        compiler_params=params(),
        cost_estimate=pl.CostEstimate(flops=40 * QT * CB, bytes_accessed=40 * QT * CB, transcendentals=0),
        name="turn",
    )(place, low, high, low_came, high_came)


def close(text, own_a, msgs_a, own_b, msgs_b):
    def kernel(text_ref, *rest):
        own, msgs = rest[0:2], (rest[2:5], rest[5:8])
        logits_ref, stats_ref = rest[8:]
        for block in range(2):
            total = own[block][...]
            for msg in msgs[block]:
                total += decode(msg, 0, QT)
            at = slice(block * CB, block * CB + CB)
            logits_ref[:, at] = text_ref[:, at] + total
        logits = logits_ref[...]
        largest = jnp.max(logits, axis=1, keepdims=True)
        total = jnp.sum(jnp.exp(logits - largest), axis=1, keepdims=True)
        eye = diagonal()
        stats_ref[0:1, :] = jnp.sum(jnp.where(eye, largest, 0.0), axis=0, keepdims=True)
        stats_ref[1:2, :] = jnp.sum(jnp.where(eye, total, 0.0), axis=0, keepdims=True)

    return pl.pallas_call(
        kernel,
        out_shape=[
            jax.ShapeDtypeStruct((QT, 2 * CB), jnp.float32),
            jax.ShapeDtypeStruct((2, QT), jnp.float32),
        ],
        compiler_params=params(24),
        cost_estimate=pl.CostEstimate(flops=30 * QT * CB, bytes_accessed=40 * QT * CB, transcendentals=QT * CB),
        name="close",
    )(text, own_a, own_b, *msgs_a, *msgs_b)


def finish(logits, stats):
    def kernel(logits_ref, stats_ref, out_ref):
        largest = jnp.max(stats_ref[:, 0, :], axis=0, keepdims=True)
        total = jnp.sum(stats_ref[:, 1, :] * jnp.exp(stats_ref[:, 0, :] - largest), axis=0, keepdims=True)
        eye = diagonal()
        largest = jnp.sum(jnp.where(eye, largest, 0.0), axis=1, keepdims=True)
        shift = jnp.sum(jnp.where(eye, jnp.log(total), 0.0), axis=1, keepdims=True)
        out_ref[...] = logits_ref[...] - largest - shift

    return pl.pallas_call(
        kernel,
        out_shape=jax.ShapeDtypeStruct(logits.shape, jnp.float32),
        compiler_params=params(24),
        name="finish",
    )(logits, stats)


def shifted(dx, dz):
    return [
        (x * SIDE + z, (x + dx) % SIDE * SIDE + (z + dz) % SIDE) for x in range(SIDE) for z in range(SIDE)
    ]


def send(message, dx, dz):
    return lax.ppermute(message, "cache", shifted(dx, dz))


def per_device(queries, cache_keys, labels, prototypes):
    width = queries.shape[1]
    own = lax.axis_index("cache")
    x, z = own // SIDE, own % SIDE
    low = lax.axis_index("cls") * (2 * CB)

    gathered = lax.all_gather(unit_rows(queries), ("cache", "cls"), axis=0, tiled=True)

    order = lax.sort(labels * 16384 + lax.iota(jnp.int32, labels.shape[0]), is_stable=False)
    start = jnp.sum((labels < low).astype(jnp.int32))
    middle = jnp.sum((labels < low + CB).astype(jnp.int32))
    stop = jnp.sum((labels < low + 2 * CB).astype(jnp.int32))
    padded = jnp.concatenate([order, jnp.zeros((CAP,), jnp.int32)])
    picked = jnp.concatenate(
        [lax.dynamic_slice(padded, (start,), (CAP,)), lax.dynamic_slice(padded, (middle,), (CAP,))]
    )
    counts = jnp.stack([middle - start, stop - middle])
    place = lax.iota(jnp.int32, 2 * CAP)
    block = place // CAP
    valid = place - block * CAP < jnp.where(block == 0, counts[0], counts[1])
    local = jnp.where(valid, picked // 16384 - low - block * CB, -1)
    rows = jnp.take(cache_keys, picked % 16384, axis=0, mode="clip")
    keys, hots = prepare(rows, local)
    tiles = (counts + KT - 1) // KT
    gathered, keys, hots = lax.optimization_barrier((gathered, keys, hots))
    q3 = gathered.reshape(SIDE * SIDE, QT, width)
    facts = jnp.stack([x, z, tiles[0], tiles[1]]).astype(jnp.int32)

    def run(facts, shifts, halves, coded, arrived=()):
        *parts, facts = sums(shifts, halves, coded, facts, q3, keys, hots, arrived)
        return parts, facts

    def send_all(parts):
        a_right, a_left, b_right, b_left = parts
        return send(a_right, 1, 0), send(a_left, -1, 0), send(b_right, 0, 1), send(b_left, 0, -1)

    far, facts = run(facts, (2, 2), (0, 1), True)
    far = send_all(far)
    free, facts = run(facts, (1, 3), (1, 0), True)
    free = send_all(free)
    full, facts = run(facts, (1, 3), (0, 1), True, far)
    full = send_all(full)
    a_low, a_high, b_low, b_high = run(
        facts, (0, 0), (0, 1), False, (free[1], free[0], free[3], free[2])
    )[0]

    text = text_scale * lax.dot_general(
        lax.dynamic_index_in_dim(q3, own, 0, keepdims=False),
        prototypes,
        (((1,), (1,)), ((), ())),
        preferred_element_type=jnp.float32,
    )

    own_a, a_plus, a_far, a_minus = turn(z[None], a_low, a_high, full[0], full[1])
    own_b, b_plus, b_far, b_minus = turn(x[None], b_low, b_high, full[2], full[3])
    a_msgs = send(a_far, 0, 2), send(a_plus, 0, 1), send(a_minus, 0, -1)
    b_msgs = send(b_far, 2, 0), send(b_plus, 1, 0), send(b_minus, -1, 0)

    logits, stats = close(text, own_a, a_msgs, own_b, b_msgs)
    return finish(logits, lax.all_gather(stats, "cls"))


def solution(mesh):
    placed = (P(("cache", "cls"), None), P("cache", None), P("cache"), P("cls", None))
    return jax.shard_map(
        per_device, mesh=mesh, in_specs=placed, out_specs=P("cache", "cls"), check_vma=False
    )
```

```python
import jax
import jax.numpy as jnp
from jax import lax
from jax.experimental import pallas as pl
from jax.experimental.pallas import tpu as pltpu
from jax.sharding import PartitionSpec as P

text_scale = 100.0
epsilon = 1e-06
SIDE = 4
CB = 640
CAP = 1280
QT = 256
KT = 256
TAIL = 16


def params(mib=58):
    return pltpu.CompilerParams(vmem_limit_bytes=mib * 1024 * 1024)


def unit_rows(matrix):
    widened = matrix.astype(jnp.float32)
    return (widened / jnp.sqrt(jnp.sum(widened * widened, axis=1, keepdims=True) + epsilon)).astype(
        jnp.bfloat16
    )


def prepare_kernel(rows_ref, labels_ref, unit_ref, hot_ref):
    unit_ref[...] = unit_rows(rows_ref[...])
    classes = lax.broadcasted_iota(jnp.int32, (KT, CB), 1)
    labels = jnp.sum(jnp.where(diagonal(), labels_ref[0], 0), axis=1, keepdims=True)
    hot_ref[...] = jnp.where(labels == classes, 1.0, 0.0).astype(jnp.bfloat16)


def prepare(rows, labels):
    count, width = rows.shape
    return pl.pallas_call(
        prepare_kernel,
        grid=(count // KT,),
        in_specs=[
            pl.BlockSpec((KT, width), lambda i: (i, 0)),
            pl.BlockSpec((1, 1, KT), lambda i: (i, 0, 0)),
        ],
        out_specs=[
            pl.BlockSpec((KT, width), lambda i: (i, 0)),
            pl.BlockSpec((KT, CB), lambda i: (i, 0)),
        ],
        out_shape=[
            jax.ShapeDtypeStruct((count, width), jnp.bfloat16),
            jax.ShapeDtypeStruct((count, CB), jnp.bfloat16),
        ],
        compiler_params=params(),
        cost_estimate=pl.CostEstimate(flops=count * width * 4, bytes_accessed=count * width * 6, transcendentals=count),
        name="prepare",
    )(rows, labels.reshape(count // KT, 1, KT))


def aligned(value):
    return pl.multiple_of(value, QT)


def diagonal():
    shape = (QT, QT)
    return lax.broadcasted_iota(jnp.int32, shape, 0) == lax.broadcasted_iota(jnp.int32, shape, 1)


def encode(values, message_ref, tile, tail_row):
    largest = jnp.maximum(jnp.max(values, axis=1, keepdims=True), 1e-30)
    exponent = jnp.ceil(jnp.log2(largest) - 14.99)
    codes = (values * jnp.exp2(-exponent) + 0.5).astype(jnp.int32)
    message_ref[pl.ds(aligned(tile * QT), QT), :] = codes.astype(jnp.int16)
    along = jnp.sum(jnp.where(diagonal(), exponent, 0.0), axis=0, keepdims=True)
    shape = (TAIL, QT)
    old = message_ref[tail_row : tail_row + TAIL, :QT].astype(jnp.int32)
    new = jnp.broadcast_to(along, shape).astype(jnp.int32)
    at = lax.broadcasted_iota(jnp.int32, shape, 0) == tile
    message_ref[tail_row : tail_row + TAIL, :QT] = jnp.where(at, new, old).astype(jnp.int16)


def clear_tail(message_ref, tail_row):
    message_ref[tail_row : tail_row + TAIL, :] = jnp.zeros((TAIL, CB), jnp.int16)


def decode(message_ref, tile, tail_row):
    shape = (TAIL, QT)
    tail = message_ref[tail_row : tail_row + TAIL, :QT].astype(jnp.float32)
    at = lax.broadcasted_iota(jnp.int32, shape, 0) == tile
    along = jnp.sum(jnp.where(at, tail, 0.0), axis=0, keepdims=True)
    exponent = jnp.sum(jnp.where(diagonal(), along, 0.0), axis=1, keepdims=True)
    codes = message_ref[pl.ds(aligned(tile * QT), QT), :].astype(jnp.float32)
    return codes * jnp.exp2(exponent)


HALF = 2 * QT
HALF_MSG = jax.ShapeDtypeStruct((HALF + TAIL, CB), jnp.int16)
TILE_MSG = jax.ShapeDtypeStruct((QT + TAIL, CB), jnp.int16)
HALF_RAW = jax.ShapeDtypeStruct((HALF, CB), jnp.float32)


SUPER = SIDE * QT
COMMON = 3
TILES = CAP // KT


def super_sums(tiles, wait_keys, wait_hots, q_ref, keys_ref, hot_ref, scores_ref, total_ref):
    width = q_ref.shape[-1]
    sharpness = float(width) ** 0.5
    queries = q_ref[...].reshape(SUPER, width)

    def step(t, carry):
        wait_keys(t)
        keys = keys_ref[pl.ds(aligned(t * KT), KT), :]
        cosine = lax.dot_general(
            queries, keys, (((1,), (1,)), ((), ())), preferred_element_type=jnp.float32
        )
        scores_ref[:, pl.ds(aligned(t * KT), KT)] = jnp.exp(sharpness * cosine).astype(jnp.bfloat16)
        return carry

    lax.fori_loop(0, tiles, step, 0)
    wait_hots()
    cut = COMMON * KT
    total_ref[...] = jnp.dot(
        scores_ref[:, :cut], hot_ref[:cut, :], preferred_element_type=jnp.float32
    )

    @pl.when(tiles > COMMON)
    def _():
        total_ref[...] += jnp.dot(
            scores_ref[:, cut:], hot_ref[cut:, :], preferred_element_type=jnp.float32
        )


def sums(shifts, halves, coded, facts, queries, keys, hots, arrived=()):
    width = keys.shape[1]
    joined = len(arrived)

    def kernel(facts_ref, q_hbm, keys_hbm, hot_hbm, *rest):
        came, outs, next_ref = rest[:joined], rest[joined : joined + 4], rest[joined + 4]
        scratch = rest[joined + 5 :]
        q_ref, keys_ref, hot_ref, scores_ref, total_ref, came_ref, msg_ref = scratch[:7]
        q_sems, key_sems, hot_sems, came_sems, out_sems = scratch[7:]
        for at in range(4):
            next_ref[at] = facts_ref[at]

        def copy_queries(block, part):
            away = shifts[part // 2]
            inner = halves[part // 2] * 2 + part % 2
            outer = lax.rem(facts_ref[block] + away, SIDE)
            chunk = jnp.where(block == 0, outer * SIDE + inner, inner * SIDE + outer)
            return pltpu.make_async_copy(q_hbm.at[chunk], q_ref.at[block, part], q_sems.at[block, part])

        def copy_keys(block, t):
            return pltpu.make_async_copy(
                keys_hbm.at[pl.ds(aligned(block * CAP + t * KT), KT), :],
                keys_ref.at[block, pl.ds(aligned(t * KT), KT), :],
                key_sems.at[block, t],
            )

        def copy_hots(block):
            return pltpu.make_async_copy(
                hot_hbm.at[pl.ds(aligned(block * CAP), CAP), :], hot_ref.at[block], hot_sems.at[block]
            )

        def copy_came(at):
            return pltpu.make_async_copy(came[at], came_ref.at[at], came_sems.at[at])

        def copy_out(at):
            source = msg_ref.at[at] if coded else total_ref.at[at // 2, pl.ds(at % 2 * HALF, HALF), :]
            return pltpu.make_async_copy(source, outs[at], out_sems.at[at])

        for block in range(2):
            for part in range(SIDE):
                copy_queries(block, part).start()

            def start(t, carry, block=block):
                copy_keys(block, t).start()
                return carry

            lax.fori_loop(0, facts_ref[2 + block], start, 0)
            copy_hots(block).start()
        for at in range(joined):
            copy_came(at).start()
        scores_ref[...] = jnp.zeros_like(scores_ref)
        if coded:
            for at in range(4):
                clear_tail(msg_ref.at[at], HALF)

        def run(block, carry):
            for part in range(SIDE):
                copy_queries(block, part).wait()
            super_sums(
                facts_ref[2 + block],
                lambda t: copy_keys(block, t).wait(),
                lambda: copy_hots(block).wait(),
                q_ref.at[block],
                keys_ref.at[block],
                hot_ref.at[block],
                scores_ref,
                total_ref.at[block],
            )
            if joined:
                @pl.when(block == 0)
                def _():
                    for at in range(joined):
                        copy_came(at).wait()

            if joined or coded:
                def body(t, carry):
                    rows = pl.ds(aligned(t * QT), QT)
                    at = 2 * block + t // 2
                    values = total_ref[block, rows, :]
                    if joined:
                        values += decode(came_ref.at[at], t % 2, HALF)
                    if coded:
                        encode(values, msg_ref.at[at], t % 2, HALF)
                    else:
                        total_ref[block, rows, :] = values
                    return carry

                lax.fori_loop(0, SIDE, body, 0)
            for at in range(4):
                @pl.when(block == at // 2)
                def _(at=at):
                    copy_out(at).start()
            return carry

        lax.fori_loop(0, 2, run, 0)
        for at in range(4):
            copy_out(at).wait()

    smem = pl.BlockSpec(memory_space=pltpu.SMEM)
    anywhere = pl.BlockSpec(memory_space=pl.ANY)
    return pl.pallas_call(
        kernel,
        in_specs=[smem] + [anywhere] * (3 + joined),
        out_specs=[anywhere] * 4 + [smem],
        out_shape=[HALF_MSG if coded else HALF_RAW] * 4 + [jax.ShapeDtypeStruct((4,), jnp.int32)],
        scratch_shapes=[
            pltpu.VMEM((2, SIDE, QT, width), jnp.bfloat16),
            pltpu.VMEM((2, CAP, width), jnp.bfloat16),
            pltpu.VMEM((2, CAP, CB), jnp.bfloat16),
            pltpu.VMEM((SUPER, CAP), jnp.bfloat16),
            pltpu.VMEM((2, SUPER, CB), jnp.float32),
            pltpu.VMEM((4,) + HALF_MSG.shape, jnp.int16),
            pltpu.VMEM((4,) + HALF_MSG.shape, jnp.int16),
            pltpu.SemaphoreType.DMA((2, SIDE)),
            pltpu.SemaphoreType.DMA((2, TILES)),
            pltpu.SemaphoreType.DMA((2,)),
            pltpu.SemaphoreType.DMA((4,)),
            pltpu.SemaphoreType.DMA((4,)),
        ],
        compiler_params=params(),
        cost_estimate=pl.CostEstimate(
            flops=2 * 4 * HALF * CAP * (width + CB),
            bytes_accessed=8 * HALF * width,
            transcendentals=2 * HALF * CAP,
        ),
        name="sums",
    )(facts, queries, keys, hots, *arrived)


def turn(place, low, high, low_came, high_came):
    def kernel(place_ref, low_hbm, high_hbm, low_msg, high_msg, own_hbm, plus_hbm, far_hbm, minus_hbm, *scratch):
        raw_ref, came_ref, msg_ref, own_ref, raw_sems, came_sems, out_sems = scratch

        def loads(half):
            raw, came = ((low_hbm, low_msg), (high_hbm, high_msg))[half]
            return (
                pltpu.make_async_copy(raw, raw_ref.at[half], raw_sems.at[half]),
                pltpu.make_async_copy(came, came_ref.at[half], came_sems.at[half]),
            )

        for half in range(2):
            for load in loads(half):
                load.start()
        for k in range(3):
            clear_tail(msg_ref.at[k], QT)
        for half in range(2):
            for load in loads(half):
                load.wait()

        def values(k):
            tile = lax.rem(place_ref[0] + k, SIDE)
            half, at = tile // 2, tile % 2
            return raw_ref[half, pl.ds(aligned(at * QT), QT), :] + decode(came_ref.at[half], at, HALF)

        def body(i, carry):
            k = jnp.where(i == 0, 2, jnp.where(i == 1, 1, 3))
            encode(values(k), msg_ref.at[i], 0, QT)
            return carry

        outs = [
            pltpu.make_async_copy(msg_ref.at[i], out, out_sems.at[i])
            for i, out in enumerate((far_hbm, plus_hbm, minus_hbm))
        ]
        outs.append(pltpu.make_async_copy(own_ref, own_hbm, out_sems.at[3]))
        lax.fori_loop(0, 3, body, 0)
        for out in outs[:3]:
            out.start()
        own_ref[...] = values(0)
        outs[3].start()
        for out in outs:
            out.wait()

    anywhere = pl.BlockSpec(memory_space=pl.ANY)
    return pl.pallas_call(
        kernel,
        in_specs=[pl.BlockSpec(memory_space=pltpu.SMEM)] + [anywhere] * 4,
        out_specs=[anywhere] * 4,
        out_shape=[jax.ShapeDtypeStruct((QT, CB), jnp.float32), TILE_MSG, TILE_MSG, TILE_MSG],
        scratch_shapes=[
            pltpu.VMEM((2, HALF, CB), jnp.float32),
            pltpu.VMEM((2,) + HALF_MSG.shape, jnp.int16),
            pltpu.VMEM((3,) + TILE_MSG.shape, jnp.int16),
            pltpu.VMEM((QT, CB), jnp.float32),
            pltpu.SemaphoreType.DMA((2,)),
            pltpu.SemaphoreType.DMA((2,)),
            pltpu.SemaphoreType.DMA((4,)),
        ],
        compiler_params=params(),
        cost_estimate=pl.CostEstimate(flops=40 * QT * CB, bytes_accessed=40 * QT * CB, transcendentals=0),
        name="turn",
    )(place, low, high, low_came, high_came)


def close(text, own_a, msgs_a, own_b, msgs_b):
    def kernel(text_ref, *rest):
        own, msgs = rest[0:2], (rest[2:5], rest[5:8])
        logits_ref, stats_ref = rest[8:]
        for block in range(2):
            total = own[block][...]
            for msg in msgs[block]:
                total += decode(msg, 0, QT)
            at = slice(block * CB, block * CB + CB)
            logits_ref[:, at] = text_ref[:, at] + total
        logits = logits_ref[...]
        largest = jnp.max(logits, axis=1, keepdims=True)
        total = jnp.sum(jnp.exp(logits - largest), axis=1, keepdims=True)
        eye = diagonal()
        stats_ref[0:1, :] = jnp.sum(jnp.where(eye, largest, 0.0), axis=0, keepdims=True)
        stats_ref[1:2, :] = jnp.sum(jnp.where(eye, total, 0.0), axis=0, keepdims=True)

    return pl.pallas_call(
        kernel,
        out_shape=[
            jax.ShapeDtypeStruct((QT, 2 * CB), jnp.float32),
            jax.ShapeDtypeStruct((2, QT), jnp.float32),
        ],
        compiler_params=params(24),
        cost_estimate=pl.CostEstimate(flops=30 * QT * CB, bytes_accessed=40 * QT * CB, transcendentals=QT * CB),
        name="close",
    )(text, own_a, own_b, *msgs_a, *msgs_b)


def finish(logits, stats):
    def kernel(logits_ref, stats_ref, out_ref):
        largest = jnp.max(stats_ref[:, 0, :], axis=0, keepdims=True)
        total = jnp.sum(stats_ref[:, 1, :] * jnp.exp(stats_ref[:, 0, :] - largest), axis=0, keepdims=True)
        eye = diagonal()
        largest = jnp.sum(jnp.where(eye, largest, 0.0), axis=1, keepdims=True)
        shift = jnp.sum(jnp.where(eye, jnp.log(total), 0.0), axis=1, keepdims=True)
        out_ref[...] = logits_ref[...] - largest - shift

    return pl.pallas_call(
        kernel,
        out_shape=jax.ShapeDtypeStruct(logits.shape, jnp.float32),
        compiler_params=params(24),
        name="finish",
    )(logits, stats)


def shifted(dx, dz):
    return [
        (x * SIDE + z, (x + dx) % SIDE * SIDE + (z + dz) % SIDE) for x in range(SIDE) for z in range(SIDE)
    ]


def send(message, dx, dz):
    return lax.ppermute(message, "cache", shifted(dx, dz))


def per_device(queries, cache_keys, labels, prototypes):
    width = queries.shape[1]
    own = lax.axis_index("cache")
    x, z = own // SIDE, own % SIDE
    low = lax.axis_index("cls") * (2 * CB)

    gathered = lax.all_gather(unit_rows(queries), ("cache", "cls"), axis=0, tiled=True)

    order = lax.sort(labels * 16384 + lax.iota(jnp.int32, labels.shape[0]), is_stable=False)
    start = jnp.sum((labels < low).astype(jnp.int32))
    middle = jnp.sum((labels < low + CB).astype(jnp.int32))
    stop = jnp.sum((labels < low + 2 * CB).astype(jnp.int32))
    padded = jnp.concatenate([order, jnp.zeros((CAP,), jnp.int32)])
    picked = jnp.concatenate(
        [lax.dynamic_slice(padded, (start,), (CAP,)), lax.dynamic_slice(padded, (middle,), (CAP,))]
    )
    counts = jnp.stack([middle - start, stop - middle])
    place = lax.iota(jnp.int32, 2 * CAP)
    block = place // CAP
    valid = place - block * CAP < jnp.where(block == 0, counts[0], counts[1])
    local = jnp.where(valid, picked // 16384 - low - block * CB, -1)
    rows = jnp.take(cache_keys, picked % 16384, axis=0, mode="clip")
    keys, hots = prepare(rows, local)
    tiles = (counts + KT - 1) // KT
    gathered, keys, hots = lax.optimization_barrier((gathered, keys, hots))
    q3 = gathered.reshape(SIDE * SIDE, QT, width)
    facts = jnp.stack([x, z, tiles[0], tiles[1]]).astype(jnp.int32)

    def run(facts, shifts, halves, coded, arrived=()):
        *parts, facts = sums(shifts, halves, coded, facts, q3, keys, hots, arrived)
        return parts, facts

    def send_all(parts):
        a_right, a_left, b_right, b_left = parts
        return send(a_right, 1, 0), send(a_left, -1, 0), send(b_right, 0, 1), send(b_left, 0, -1)

    far, facts = run(facts, (2, 2), (0, 1), True)
    far = send_all(far)
    free, facts = run(facts, (1, 3), (1, 0), True)
    free = send_all(free)
    full, facts = run(facts, (1, 3), (0, 1), True, far)
    full = send_all(full)
    a_low, a_high, b_low, b_high = run(
        facts, (0, 0), (0, 1), False, (free[1], free[0], free[3], free[2])
    )[0]

    text = text_scale * lax.dot_general(
        lax.dynamic_index_in_dim(q3, own, 0, keepdims=False),
        prototypes,
        (((1,), (1,)), ((), ())),
        preferred_element_type=jnp.float32,
    )

    own_a, a_plus, a_far, a_minus = turn(z[None], a_low, a_high, full[0], full[1])
    own_b, b_plus, b_far, b_minus = turn(x[None], b_low, b_high, full[2], full[3])
    a_msgs = send(a_far, 0, 2), send(a_plus, 0, 1), send(a_minus, 0, -1)
    b_msgs = send(b_far, 2, 0), send(b_plus, 1, 0), send(b_minus, -1, 0)

    logits, stats = close(text, own_a, a_msgs, own_b, b_msgs)
    return finish(logits, lax.all_gather(stats, "cls"))


def solution(mesh):
    placed = (P(("cache", "cls"), None), P("cache", None), P("cache"), P("cls", None))
    return jax.shard_map(
        per_device, mesh=mesh, in_specs=placed, out_specs=P("cache", "cls"), check_vma=False
    )
```

```python
import math

import jax
import jax.numpy as jnp
from jax import lax
from jax.experimental import pallas as pl
from jax.experimental.pallas import tpu as pltpu
from jax.sharding import PartitionSpec as P

text_scale = 100.0
epsilon = 1e-06
SIDE = 4
CB = 640
CAP = 1280
QT = 256
KT = 256
TAIL = 16


def params(mib=36):
    return pltpu.CompilerParams(vmem_limit_bytes=mib * 1024 * 1024)


def unit_rows(matrix):
    widened = matrix.astype(jnp.float32)
    return (widened / jnp.sqrt(jnp.sum(widened * widened, axis=1, keepdims=True) + epsilon)).astype(
        jnp.bfloat16
    )


def prepare_kernel(facts_ref, rows_ref, labels_ref, unit_ref, hot_ref, next_ref):
    for at in range(4):
        next_ref[at] = facts_ref[at]
    unit_ref[...] = unit_rows(rows_ref[...])
    classes = lax.broadcasted_iota(jnp.int32, (KT, CB), 1)
    labels = jnp.sum(jnp.where(diagonal(), labels_ref[0], 0), axis=1, keepdims=True)
    hot_ref[...] = jnp.where(labels == classes, 1.0, 0.0).astype(jnp.bfloat16)


def prepare(facts, rows, labels):
    count, width = rows.shape
    return pl.pallas_call(
        prepare_kernel,
        grid=(count // KT,),
        in_specs=[
            pl.BlockSpec(memory_space=pltpu.SMEM),
            pl.BlockSpec((KT, width), lambda i: (i, 0)),
            pl.BlockSpec((1, 1, KT), lambda i: (i, 0, 0)),
        ],
        out_specs=[
            pl.BlockSpec((KT, width), lambda i: (i, 0)),
            pl.BlockSpec((KT, CB), lambda i: (i, 0)),
            pl.BlockSpec(memory_space=pltpu.SMEM),
        ],
        out_shape=[
            jax.ShapeDtypeStruct((count, width), jnp.bfloat16),
            jax.ShapeDtypeStruct((count, CB), jnp.bfloat16),
            jax.ShapeDtypeStruct((4,), jnp.int32),
        ],
        compiler_params=params(),
        cost_estimate=pl.CostEstimate(flops=count * width * 4, bytes_accessed=count * width * 6, transcendentals=count),
        name="prepare",
    )(facts, rows, labels.reshape(count // KT, 1, KT))


def aligned(value):
    return pl.multiple_of(value, QT)


def diagonal():
    shape = (QT, QT)
    return lax.broadcasted_iota(jnp.int32, shape, 0) == lax.broadcasted_iota(jnp.int32, shape, 1)


def encode(values, message_ref, tile, tail_row):
    largest = jnp.maximum(jnp.max(values, axis=1, keepdims=True), 1e-30)
    exponent = jnp.ceil(jnp.log2(largest) - 14.99)
    codes = (values * jnp.exp2(-exponent) + 0.5).astype(jnp.int32)
    message_ref[pl.ds(aligned(tile * QT), QT), :] = codes.astype(jnp.int16)
    along = jnp.sum(jnp.where(diagonal(), exponent, 0.0), axis=0, keepdims=True)
    shape = (TAIL, QT)
    old = message_ref[tail_row : tail_row + TAIL, :QT].astype(jnp.int32)
    new = jnp.broadcast_to(along, shape).astype(jnp.int32)
    at = lax.broadcasted_iota(jnp.int32, shape, 0) == tile
    message_ref[tail_row : tail_row + TAIL, :QT] = jnp.where(at, new, old).astype(jnp.int16)


def clear_tail(message_ref, tail_row):
    message_ref[tail_row : tail_row + TAIL, :] = jnp.zeros((TAIL, CB), jnp.int16)


def decode(message_ref, tile, tail_row):
    shape = (TAIL, QT)
    tail = message_ref[tail_row : tail_row + TAIL, :QT].astype(jnp.float32)
    at = lax.broadcasted_iota(jnp.int32, shape, 0) == tile
    along = jnp.sum(jnp.where(at, tail, 0.0), axis=0, keepdims=True)
    exponent = jnp.sum(jnp.where(diagonal(), along, 0.0), axis=1, keepdims=True)
    codes = message_ref[pl.ds(aligned(tile * QT), QT), :].astype(jnp.float32)
    return codes * jnp.exp2(exponent)


HALF = 2 * QT
HALF_MSG = jax.ShapeDtypeStruct((HALF + TAIL, CB), jnp.int16)
TILE_MSG = jax.ShapeDtypeStruct((QT + TAIL, CB), jnp.int16)
HALF_RAW = jax.ShapeDtypeStruct((HALF, CB), jnp.float32)


SUPER = SIDE * QT
COMMON = 3
TILES = CAP // KT


def super_sums(tiles, wait_keys, wait_hots, q_ref, keys_ref, hot_ref, scores_ref, total_ref):
    width = q_ref.shape[-1]
    sharpness = float(width) ** 0.5 * math.log2(math.e)
    queries = q_ref[...].reshape(SUPER, width)

    def step(t, carry):
        wait_keys(t)
        at = pl.ds(aligned(t * KT), KT)
        cosine = lax.dot_general(
            queries, keys_ref[at, :], (((1,), (1,)), ((), ())), preferred_element_type=jnp.float32
        )
        scores_ref[:, at] = jnp.exp2(sharpness * cosine).astype(jnp.bfloat16)
        return carry

    lax.fori_loop(0, tiles, step, 0)
    wait_hots()
    cut = COMMON * KT
    total_ref[...] = jnp.dot(
        scores_ref[:, :cut], hot_ref[:cut, :], preferred_element_type=jnp.float32
    )

    @pl.when(tiles > COMMON)
    def _():
        total_ref[...] += jnp.dot(
            scores_ref[:, cut:], hot_ref[cut:, :], preferred_element_type=jnp.float32
        )


def sums(shifts, halves, coded, facts, queries, keys, hots, arrived=()):
    width = keys.shape[1]
    joined = len(arrived)

    def kernel(facts_ref, q_hbm, keys_hbm, hot_hbm, *rest):
        came, outs, next_ref = rest[:joined], rest[joined : joined + 4], rest[joined + 4]
        scratch = rest[joined + 5 :]
        q_ref, keys_ref, hot_ref, scores_ref, total_ref, came_ref, msg_ref = scratch[:7]
        q_sems, key_sems, hot_sems, came_sems, out_sems = scratch[7:]
        for at in range(4):
            next_ref[at] = facts_ref[at]

        def copy_queries(block, part):
            away = shifts[part // 2]
            inner = halves[part // 2] * 2 + part % 2
            outer = lax.rem(facts_ref[block] + away, SIDE)
            chunk = jnp.where(block == 0, outer * SIDE + inner, inner * SIDE + outer)
            return pltpu.make_async_copy(q_hbm.at[chunk], q_ref.at[block, part], q_sems.at[block, part])

        def copy_keys(block, t):
            return pltpu.make_async_copy(
                keys_hbm.at[pl.ds(aligned(block * CAP + t * KT), KT), :],
                keys_ref.at[block, pl.ds(aligned(t * KT), KT), :],
                key_sems.at[block, t],
            )

        def copy_hots(block):
            return pltpu.make_async_copy(
                hot_hbm.at[pl.ds(aligned(block * CAP), CAP), :], hot_ref.at[block], hot_sems.at[block]
            )

        def copy_came(at):
            return pltpu.make_async_copy(came[at], came_ref.at[at], came_sems.at[at])

        def copy_out(at):
            source = msg_ref.at[at] if coded else total_ref.at[at // 2, pl.ds(at % 2 * HALF, HALF), :]
            return pltpu.make_async_copy(source, outs[at], out_sems.at[at])

        for block in range(2):
            for part in range(SIDE):
                copy_queries(block, part).start()

            def start(t, carry, block=block):
                copy_keys(block, t).start()
                return carry

            lax.fori_loop(0, facts_ref[2 + block], start, 0)
            copy_hots(block).start()
        for at in range(joined):
            copy_came(at).start()
        scores_ref[:, COMMON * KT :] = jnp.zeros((SUPER, CAP - COMMON * KT), jnp.bfloat16)
        if coded:
            for at in range(4):
                clear_tail(msg_ref.at[at], HALF)

        def run(block, carry):
            for part in range(SIDE):
                copy_queries(block, part).wait()
            super_sums(
                facts_ref[2 + block],
                lambda t: copy_keys(block, t).wait(),
                lambda: copy_hots(block).wait(),
                q_ref.at[block],
                keys_ref.at[block],
                hot_ref.at[block],
                scores_ref,
                total_ref.at[block],
            )
            if joined:
                @pl.when(block == 0)
                def _():
                    for at in range(joined):
                        copy_came(at).wait()

            if joined or coded:
                def body(t, carry):
                    rows = pl.ds(aligned(t * QT), QT)
                    at = 2 * block + t // 2
                    values = total_ref[block, rows, :]
                    if joined:
                        values += decode(came_ref.at[at], t % 2, HALF)
                    if coded:
                        encode(values, msg_ref.at[at], t % 2, HALF)
                    else:
                        total_ref[block, rows, :] = values
                    return carry

                lax.fori_loop(0, SIDE, body, 0)
            for at in range(4):
                @pl.when(block == at // 2)
                def _(at=at):
                    copy_out(at).start()
            return carry

        lax.fori_loop(0, 2, run, 0)
        for at in range(4):
            copy_out(at).wait()

    smem = pl.BlockSpec(memory_space=pltpu.SMEM)
    anywhere = pl.BlockSpec(memory_space=pl.ANY)
    return pl.pallas_call(
        kernel,
        in_specs=[smem] + [anywhere] * (3 + joined),
        out_specs=[anywhere] * 4 + [smem],
        out_shape=[HALF_MSG if coded else HALF_RAW] * 4 + [jax.ShapeDtypeStruct((4,), jnp.int32)],
        scratch_shapes=[
            pltpu.VMEM((2, SIDE, QT, width), jnp.bfloat16),
            pltpu.VMEM((2, CAP, width), jnp.bfloat16),
            pltpu.VMEM((2, CAP, CB), jnp.bfloat16),
            pltpu.VMEM((SUPER, CAP), jnp.bfloat16),
            pltpu.VMEM((2, SUPER, CB), jnp.float32),
            pltpu.VMEM((4,) + HALF_MSG.shape, jnp.int16),
            pltpu.VMEM((4,) + HALF_MSG.shape, jnp.int16),
            pltpu.SemaphoreType.DMA((2, SIDE)),
            pltpu.SemaphoreType.DMA((2, TILES)),
            pltpu.SemaphoreType.DMA((2,)),
            pltpu.SemaphoreType.DMA((4,)),
            pltpu.SemaphoreType.DMA((4,)),
        ],
        compiler_params=params(),
        cost_estimate=pl.CostEstimate(
            flops=2 * 4 * HALF * CAP * (width + CB),
            bytes_accessed=8 * HALF * width,
            transcendentals=2 * HALF * CAP,
        ),
        name="sums",
    )(facts, queries, keys, hots, *arrived)


def turn(place, low, high, low_came, high_came):
    def kernel(place_ref, low_hbm, high_hbm, low_msg, high_msg, own_hbm, plus_hbm, far_hbm, minus_hbm, *scratch):
        raw_ref, came_ref, msg_ref, own_ref, raw_sems, came_sems, out_sems = scratch

        def loads(half):
            raw, came = ((low_hbm, low_msg), (high_hbm, high_msg))[half]
            return (
                pltpu.make_async_copy(raw, raw_ref.at[half], raw_sems.at[half]),
                pltpu.make_async_copy(came, came_ref.at[half], came_sems.at[half]),
            )

        for half in range(2):
            for load in loads(half):
                load.start()
        for k in range(3):
            clear_tail(msg_ref.at[k], QT)
        for half in range(2):
            for load in loads(half):
                load.wait()

        def values(k):
            tile = lax.rem(place_ref[0] + k, SIDE)
            half, at = tile // 2, tile % 2
            return raw_ref[half, pl.ds(aligned(at * QT), QT), :] + decode(came_ref.at[half], at, HALF)

        def body(i, carry):
            k = jnp.where(i == 0, 2, jnp.where(i == 1, 1, 3))
            encode(values(k), msg_ref.at[i], 0, QT)
            return carry

        outs = [
            pltpu.make_async_copy(msg_ref.at[i], out, out_sems.at[i])
            for i, out in enumerate((far_hbm, plus_hbm, minus_hbm))
        ]
        outs.append(pltpu.make_async_copy(own_ref, own_hbm, out_sems.at[3]))
        lax.fori_loop(0, 3, body, 0)
        for out in outs[:3]:
            out.start()
        own_ref[...] = values(0)
        outs[3].start()
        for out in outs:
            out.wait()

    anywhere = pl.BlockSpec(memory_space=pl.ANY)
    return pl.pallas_call(
        kernel,
        in_specs=[pl.BlockSpec(memory_space=pltpu.SMEM)] + [anywhere] * 4,
        out_specs=[anywhere] * 4,
        out_shape=[jax.ShapeDtypeStruct((QT, CB), jnp.float32), TILE_MSG, TILE_MSG, TILE_MSG],
        scratch_shapes=[
            pltpu.VMEM((2, HALF, CB), jnp.float32),
            pltpu.VMEM((2,) + HALF_MSG.shape, jnp.int16),
            pltpu.VMEM((3,) + TILE_MSG.shape, jnp.int16),
            pltpu.VMEM((QT, CB), jnp.float32),
            pltpu.SemaphoreType.DMA((2,)),
            pltpu.SemaphoreType.DMA((2,)),
            pltpu.SemaphoreType.DMA((4,)),
        ],
        compiler_params=params(),
        cost_estimate=pl.CostEstimate(flops=40 * QT * CB, bytes_accessed=40 * QT * CB, transcendentals=0),
        name="turn",
    )(place, low, high, low_came, high_came)


def close(text, own_a, msgs_a, own_b, msgs_b):
    def kernel(text_ref, *rest):
        own, msgs = rest[0:2], (rest[2:5], rest[5:8])
        logits_ref, stats_ref = rest[8:]
        for block in range(2):
            total = own[block][...]
            for msg in msgs[block]:
                total += decode(msg, 0, QT)
            at = slice(block * CB, block * CB + CB)
            logits_ref[:, at] = text_ref[:, at] + total
        logits = logits_ref[...]
        largest = jnp.max(logits, axis=1, keepdims=True)
        total = jnp.sum(jnp.exp(logits - largest), axis=1, keepdims=True)
        eye = diagonal()
        stats_ref[0:1, :] = jnp.sum(jnp.where(eye, largest, 0.0), axis=0, keepdims=True)
        stats_ref[1:2, :] = jnp.sum(jnp.where(eye, total, 0.0), axis=0, keepdims=True)

    return pl.pallas_call(
        kernel,
        out_shape=[
            jax.ShapeDtypeStruct((QT, 2 * CB), jnp.float32),
            jax.ShapeDtypeStruct((2, QT), jnp.float32),
        ],
        compiler_params=params(),
        cost_estimate=pl.CostEstimate(flops=30 * QT * CB, bytes_accessed=40 * QT * CB, transcendentals=QT * CB),
        name="close",
    )(text, own_a, own_b, *msgs_a, *msgs_b)


def finish(logits, stats):
    def kernel(logits_ref, stats_ref, out_ref):
        largest = jnp.max(stats_ref[:, 0, :], axis=0, keepdims=True)
        total = jnp.sum(stats_ref[:, 1, :] * jnp.exp(stats_ref[:, 0, :] - largest), axis=0, keepdims=True)
        eye = diagonal()
        largest = jnp.sum(jnp.where(eye, largest, 0.0), axis=1, keepdims=True)
        shift = jnp.sum(jnp.where(eye, jnp.log(total), 0.0), axis=1, keepdims=True)
        out_ref[...] = logits_ref[...] - largest - shift

    return pl.pallas_call(
        kernel,
        out_shape=jax.ShapeDtypeStruct(logits.shape, jnp.float32),
        compiler_params=params(),
        name="finish",
    )(logits, stats)


def shifted(dx, dz):
    return [
        (x * SIDE + z, (x + dx) % SIDE * SIDE + (z + dz) % SIDE) for x in range(SIDE) for z in range(SIDE)
    ]


def send(message, dx, dz):
    return lax.ppermute(message, "cache", shifted(dx, dz))


def per_device(queries, cache_keys, labels, prototypes):
    width = queries.shape[1]
    own = lax.axis_index("cache")
    x, z = own // SIDE, own % SIDE
    low = lax.axis_index("cls") * (2 * CB)

    unit_queries = unit_rows(queries)
    gathered = lax.all_gather(unit_queries, ("cache", "cls"), axis=0, tiled=True)

    order = lax.sort(labels * 16384 + lax.iota(jnp.int32, labels.shape[0]), is_stable=False)
    start = jnp.sum((labels < low).astype(jnp.int32))
    middle = jnp.sum((labels < low + CB).astype(jnp.int32))
    stop = jnp.sum((labels < low + 2 * CB).astype(jnp.int32))
    padded = jnp.concatenate([order, jnp.zeros((CAP,), jnp.int32)])
    picked = jnp.concatenate(
        [lax.dynamic_slice(padded, (start,), (CAP,)), lax.dynamic_slice(padded, (middle,), (CAP,))]
    )
    counts = jnp.stack([middle - start, stop - middle])
    place = lax.iota(jnp.int32, 2 * CAP)
    block = place // CAP
    valid = place - block * CAP < jnp.where(block == 0, counts[0], counts[1])
    local = jnp.where(valid, picked // 16384 - low - block * CB, -1)
    rows = jnp.take(cache_keys, picked % 16384, axis=0, mode="clip")
    text = text_scale * lax.dot_general(
        lax.all_gather(unit_queries, "cls", axis=0, tiled=True),
        prototypes,
        (((1,), (1,)), ((), ())),
        preferred_element_type=jnp.float32,
    )
    rows, text = lax.optimization_barrier((rows, text))
    tiles = jnp.maximum((counts + KT - 1) // KT, COMMON)
    facts = jnp.stack([x, z, tiles[0], tiles[1]]).astype(jnp.int32)
    keys, hots, facts = prepare(facts, rows, local)
    gathered, facts = lax.optimization_barrier((gathered, facts))
    q3 = gathered.reshape(SIDE * SIDE, QT, width)

    def run(facts, shifts, halves, coded, arrived=()):
        *parts, facts = sums(shifts, halves, coded, facts, q3, keys, hots, arrived)
        return parts, facts

    def send_all(parts):
        a_right, a_left, b_right, b_left = parts
        return send(a_right, 1, 0), send(a_left, -1, 0), send(b_right, 0, 1), send(b_left, 0, -1)

    far, facts = run(facts, (2, 2), (0, 1), True)
    far = send_all(far)
    free, facts = run(facts, (1, 3), (1, 0), True)
    free = send_all(free)
    full, facts = run(facts, (1, 3), (0, 1), True, far)
    full = send_all(full)
    a_low, a_high, b_low, b_high = run(
        facts, (0, 0), (0, 1), False, (free[1], free[0], free[3], free[2])
    )[0]

    own_a, a_plus, a_far, a_minus = turn(z[None], a_low, a_high, full[0], full[1])
    own_b, b_plus, b_far, b_minus = turn(x[None], b_low, b_high, full[2], full[3])
    a_msgs = send(a_far, 0, 2), send(a_plus, 0, 1), send(a_minus, 0, -1)
    b_msgs = send(b_far, 2, 0), send(b_plus, 1, 0), send(b_minus, -1, 0)

    logits, stats = close(text, own_a, a_msgs, own_b, b_msgs)
    return finish(logits, lax.all_gather(stats, "cls"))


def solution(mesh):
    placed = (P(("cache", "cls"), None), P("cache", None), P("cache"), P("cls", None))
    return jax.shard_map(
        per_device, mesh=mesh, in_specs=placed, out_specs=P("cache", "cls"), check_vma=False
    )
```

```python
import math

import jax
import jax.numpy as jnp
from jax import lax
from jax.experimental import pallas as pl
from jax.experimental.pallas import tpu as pltpu
from jax.sharding import PartitionSpec as P

text_scale = 100.0
epsilon = 1e-06
SIDE = 4
CB = 640
CAP = 1280
QT = 256
KT = 256
TAIL = 16


def params(mib=44):
    return pltpu.CompilerParams(vmem_limit_bytes=mib * 1024 * 1024)


def unit_rows(matrix):
    widened = matrix.astype(jnp.float32)
    return (widened / jnp.sqrt(jnp.sum(widened * widened, axis=1, keepdims=True) + epsilon)).astype(
        jnp.bfloat16
    )


def prepare_kernel(facts_ref, rows_ref, labels_ref, unit_ref, hot_ref, next_ref):
    for at in range(4):
        next_ref[at] = facts_ref[at]
    unit_ref[...] = unit_rows(rows_ref[...])
    classes = lax.broadcasted_iota(jnp.int32, (KT, CB), 1)
    labels = jnp.sum(jnp.where(diagonal(), labels_ref[0], 0), axis=1, keepdims=True)
    hot_ref[...] = jnp.where(labels == classes, 1.0, 0.0).astype(jnp.bfloat16)


def prepare(facts, rows, labels):
    count, width = rows.shape
    return pl.pallas_call(
        prepare_kernel,
        grid=(count // KT,),
        in_specs=[
            pl.BlockSpec(memory_space=pltpu.SMEM),
            pl.BlockSpec((KT, width), lambda i: (i, 0)),
            pl.BlockSpec((1, 1, KT), lambda i: (i, 0, 0)),
        ],
        out_specs=[
            pl.BlockSpec((KT, width), lambda i: (i, 0)),
            pl.BlockSpec((KT, CB), lambda i: (i, 0)),
            pl.BlockSpec(memory_space=pltpu.SMEM),
        ],
        out_shape=[
            jax.ShapeDtypeStruct((count, width), jnp.bfloat16),
            jax.ShapeDtypeStruct((count, CB), jnp.bfloat16),
            jax.ShapeDtypeStruct((4,), jnp.int32),
        ],
        compiler_params=params(),
        cost_estimate=pl.CostEstimate(flops=count * width * 4, bytes_accessed=count * width * 6, transcendentals=count),
        name="prepare",
    )(facts, rows, labels.reshape(count // KT, 1, KT))


def unit_kernel(rows_ref, unit_ref):
    unit_ref[...] = unit_rows(rows_ref[...])


def unit_small(rows):
    return pl.pallas_call(
        unit_kernel,
        out_shape=jax.ShapeDtypeStruct(rows.shape, jnp.bfloat16),
        compiler_params=params(),
        name="unit",
    )(rows)


def aligned(value):
    return pl.multiple_of(value, QT)


def diagonal():
    shape = (QT, QT)
    return lax.broadcasted_iota(jnp.int32, shape, 0) == lax.broadcasted_iota(jnp.int32, shape, 1)


def encode(values, message_ref, tile, tail_row):
    largest = jnp.maximum(jnp.max(values, axis=1, keepdims=True), 1e-30)
    exponent = jnp.ceil(jnp.log2(largest) - 14.99)
    codes = (values * jnp.exp2(-exponent) + 0.5).astype(jnp.int32)
    message_ref[pl.ds(aligned(tile * QT), QT), :] = codes.astype(jnp.int16)
    along = jnp.sum(jnp.where(diagonal(), exponent, 0.0), axis=0, keepdims=True)
    shape = (TAIL, QT)
    old = message_ref[tail_row : tail_row + TAIL, :QT].astype(jnp.int32)
    new = jnp.broadcast_to(along, shape).astype(jnp.int32)
    at = lax.broadcasted_iota(jnp.int32, shape, 0) == tile
    message_ref[tail_row : tail_row + TAIL, :QT] = jnp.where(at, new, old).astype(jnp.int16)


def clear_tail(message_ref, tail_row):
    message_ref[tail_row : tail_row + TAIL, :] = jnp.zeros((TAIL, CB), jnp.int16)


def decode(message_ref, tile, tail_row):
    shape = (TAIL, QT)
    tail = message_ref[tail_row : tail_row + TAIL, :QT].astype(jnp.float32)
    at = lax.broadcasted_iota(jnp.int32, shape, 0) == tile
    along = jnp.sum(jnp.where(at, tail, 0.0), axis=0, keepdims=True)
    exponent = jnp.sum(jnp.where(diagonal(), along, 0.0), axis=1, keepdims=True)
    codes = message_ref[pl.ds(aligned(tile * QT), QT), :].astype(jnp.float32)
    return codes * jnp.exp2(exponent)


HALF = 2 * QT
HALF_MSG = jax.ShapeDtypeStruct((HALF + TAIL, CB), jnp.int16)
TILE_MSG = jax.ShapeDtypeStruct((QT + TAIL, CB), jnp.int16)
HALF_RAW = jax.ShapeDtypeStruct((HALF, CB), jnp.float32)


SUPER = SIDE * QT
COMMON = 3
TILES = CAP // KT


def super_sums(tiles, wait_keys, wait_hots, q_ref, keys_ref, hot_ref, scores_ref, total_ref):
    width = q_ref.shape[-1]
    sharpness = float(width) ** 0.5 * math.log2(math.e)
    queries = q_ref[...].reshape(SUPER, width)

    def step(t, carry):
        wait_keys(t)
        at = pl.ds(aligned(t * KT), KT)
        cosine = lax.dot_general(
            queries, keys_ref[at, :], (((1,), (1,)), ((), ())), preferred_element_type=jnp.float32
        )
        scores_ref[:, at] = jnp.exp2(sharpness * cosine).astype(jnp.bfloat16)
        return carry

    lax.fori_loop(0, tiles, step, 0)
    wait_hots()
    cut = COMMON * KT
    total_ref[...] = jnp.dot(
        scores_ref[:, :cut], hot_ref[:cut, :], preferred_element_type=jnp.float32
    )

    @pl.when(tiles > COMMON)
    def _():
        total_ref[...] += jnp.dot(
            scores_ref[:, cut:], hot_ref[cut:, :], preferred_element_type=jnp.float32
        )


def sums(shifts, halves, coded, facts, queries, keys, hots, arrived=()):
    width = keys.shape[1]
    joined = len(arrived)

    def kernel(facts_ref, q_hbm, keys_hbm, hot_hbm, *rest):
        came, outs, next_ref = rest[:joined], rest[joined : joined + 4], rest[joined + 4]
        scratch = rest[joined + 5 :]
        q_ref, keys_ref, hot_ref, scores_ref, total_ref, came_ref, msg_ref = scratch[:7]
        q_sems, key_sems, hot_sems, came_sems, out_sems = scratch[7:]
        for at in range(4):
            next_ref[at] = facts_ref[at]

        def copy_queries(block, part):
            away = shifts[part // 2]
            inner = halves[part // 2] * 2 + part % 2
            outer = lax.rem(facts_ref[block] + away, SIDE)
            chunk = jnp.where(block == 0, outer * SIDE + inner, inner * SIDE + outer)
            return pltpu.make_async_copy(q_hbm.at[chunk], q_ref.at[block, part], q_sems.at[block, part])

        def copy_keys(block, t):
            return pltpu.make_async_copy(
                keys_hbm.at[pl.ds(aligned(block * CAP + t * KT), KT), :],
                keys_ref.at[block, pl.ds(aligned(t * KT), KT), :],
                key_sems.at[block, t],
            )

        def copy_hots(block):
            return pltpu.make_async_copy(
                hot_hbm.at[pl.ds(aligned(block * CAP), CAP), :], hot_ref.at[block], hot_sems.at[block]
            )

        def copy_came(at):
            return pltpu.make_async_copy(came[at], came_ref.at[at], came_sems.at[at])

        def copy_out(at):
            source = msg_ref.at[at] if coded else total_ref.at[at // 2, pl.ds(at % 2 * HALF, HALF), :]
            return pltpu.make_async_copy(source, outs[at], out_sems.at[at])

        for block in range(2):
            for part in range(SIDE):
                copy_queries(block, part).start()

            def start(t, carry, block=block):
                copy_keys(block, t).start()
                return carry

            lax.fori_loop(0, facts_ref[2 + block], start, 0)
            copy_hots(block).start()
        for at in range(joined):
            copy_came(at).start()
        scores_ref[:, COMMON * KT :] = jnp.zeros((SUPER, CAP - COMMON * KT), jnp.bfloat16)
        if coded:
            for at in range(4):
                clear_tail(msg_ref.at[at], HALF)

        def run(block, carry):
            for part in range(SIDE):
                copy_queries(block, part).wait()
            super_sums(
                facts_ref[2 + block],
                lambda t: copy_keys(block, t).wait(),
                lambda: copy_hots(block).wait(),
                q_ref.at[block],
                keys_ref.at[block],
                hot_ref.at[block],
                scores_ref,
                total_ref.at[block],
            )
            if joined:
                @pl.when(block == 0)
                def _():
                    for at in range(joined):
                        copy_came(at).wait()

            if joined or coded:
                def body(t, carry):
                    rows = pl.ds(aligned(t * QT), QT)
                    at = 2 * block + t // 2
                    values = total_ref[block, rows, :]
                    if joined:
                        values += decode(came_ref.at[at], t % 2, HALF)
                    if coded:
                        encode(values, msg_ref.at[at], t % 2, HALF)
                    else:
                        total_ref[block, rows, :] = values
                    return carry

                lax.fori_loop(0, SIDE, body, 0)
            for at in range(4):
                @pl.when(block == at // 2)
                def _(at=at):
                    copy_out(at).start()
            return carry

        lax.fori_loop(0, 2, run, 0)
        for at in range(4):
            copy_out(at).wait()

    smem = pl.BlockSpec(memory_space=pltpu.SMEM)
    anywhere = pl.BlockSpec(memory_space=pl.ANY)
    return pl.pallas_call(
        kernel,
        in_specs=[smem] + [anywhere] * (3 + joined),
        out_specs=[anywhere] * 4 + [smem],
        out_shape=[HALF_MSG if coded else HALF_RAW] * 4 + [jax.ShapeDtypeStruct((4,), jnp.int32)],
        scratch_shapes=[
            pltpu.VMEM((2, SIDE, QT, width), jnp.bfloat16),
            pltpu.VMEM((2, CAP, width), jnp.bfloat16),
            pltpu.VMEM((2, CAP, CB), jnp.bfloat16),
            pltpu.VMEM((SUPER, CAP), jnp.bfloat16),
            pltpu.VMEM((2, SUPER, CB), jnp.float32),
            pltpu.VMEM((4,) + HALF_MSG.shape, jnp.int16),
            pltpu.VMEM((4,) + HALF_MSG.shape, jnp.int16),
            pltpu.SemaphoreType.DMA((2, SIDE)),
            pltpu.SemaphoreType.DMA((2, TILES)),
            pltpu.SemaphoreType.DMA((2,)),
            pltpu.SemaphoreType.DMA((4,)),
            pltpu.SemaphoreType.DMA((4,)),
        ],
        compiler_params=params(),
        cost_estimate=pl.CostEstimate(
            flops=2 * 4 * HALF * CAP * (width + CB),
            bytes_accessed=8 * HALF * width,
            transcendentals=2 * HALF * CAP,
        ),
        name="sums",
    )(facts, queries, keys, hots, *arrived)


def turn(place, low, high, low_came, high_came):
    def kernel(place_ref, low_hbm, high_hbm, low_msg, high_msg, own_hbm, plus_hbm, far_hbm, minus_hbm, *scratch):
        raw_ref, came_ref, msg_ref, own_ref, raw_sems, came_sems, out_sems = scratch

        def loads(half):
            raw, came = ((low_hbm, low_msg), (high_hbm, high_msg))[half]
            return (
                pltpu.make_async_copy(raw, raw_ref.at[half], raw_sems.at[half]),
                pltpu.make_async_copy(came, came_ref.at[half], came_sems.at[half]),
            )

        for half in range(2):
            for load in loads(half):
                load.start()
        for k in range(3):
            clear_tail(msg_ref.at[k], QT)
        for half in range(2):
            for load in loads(half):
                load.wait()

        def values(k):
            tile = lax.rem(place_ref[0] + k, SIDE)
            half, at = tile // 2, tile % 2
            return raw_ref[half, pl.ds(aligned(at * QT), QT), :] + decode(came_ref.at[half], at, HALF)

        def body(i, carry):
            k = jnp.where(i == 0, 2, jnp.where(i == 1, 1, 3))
            encode(values(k), msg_ref.at[i], 0, QT)
            return carry

        outs = [
            pltpu.make_async_copy(msg_ref.at[i], out, out_sems.at[i])
            for i, out in enumerate((far_hbm, plus_hbm, minus_hbm))
        ]
        outs.append(pltpu.make_async_copy(own_ref, own_hbm, out_sems.at[3]))
        lax.fori_loop(0, 3, body, 0)
        for out in outs[:3]:
            out.start()
        own_ref[...] = values(0)
        outs[3].start()
        for out in outs:
            out.wait()

    anywhere = pl.BlockSpec(memory_space=pl.ANY)
    return pl.pallas_call(
        kernel,
        in_specs=[pl.BlockSpec(memory_space=pltpu.SMEM)] + [anywhere] * 4,
        out_specs=[anywhere] * 4,
        out_shape=[jax.ShapeDtypeStruct((QT, CB), jnp.float32), TILE_MSG, TILE_MSG, TILE_MSG],
        scratch_shapes=[
            pltpu.VMEM((2, HALF, CB), jnp.float32),
            pltpu.VMEM((2,) + HALF_MSG.shape, jnp.int16),
            pltpu.VMEM((3,) + TILE_MSG.shape, jnp.int16),
            pltpu.VMEM((QT, CB), jnp.float32),
            pltpu.SemaphoreType.DMA((2,)),
            pltpu.SemaphoreType.DMA((2,)),
            pltpu.SemaphoreType.DMA((4,)),
        ],
        compiler_params=params(),
        cost_estimate=pl.CostEstimate(flops=40 * QT * CB, bytes_accessed=40 * QT * CB, transcendentals=0),
        name="turn",
    )(place, low, high, low_came, high_came)


def close(text, own_a, msgs_a, own_b, msgs_b):
    def kernel(text_ref, *rest):
        own, msgs = rest[0:2], (rest[2:5], rest[5:8])
        logits_ref, stats_ref = rest[8:]
        for block in range(2):
            total = own[block][...]
            for msg in msgs[block]:
                total += decode(msg, 0, QT)
            at = slice(block * CB, block * CB + CB)
            logits_ref[:, at] = text_ref[:, at] + total
        logits = logits_ref[...]
        largest = jnp.max(logits, axis=1, keepdims=True)
        total = jnp.sum(jnp.exp(logits - largest), axis=1, keepdims=True)
        eye = diagonal()
        stats_ref[0:1, :] = jnp.sum(jnp.where(eye, largest, 0.0), axis=0, keepdims=True)
        stats_ref[1:2, :] = jnp.sum(jnp.where(eye, total, 0.0), axis=0, keepdims=True)

    return pl.pallas_call(
        kernel,
        out_shape=[
            jax.ShapeDtypeStruct((QT, 2 * CB), jnp.float32),
            jax.ShapeDtypeStruct((2, QT), jnp.float32),
        ],
        compiler_params=params(),
        cost_estimate=pl.CostEstimate(flops=30 * QT * CB, bytes_accessed=40 * QT * CB, transcendentals=QT * CB),
        name="close",
    )(text, own_a, own_b, *msgs_a, *msgs_b)


def finish(logits, stats):
    def kernel(logits_ref, stats_ref, out_ref):
        largest = jnp.max(stats_ref[:, 0, :], axis=0, keepdims=True)
        total = jnp.sum(stats_ref[:, 1, :] * jnp.exp(stats_ref[:, 0, :] - largest), axis=0, keepdims=True)
        eye = diagonal()
        largest = jnp.sum(jnp.where(eye, largest, 0.0), axis=1, keepdims=True)
        shift = jnp.sum(jnp.where(eye, jnp.log(total), 0.0), axis=1, keepdims=True)
        out_ref[...] = logits_ref[...] - largest - shift

    return pl.pallas_call(
        kernel,
        out_shape=jax.ShapeDtypeStruct(logits.shape, jnp.float32),
        compiler_params=params(),
        name="finish",
    )(logits, stats)


def shifted(dx, dz):
    return [
        (x * SIDE + z, (x + dx) % SIDE * SIDE + (z + dz) % SIDE) for x in range(SIDE) for z in range(SIDE)
    ]


def send(message, dx, dz):
    return lax.ppermute(message, "cache", shifted(dx, dz))


def per_device(queries, cache_keys, labels, prototypes):
    width = queries.shape[1]
    own = lax.axis_index("cache")
    x, z = own // SIDE, own % SIDE
    low = lax.axis_index("cls") * (2 * CB)

    unit_queries = unit_small(queries)
    gathered = lax.all_gather(unit_queries, ("cache", "cls"), axis=0, tiled=True)

    order = lax.sort(labels * 16384 + lax.iota(jnp.int32, labels.shape[0]), is_stable=False)
    start = jnp.sum((labels < low).astype(jnp.int32))
    middle = jnp.sum((labels < low + CB).astype(jnp.int32))
    stop = jnp.sum((labels < low + 2 * CB).astype(jnp.int32))
    padded = jnp.concatenate([order, jnp.zeros((CAP,), jnp.int32)])
    picked = jnp.concatenate(
        [lax.dynamic_slice(padded, (start,), (CAP,)), lax.dynamic_slice(padded, (middle,), (CAP,))]
    )
    counts = jnp.stack([middle - start, stop - middle])
    place = lax.iota(jnp.int32, 2 * CAP)
    block = place // CAP
    valid = place - block * CAP < jnp.where(block == 0, counts[0], counts[1])
    local = jnp.where(valid, picked // 16384 - low - block * CB, -1)
    rows = jnp.take(cache_keys, picked % 16384, axis=0, mode="clip")
    text = text_scale * lax.dot_general(
        lax.all_gather(unit_queries, "cls", axis=0, tiled=True),
        prototypes,
        (((1,), (1,)), ((), ())),
        preferred_element_type=jnp.float32,
    )
    rows, text = lax.optimization_barrier((rows, text))
    tiles = jnp.maximum((counts + KT - 1) // KT, COMMON)
    facts = jnp.stack([x, z, tiles[0], tiles[1]]).astype(jnp.int32)
    keys, hots, facts = prepare(facts, rows, local)
    gathered, facts = lax.optimization_barrier((gathered, facts))
    q3 = gathered.reshape(SIDE * SIDE, QT, width)

    def run(facts, shifts, halves, coded, arrived=()):
        *parts, facts = sums(shifts, halves, coded, facts, q3, keys, hots, arrived)
        return parts, facts

    def send_all(parts):
        a_right, a_left, b_right, b_left = parts
        return send(a_right, 1, 0), send(a_left, -1, 0), send(b_right, 0, 1), send(b_left, 0, -1)

    far, facts = run(facts, (2, 2), (0, 1), True)
    far = send_all(far)
    free, facts = run(facts, (1, 3), (1, 0), True)
    free = send_all(free)
    full, facts = run(facts, (1, 3), (0, 1), True, far)
    full = send_all(full)
    a_low, a_high, b_low, b_high = run(
        facts, (0, 0), (0, 1), False, (free[1], free[0], free[3], free[2])
    )[0]

    own_a, a_plus, a_far, a_minus = turn(z[None], a_low, a_high, full[0], full[1])
    own_b, b_plus, b_far, b_minus = turn(x[None], b_low, b_high, full[2], full[3])
    a_msgs = send(a_far, 0, 2), send(a_plus, 0, 1), send(a_minus, 0, -1)
    b_msgs = send(b_far, 2, 0), send(b_plus, 1, 0), send(b_minus, -1, 0)

    logits, stats = close(text, own_a, a_msgs, own_b, b_msgs)
    return finish(logits, lax.all_gather(stats, "cls"))


def solution(mesh):
    placed = (P(("cache", "cls"), None), P("cache", None), P("cache"), P("cls", None))
    return jax.shard_map(
        per_device, mesh=mesh, in_specs=placed, out_specs=P("cache", "cls"), check_vma=False
    )
```

```python
import math

import jax
import jax.numpy as jnp
from jax import lax
from jax.experimental import pallas as pl
from jax.experimental.pallas import tpu as pltpu
from jax.sharding import PartitionSpec as P

text_scale = 100.0
epsilon = 1e-06
SIDE = 4
CB = 640
CAP = 1280
QT = 256
KT = 256
TAIL = 16


def params(mib=36):
    return pltpu.CompilerParams(vmem_limit_bytes=mib * 1024 * 1024)


def unit_rows(matrix):
    widened = matrix.astype(jnp.float32)
    return (widened / jnp.sqrt(jnp.sum(widened * widened, axis=1, keepdims=True) + epsilon)).astype(
        jnp.bfloat16
    )


def prepare_kernel(facts_ref, rows_ref, labels_ref, unit_ref, hot_ref, next_ref):
    for at in range(4):
        next_ref[at] = facts_ref[at]
    unit_ref[...] = unit_rows(rows_ref[...])
    classes = lax.broadcasted_iota(jnp.int32, (KT, CB), 1)
    labels = jnp.sum(jnp.where(diagonal(), labels_ref[0], 0), axis=1, keepdims=True)
    hot_ref[...] = jnp.where(labels == classes, 1.0, 0.0).astype(jnp.bfloat16)


def prepare(facts, rows, labels):
    count, width = rows.shape
    return pl.pallas_call(
        prepare_kernel,
        grid=(count // KT,),
        in_specs=[
            pl.BlockSpec(memory_space=pltpu.SMEM),
            pl.BlockSpec((KT, width), lambda i: (i, 0)),
            pl.BlockSpec((1, 1, KT), lambda i: (i, 0, 0)),
        ],
        out_specs=[
            pl.BlockSpec((KT, width), lambda i: (i, 0)),
            pl.BlockSpec((KT, CB), lambda i: (i, 0)),
            pl.BlockSpec(memory_space=pltpu.SMEM),
        ],
        out_shape=[
            jax.ShapeDtypeStruct((count, width), jnp.bfloat16),
            jax.ShapeDtypeStruct((count, CB), jnp.bfloat16),
            jax.ShapeDtypeStruct((4,), jnp.int32),
        ],
        compiler_params=params(),
        cost_estimate=pl.CostEstimate(flops=count * width * 4, bytes_accessed=count * width * 6, transcendentals=count),
        name="prepare",
    )(facts, rows, labels.reshape(count // KT, 1, KT))


def unit_kernel(rows_ref, unit_ref):
    unit_ref[...] = unit_rows(rows_ref[...])


def unit_small(rows):
    return pl.pallas_call(
        unit_kernel,
        out_shape=jax.ShapeDtypeStruct(rows.shape, jnp.bfloat16),
        compiler_params=params(),
        name="unit",
    )(rows)


def aligned(value):
    return pl.multiple_of(value, QT)


def diagonal():
    shape = (QT, QT)
    return lax.broadcasted_iota(jnp.int32, shape, 0) == lax.broadcasted_iota(jnp.int32, shape, 1)


def encode(values, message_ref, tile, tail_row):
    largest = jnp.maximum(jnp.max(values, axis=1, keepdims=True), 1e-30)
    exponent = jnp.ceil(jnp.log2(largest) - 14.99)
    codes = (values * jnp.exp2(-exponent) + 0.5).astype(jnp.int32)
    message_ref[pl.ds(aligned(tile * QT), QT), :] = codes.astype(jnp.int16)
    along = jnp.sum(jnp.where(diagonal(), exponent, 0.0), axis=0, keepdims=True)
    shape = (TAIL, QT)
    old = message_ref[tail_row : tail_row + TAIL, :QT].astype(jnp.int32)
    new = jnp.broadcast_to(along, shape).astype(jnp.int32)
    at = lax.broadcasted_iota(jnp.int32, shape, 0) == tile
    message_ref[tail_row : tail_row + TAIL, :QT] = jnp.where(at, new, old).astype(jnp.int16)


def clear_tail(message_ref, tail_row):
    message_ref[tail_row : tail_row + TAIL, :] = jnp.zeros((TAIL, CB), jnp.int16)


def decode(message_ref, tile, tail_row):
    shape = (TAIL, QT)
    tail = message_ref[tail_row : tail_row + TAIL, :QT].astype(jnp.float32)
    at = lax.broadcasted_iota(jnp.int32, shape, 0) == tile
    along = jnp.sum(jnp.where(at, tail, 0.0), axis=0, keepdims=True)
    exponent = jnp.sum(jnp.where(diagonal(), along, 0.0), axis=1, keepdims=True)
    codes = message_ref[pl.ds(aligned(tile * QT), QT), :].astype(jnp.float32)
    return codes * jnp.exp2(exponent)


HALF = 2 * QT
HALF_MSG = jax.ShapeDtypeStruct((HALF + TAIL, CB), jnp.int16)
TILE_MSG = jax.ShapeDtypeStruct((QT + TAIL, CB), jnp.int16)
HALF_RAW = jax.ShapeDtypeStruct((HALF, CB), jnp.float32)


SUPER = SIDE * QT
COMMON = 3


def super_sums(tiles, q_ref, keys_ref, hot_ref, scores_ref, total_ref):
    width = q_ref.shape[-1]
    sharpness = float(width) ** 0.5 * math.log2(math.e)
    queries = q_ref[...].reshape(SUPER, width)

    def step(t, carry):
        at = pl.ds(aligned(t * KT), KT)
        cosine = lax.dot_general(
            queries, keys_ref[at, :], (((1,), (1,)), ((), ())), preferred_element_type=jnp.float32
        )
        scores_ref[:, at] = jnp.exp2(sharpness * cosine).astype(jnp.bfloat16)
        return carry

    lax.fori_loop(0, tiles, step, 0)
    cut = COMMON * KT
    total_ref[...] = jnp.dot(
        scores_ref[:, :cut], hot_ref[:cut, :], preferred_element_type=jnp.float32
    )

    @pl.when(tiles > COMMON)
    def _():
        total_ref[...] += jnp.dot(
            scores_ref[:, cut:], hot_ref[cut:, :], preferred_element_type=jnp.float32
        )


def sums(shifts, halves, coded, facts, queries, keys, hots, arrived=()):
    width = keys.shape[1]
    joined = len(arrived)

    def kernel(facts_ref, q_hbm, keys_ref, hot_ref, *rest):
        came, outs, next_ref = rest[:joined], rest[joined : joined + 4], rest[joined + 4]
        scratch = rest[joined + 5 :]
        q_ref, scores_ref, total_ref, came_ref, msg_ref, q_sems, came_sems, out_sems = scratch
        for at in range(4):
            next_ref[at] = facts_ref[at]

        def copy_queries(block, part):
            away = shifts[part // 2]
            inner = halves[part // 2] * 2 + part % 2
            outer = lax.rem(facts_ref[block] + away, SIDE)
            chunk = jnp.where(block == 0, outer * SIDE + inner, inner * SIDE + outer)
            return pltpu.make_async_copy(q_hbm.at[chunk], q_ref.at[block, part], q_sems.at[block, part])

        def copy_came(at):
            return pltpu.make_async_copy(came[at], came_ref.at[at], came_sems.at[at])

        def copy_out(at):
            source = msg_ref.at[at] if coded else total_ref.at[at // 2, pl.ds(at % 2 * HALF, HALF), :]
            return pltpu.make_async_copy(source, outs[at], out_sems.at[at])

        for block in range(2):
            for part in range(SIDE):
                copy_queries(block, part).start()
        for at in range(joined):
            copy_came(at).start()
        scores_ref[:, COMMON * KT :] = jnp.zeros((SUPER, CAP - COMMON * KT), jnp.bfloat16)
        if coded:
            for at in range(4):
                clear_tail(msg_ref.at[at], HALF)

        def run(block, carry):
            for part in range(SIDE):
                copy_queries(block, part).wait()
            super_sums(
                facts_ref[2 + block],
                q_ref.at[block],
                keys_ref.at[pl.ds(aligned(block * CAP), CAP), :],
                hot_ref.at[pl.ds(aligned(block * CAP), CAP), :],
                scores_ref,
                total_ref.at[block],
            )
            if joined:
                @pl.when(block == 0)
                def _():
                    for at in range(joined):
                        copy_came(at).wait()

            if joined or coded:
                def body(t, carry):
                    rows = pl.ds(aligned(t * QT), QT)
                    at = 2 * block + t // 2
                    values = total_ref[block, rows, :]
                    if joined:
                        values += decode(came_ref.at[at], t % 2, HALF)
                    if coded:
                        encode(values, msg_ref.at[at], t % 2, HALF)
                    else:
                        total_ref[block, rows, :] = values
                    return carry

                lax.fori_loop(0, SIDE, body, 0)
            for at in range(4):
                @pl.when(block == at // 2)
                def _(at=at):
                    copy_out(at).start()
            return carry

        lax.fori_loop(0, 2, run, 0)
        for at in range(4):
            copy_out(at).wait()

    vmem, smem = pl.BlockSpec(memory_space=pltpu.VMEM), pl.BlockSpec(memory_space=pltpu.SMEM)
    anywhere = pl.BlockSpec(memory_space=pl.ANY)
    return pl.pallas_call(
        kernel,
        in_specs=[smem, anywhere, vmem, vmem] + [anywhere] * joined,
        out_specs=[anywhere] * 4 + [smem],
        out_shape=[HALF_MSG if coded else HALF_RAW] * 4 + [jax.ShapeDtypeStruct((4,), jnp.int32)],
        scratch_shapes=[
            pltpu.VMEM((2, SIDE, QT, width), jnp.bfloat16),
            pltpu.VMEM((SUPER, CAP), jnp.bfloat16),
            pltpu.VMEM((2, SUPER, CB), jnp.float32),
            pltpu.VMEM((4,) + HALF_MSG.shape, jnp.int16),
            pltpu.VMEM((4,) + HALF_MSG.shape, jnp.int16),
            pltpu.SemaphoreType.DMA((2, SIDE)),
            pltpu.SemaphoreType.DMA((4,)),
            pltpu.SemaphoreType.DMA((4,)),
        ],
        compiler_params=params(),
        cost_estimate=pl.CostEstimate(
            flops=2 * 4 * HALF * CAP * (width + CB),
            bytes_accessed=8 * HALF * width,
            transcendentals=2 * HALF * CAP,
        ),
        name="sums",
    )(facts, queries, keys, hots, *arrived)


def turn(place, low, high, low_came, high_came):
    def kernel(place_ref, low_hbm, high_hbm, low_msg, high_msg, own_hbm, plus_hbm, far_hbm, minus_hbm, *scratch):
        raw_ref, came_ref, msg_ref, own_ref, raw_sems, came_sems, out_sems = scratch

        def loads(half):
            raw, came = ((low_hbm, low_msg), (high_hbm, high_msg))[half]
            return (
                pltpu.make_async_copy(raw, raw_ref.at[half], raw_sems.at[half]),
                pltpu.make_async_copy(came, came_ref.at[half], came_sems.at[half]),
            )

        for half in range(2):
            for load in loads(half):
                load.start()
        for k in range(3):
            clear_tail(msg_ref.at[k], QT)
        for half in range(2):
            for load in loads(half):
                load.wait()

        def values(k):
            tile = lax.rem(place_ref[0] + k, SIDE)
            half, at = tile // 2, tile % 2
            return raw_ref[half, pl.ds(aligned(at * QT), QT), :] + decode(came_ref.at[half], at, HALF)

        def body(i, carry):
            k = jnp.where(i == 0, 2, jnp.where(i == 1, 1, 3))
            encode(values(k), msg_ref.at[i], 0, QT)
            return carry

        outs = [
            pltpu.make_async_copy(msg_ref.at[i], out, out_sems.at[i])
            for i, out in enumerate((far_hbm, plus_hbm, minus_hbm))
        ]
        outs.append(pltpu.make_async_copy(own_ref, own_hbm, out_sems.at[3]))
        lax.fori_loop(0, 3, body, 0)
        for out in outs[:3]:
            out.start()
        own_ref[...] = values(0)
        outs[3].start()
        for out in outs:
            out.wait()

    anywhere = pl.BlockSpec(memory_space=pl.ANY)
    return pl.pallas_call(
        kernel,
        in_specs=[pl.BlockSpec(memory_space=pltpu.SMEM)] + [anywhere] * 4,
        out_specs=[anywhere] * 4,
        out_shape=[jax.ShapeDtypeStruct((QT, CB), jnp.float32), TILE_MSG, TILE_MSG, TILE_MSG],
        scratch_shapes=[
            pltpu.VMEM((2, HALF, CB), jnp.float32),
            pltpu.VMEM((2,) + HALF_MSG.shape, jnp.int16),
            pltpu.VMEM((3,) + TILE_MSG.shape, jnp.int16),
            pltpu.VMEM((QT, CB), jnp.float32),
            pltpu.SemaphoreType.DMA((2,)),
            pltpu.SemaphoreType.DMA((2,)),
            pltpu.SemaphoreType.DMA((4,)),
        ],
        compiler_params=params(),
        cost_estimate=pl.CostEstimate(flops=40 * QT * CB, bytes_accessed=40 * QT * CB, transcendentals=0),
        name="turn",
    )(place, low, high, low_came, high_came)


def close(text, own_a, msgs_a, own_b, msgs_b):
    def kernel(text_ref, *rest):
        own, msgs = rest[0:2], (rest[2:5], rest[5:8])
        logits_ref, stats_ref = rest[8:]
        for block in range(2):
            total = own[block][...]
            for msg in msgs[block]:
                total += decode(msg, 0, QT)
            at = slice(block * CB, block * CB + CB)
            logits_ref[:, at] = text_ref[:, at] + total
        logits = logits_ref[...]
        largest = jnp.max(logits, axis=1, keepdims=True)
        total = jnp.sum(jnp.exp(logits - largest), axis=1, keepdims=True)
        eye = diagonal()
        stats_ref[0:1, :] = jnp.sum(jnp.where(eye, largest, 0.0), axis=0, keepdims=True)
        stats_ref[1:2, :] = jnp.sum(jnp.where(eye, total, 0.0), axis=0, keepdims=True)

    return pl.pallas_call(
        kernel,
        out_shape=[
            jax.ShapeDtypeStruct((QT, 2 * CB), jnp.float32),
            jax.ShapeDtypeStruct((2, QT), jnp.float32),
        ],
        compiler_params=params(),
        cost_estimate=pl.CostEstimate(flops=30 * QT * CB, bytes_accessed=40 * QT * CB, transcendentals=QT * CB),
        name="close",
    )(text, own_a, own_b, *msgs_a, *msgs_b)


def finish(logits, stats):
    def kernel(logits_ref, stats_ref, out_ref):
        largest = jnp.max(stats_ref[:, 0, :], axis=0, keepdims=True)
        total = jnp.sum(stats_ref[:, 1, :] * jnp.exp(stats_ref[:, 0, :] - largest), axis=0, keepdims=True)
        eye = diagonal()
        largest = jnp.sum(jnp.where(eye, largest, 0.0), axis=1, keepdims=True)
        shift = jnp.sum(jnp.where(eye, jnp.log(total), 0.0), axis=1, keepdims=True)
        out_ref[...] = logits_ref[...] - largest - shift

    return pl.pallas_call(
        kernel,
        out_shape=jax.ShapeDtypeStruct(logits.shape, jnp.float32),
        compiler_params=params(),
        name="finish",
    )(logits, stats)


def shifted(dx, dz):
    return [
        (x * SIDE + z, (x + dx) % SIDE * SIDE + (z + dz) % SIDE) for x in range(SIDE) for z in range(SIDE)
    ]


def send(message, dx, dz):
    return lax.ppermute(message, "cache", shifted(dx, dz))


def per_device(queries, cache_keys, labels, prototypes):
    width = queries.shape[1]
    own = lax.axis_index("cache")
    x, z = own // SIDE, own % SIDE
    low = lax.axis_index("cls") * (2 * CB)

    unit_queries = unit_small(queries)
    gathered = lax.all_gather(unit_queries, ("cache", "cls"), axis=0, tiled=True)

    order = lax.sort(labels * 16384 + lax.iota(jnp.int32, labels.shape[0]), is_stable=False)
    start = jnp.sum((labels < low).astype(jnp.int32))
    middle = jnp.sum((labels < low + CB).astype(jnp.int32))
    stop = jnp.sum((labels < low + 2 * CB).astype(jnp.int32))
    padded = jnp.concatenate([order, jnp.zeros((CAP,), jnp.int32)])
    picked = jnp.concatenate(
        [lax.dynamic_slice(padded, (start,), (CAP,)), lax.dynamic_slice(padded, (middle,), (CAP,))]
    )
    counts = jnp.stack([middle - start, stop - middle])
    place = lax.iota(jnp.int32, 2 * CAP)
    block = place // CAP
    valid = place - block * CAP < jnp.where(block == 0, counts[0], counts[1])
    local = jnp.where(valid, picked // 16384 - low - block * CB, -1)
    rows = jnp.take(cache_keys, picked % 16384, axis=0, mode="clip")
    text = text_scale * lax.dot_general(
        lax.all_gather(unit_queries, "cls", axis=0, tiled=True),
        prototypes,
        (((1,), (1,)), ((), ())),
        preferred_element_type=jnp.float32,
    )
    rows, text = lax.optimization_barrier((rows, text))
    tiles = jnp.maximum((counts + KT - 1) // KT, COMMON)
    facts = jnp.stack([x, z, tiles[0], tiles[1]]).astype(jnp.int32)
    keys, hots, facts = prepare(facts, rows, local)
    gathered, facts = lax.optimization_barrier((gathered, facts))
    q3 = gathered.reshape(SIDE * SIDE, QT, width)

    def run(facts, shifts, halves, coded, arrived=()):
        *parts, facts = sums(shifts, halves, coded, facts, q3, keys, hots, arrived)
        return parts, facts

    def send_all(parts):
        a_right, a_left, b_right, b_left = parts
        return send(a_right, 1, 0), send(a_left, -1, 0), send(b_right, 0, 1), send(b_left, 0, -1)

    far, facts = run(facts, (2, 2), (0, 1), True)
    far = send_all(far)
    free, facts = run(facts, (1, 3), (1, 0), True)
    free = send_all(free)
    full, facts = run(facts, (1, 3), (0, 1), True, far)
    full = send_all(full)
    a_low, a_high, b_low, b_high = run(
        facts, (0, 0), (0, 1), False, (free[1], free[0], free[3], free[2])
    )[0]

    own_a, a_plus, a_far, a_minus = turn(z[None], a_low, a_high, full[0], full[1])
    own_b, b_plus, b_far, b_minus = turn(x[None], b_low, b_high, full[2], full[3])
    a_msgs = send(a_far, 0, 2), send(a_plus, 0, 1), send(a_minus, 0, -1)
    b_msgs = send(b_far, 2, 0), send(b_plus, 1, 0), send(b_minus, -1, 0)

    logits, stats = close(text, own_a, a_msgs, own_b, b_msgs)
    return finish(logits, lax.all_gather(stats, "cls"))


def solution(mesh):
    placed = (P(("cache", "cls"), None), P("cache", None), P("cache"), P("cls", None))
    return jax.shard_map(
        per_device, mesh=mesh, in_specs=placed, out_specs=P("cache", "cls"), check_vma=False
    )
```

```python
import math

import jax
import jax.numpy as jnp
from jax import lax
from jax.experimental import pallas as pl
from jax.experimental.pallas import tpu as pltpu
from jax.sharding import PartitionSpec as P

text_scale = 100.0
epsilon = 1e-06
SIDE = 4
CB = 640
CAP = 1280
QT = 256
KT = 256
TAIL = 16


def params(mib=36):
    return pltpu.CompilerParams(vmem_limit_bytes=mib * 1024 * 1024)


def unit_rows(matrix):
    widened = matrix.astype(jnp.float32)
    return (widened / jnp.sqrt(jnp.sum(widened * widened, axis=1, keepdims=True) + epsilon)).astype(
        jnp.bfloat16
    )


def prepare_kernel(facts_ref, rows_ref, labels_ref, unit_ref, hot_ref, next_ref):
    for at in range(4):
        next_ref[at] = facts_ref[at]
    unit_ref[...] = unit_rows(rows_ref[...])
    classes = lax.broadcasted_iota(jnp.int32, (KT, CB), 1)
    labels = jnp.sum(jnp.where(diagonal(), labels_ref[0], 0), axis=1, keepdims=True)
    hot_ref[...] = jnp.where(labels == classes, 1.0, 0.0).astype(jnp.bfloat16)


def prepare(facts, rows, labels):
    count, width = rows.shape
    return pl.pallas_call(
        prepare_kernel,
        grid=(count // KT,),
        in_specs=[
            pl.BlockSpec(memory_space=pltpu.SMEM),
            pl.BlockSpec((KT, width), lambda i: (i, 0)),
            pl.BlockSpec((1, 1, KT), lambda i: (i, 0, 0)),
        ],
        out_specs=[
            pl.BlockSpec((KT, width), lambda i: (i, 0)),
            pl.BlockSpec((KT, CB), lambda i: (i, 0)),
            pl.BlockSpec(memory_space=pltpu.SMEM),
        ],
        out_shape=[
            jax.ShapeDtypeStruct((count, width), jnp.bfloat16),
            jax.ShapeDtypeStruct((count, CB), jnp.bfloat16),
            jax.ShapeDtypeStruct((4,), jnp.int32),
        ],
        compiler_params=params(),
        cost_estimate=pl.CostEstimate(flops=count * width * 4, bytes_accessed=count * width * 6, transcendentals=count),
        name="prepare",
    )(facts, rows, labels.reshape(count // KT, 1, KT))


def unit_kernel(rows_ref, unit_ref):
    unit_ref[...] = unit_rows(rows_ref[...])


def unit_small(rows):
    return pl.pallas_call(
        unit_kernel,
        out_shape=jax.ShapeDtypeStruct(rows.shape, jnp.bfloat16),
        compiler_params=params(),
        name="unit",
    )(rows)


def aligned(value):
    return pl.multiple_of(value, QT)


def diagonal():
    shape = (QT, QT)
    return lax.broadcasted_iota(jnp.int32, shape, 0) == lax.broadcasted_iota(jnp.int32, shape, 1)


def encode(values, message_ref, tile, tail_row):
    largest = jnp.maximum(jnp.max(values, axis=1, keepdims=True), 1e-30)
    exponent = jnp.ceil(jnp.log2(largest) - 14.99)
    codes = (values * jnp.exp2(-exponent) + 0.5).astype(jnp.int32)
    message_ref[pl.ds(aligned(tile * QT), QT), :] = codes.astype(jnp.int16)
    along = jnp.sum(jnp.where(diagonal(), exponent, 0.0), axis=0, keepdims=True)
    shape = (TAIL, QT)
    old = message_ref[tail_row : tail_row + TAIL, :QT].astype(jnp.int32)
    new = jnp.broadcast_to(along, shape).astype(jnp.int32)
    at = lax.broadcasted_iota(jnp.int32, shape, 0) == tile
    message_ref[tail_row : tail_row + TAIL, :QT] = jnp.where(at, new, old).astype(jnp.int16)


def clear_tail(message_ref, tail_row):
    message_ref[tail_row : tail_row + TAIL, :] = jnp.zeros((TAIL, CB), jnp.int16)


def decode(message_ref, tile, tail_row):
    shape = (TAIL, QT)
    tail = message_ref[tail_row : tail_row + TAIL, :QT].astype(jnp.float32)
    at = lax.broadcasted_iota(jnp.int32, shape, 0) == tile
    along = jnp.sum(jnp.where(at, tail, 0.0), axis=0, keepdims=True)
    exponent = jnp.sum(jnp.where(diagonal(), along, 0.0), axis=1, keepdims=True)
    codes = message_ref[pl.ds(aligned(tile * QT), QT), :].astype(jnp.float32)
    return codes * jnp.exp2(exponent)


HALF = 2 * QT
HALF_MSG = jax.ShapeDtypeStruct((HALF + TAIL, CB), jnp.int16)
TILE_MSG = jax.ShapeDtypeStruct((QT + TAIL, CB), jnp.int16)
HALF_RAW = jax.ShapeDtypeStruct((HALF, CB), jnp.float32)


SUPER = SIDE * QT
COMMON = 3


def super_sums(tiles, q_ref, keys_ref, hot_ref, scores_ref, total_ref):
    width = q_ref.shape[-1]
    sharpness = float(width) ** 0.5 * math.log2(math.e)
    queries = q_ref[...].reshape(SUPER, width)

    def scores(rows, at):
        cosine = lax.dot_general(
            rows, keys_ref[at, :], (((1,), (1,)), ((), ())), preferred_element_type=jnp.float32
        )
        return jnp.exp2(sharpness * cosine).astype(jnp.bfloat16)

    cut = COMMON * KT
    for t in range(COMMON):
        at = pl.ds(t * KT, KT)
        scores_ref[:, at] = scores(queries, at)
    total_ref[...] = jnp.dot(scores_ref[...], hot_ref[:cut, :], preferred_element_type=jnp.float32)

    def rest(i, carry):
        half = lax.rem(i, 2)
        at = pl.ds(aligned((COMMON + lax.div(i, 2)) * KT), KT)
        rows = pl.ds(aligned(half * HALF), HALF)
        part = q_ref[pl.ds(half * 2, 2)].reshape(HALF, width)
        total_ref[rows, :] += jnp.dot(
            scores(part, at), hot_ref[at, :], preferred_element_type=jnp.float32
        )
        return carry

    lax.fori_loop(0, 2 * (tiles - COMMON), rest, 0)


def sums(shifts, halves, coded, facts, queries, keys, hots, arrived=()):
    width = keys.shape[1]
    joined = len(arrived)

    def kernel(facts_ref, q_hbm, keys_ref, hot_ref, *rest):
        came, outs, next_ref = rest[:joined], rest[joined : joined + 4], rest[joined + 4]
        scratch = rest[joined + 5 :]
        q_ref, scores_ref, total_ref, came_ref, msg_ref, q_sems, came_sems, out_sems = scratch
        for at in range(4):
            next_ref[at] = facts_ref[at]

        def copy_queries(block, part):
            away = shifts[part // 2]
            inner = halves[part // 2] * 2 + part % 2
            outer = lax.rem(facts_ref[block] + away, SIDE)
            chunk = jnp.where(block == 0, outer * SIDE + inner, inner * SIDE + outer)
            return pltpu.make_async_copy(q_hbm.at[chunk], q_ref.at[block, part], q_sems.at[block, part])

        def copy_came(at):
            return pltpu.make_async_copy(came[at], came_ref.at[at], came_sems.at[at])

        def copy_out(at):
            source = msg_ref.at[at] if coded else total_ref.at[at // 2, pl.ds(at % 2 * HALF, HALF), :]
            return pltpu.make_async_copy(source, outs[at], out_sems.at[at])

        for block in range(2):
            for part in range(SIDE):
                copy_queries(block, part).start()
        for at in range(joined):
            copy_came(at).start()
        if coded:
            for at in range(4):
                clear_tail(msg_ref.at[at], HALF)

        def run(block, carry):
            for part in range(SIDE):
                copy_queries(block, part).wait()
            super_sums(
                facts_ref[2 + block],
                q_ref.at[block],
                keys_ref.at[pl.ds(aligned(block * CAP), CAP), :],
                hot_ref.at[pl.ds(aligned(block * CAP), CAP), :],
                scores_ref,
                total_ref.at[block],
            )
            if joined:
                @pl.when(block == 0)
                def _():
                    for at in range(joined):
                        copy_came(at).wait()

            if joined or coded:
                def body(t, carry):
                    rows = pl.ds(aligned(t * QT), QT)
                    at = 2 * block + t // 2
                    values = total_ref[block, rows, :]
                    if joined:
                        values += decode(came_ref.at[at], t % 2, HALF)
                    if coded:
                        encode(values, msg_ref.at[at], t % 2, HALF)
                    else:
                        total_ref[block, rows, :] = values
                    return carry

                lax.fori_loop(0, SIDE, body, 0)
            for at in range(4):
                @pl.when(block == at // 2)
                def _(at=at):
                    copy_out(at).start()
            return carry

        lax.fori_loop(0, 2, run, 0)
        for at in range(4):
            copy_out(at).wait()

    vmem, smem = pl.BlockSpec(memory_space=pltpu.VMEM), pl.BlockSpec(memory_space=pltpu.SMEM)
    anywhere = pl.BlockSpec(memory_space=pl.ANY)
    return pl.pallas_call(
        kernel,
        in_specs=[smem, anywhere, vmem, vmem] + [anywhere] * joined,
        out_specs=[anywhere] * 4 + [smem],
        out_shape=[HALF_MSG if coded else HALF_RAW] * 4 + [jax.ShapeDtypeStruct((4,), jnp.int32)],
        scratch_shapes=[
            pltpu.VMEM((2, SIDE, QT, width), jnp.bfloat16),
            pltpu.VMEM((SUPER, COMMON * KT), jnp.bfloat16),
            pltpu.VMEM((2, SUPER, CB), jnp.float32),
            pltpu.VMEM((4,) + HALF_MSG.shape, jnp.int16),
            pltpu.VMEM((4,) + HALF_MSG.shape, jnp.int16),
            pltpu.SemaphoreType.DMA((2, SIDE)),
            pltpu.SemaphoreType.DMA((4,)),
            pltpu.SemaphoreType.DMA((4,)),
        ],
        compiler_params=params(),
        cost_estimate=pl.CostEstimate(
            flops=2 * 4 * HALF * CAP * (width + CB),
            bytes_accessed=8 * HALF * width,
            transcendentals=2 * HALF * CAP,
        ),
        name="sums",
    )(facts, queries, keys, hots, *arrived)


def turn(place, low, high, low_came, high_came):
    def kernel(place_ref, low_hbm, high_hbm, low_msg, high_msg, own_hbm, plus_hbm, far_hbm, minus_hbm, *scratch):
        raw_ref, came_ref, msg_ref, own_ref, raw_sems, came_sems, out_sems = scratch

        def loads(half):
            raw, came = ((low_hbm, low_msg), (high_hbm, high_msg))[half]
            return (
                pltpu.make_async_copy(raw, raw_ref.at[half], raw_sems.at[half]),
                pltpu.make_async_copy(came, came_ref.at[half], came_sems.at[half]),
            )

        for half in range(2):
            for load in loads(half):
                load.start()
        for k in range(3):
            clear_tail(msg_ref.at[k], QT)
        for half in range(2):
            for load in loads(half):
                load.wait()

        def values(k):
            tile = lax.rem(place_ref[0] + k, SIDE)
            half, at = tile // 2, tile % 2
            return raw_ref[half, pl.ds(aligned(at * QT), QT), :] + decode(came_ref.at[half], at, HALF)

        def body(i, carry):
            k = jnp.where(i == 0, 2, jnp.where(i == 1, 1, 3))
            encode(values(k), msg_ref.at[i], 0, QT)
            return carry

        outs = [
            pltpu.make_async_copy(msg_ref.at[i], out, out_sems.at[i])
            for i, out in enumerate((far_hbm, plus_hbm, minus_hbm))
        ]
        outs.append(pltpu.make_async_copy(own_ref, own_hbm, out_sems.at[3]))
        lax.fori_loop(0, 3, body, 0)
        for out in outs[:3]:
            out.start()
        own_ref[...] = values(0)
        outs[3].start()
        for out in outs:
            out.wait()

    anywhere = pl.BlockSpec(memory_space=pl.ANY)
    return pl.pallas_call(
        kernel,
        in_specs=[pl.BlockSpec(memory_space=pltpu.SMEM)] + [anywhere] * 4,
        out_specs=[anywhere] * 4,
        out_shape=[jax.ShapeDtypeStruct((QT, CB), jnp.float32), TILE_MSG, TILE_MSG, TILE_MSG],
        scratch_shapes=[
            pltpu.VMEM((2, HALF, CB), jnp.float32),
            pltpu.VMEM((2,) + HALF_MSG.shape, jnp.int16),
            pltpu.VMEM((3,) + TILE_MSG.shape, jnp.int16),
            pltpu.VMEM((QT, CB), jnp.float32),
            pltpu.SemaphoreType.DMA((2,)),
            pltpu.SemaphoreType.DMA((2,)),
            pltpu.SemaphoreType.DMA((4,)),
        ],
        compiler_params=params(),
        cost_estimate=pl.CostEstimate(flops=40 * QT * CB, bytes_accessed=40 * QT * CB, transcendentals=0),
        name="turn",
    )(place, low, high, low_came, high_came)


def close(text, own_a, msgs_a, own_b, msgs_b):
    def kernel(text_ref, *rest):
        own, msgs = rest[0:2], (rest[2:5], rest[5:8])
        logits_ref, stats_ref = rest[8:]
        for block in range(2):
            total = own[block][...]
            for msg in msgs[block]:
                total += decode(msg, 0, QT)
            at = slice(block * CB, block * CB + CB)
            logits_ref[:, at] = text_ref[:, at] + total
        logits = logits_ref[...]
        largest = jnp.max(logits, axis=1, keepdims=True)
        total = jnp.sum(jnp.exp(logits - largest), axis=1, keepdims=True)
        eye = diagonal()
        stats_ref[0:1, :] = jnp.sum(jnp.where(eye, largest, 0.0), axis=0, keepdims=True)
        stats_ref[1:2, :] = jnp.sum(jnp.where(eye, total, 0.0), axis=0, keepdims=True)

    return pl.pallas_call(
        kernel,
        out_shape=[
            jax.ShapeDtypeStruct((QT, 2 * CB), jnp.float32),
            jax.ShapeDtypeStruct((2, QT), jnp.float32),
        ],
        compiler_params=params(),
        cost_estimate=pl.CostEstimate(flops=30 * QT * CB, bytes_accessed=40 * QT * CB, transcendentals=QT * CB),
        name="close",
    )(text, own_a, own_b, *msgs_a, *msgs_b)


def finish(logits, stats):
    def kernel(logits_ref, stats_ref, out_ref):
        largest = jnp.max(stats_ref[:, 0, :], axis=0, keepdims=True)
        total = jnp.sum(stats_ref[:, 1, :] * jnp.exp(stats_ref[:, 0, :] - largest), axis=0, keepdims=True)
        eye = diagonal()
        largest = jnp.sum(jnp.where(eye, largest, 0.0), axis=1, keepdims=True)
        shift = jnp.sum(jnp.where(eye, jnp.log(total), 0.0), axis=1, keepdims=True)
        out_ref[...] = logits_ref[...] - largest - shift

    return pl.pallas_call(
        kernel,
        out_shape=jax.ShapeDtypeStruct(logits.shape, jnp.float32),
        compiler_params=params(),
        name="finish",
    )(logits, stats)


def shifted(dx, dz):
    return [
        (x * SIDE + z, (x + dx) % SIDE * SIDE + (z + dz) % SIDE) for x in range(SIDE) for z in range(SIDE)
    ]


def send(message, dx, dz):
    return lax.ppermute(message, "cache", shifted(dx, dz))


def per_device(queries, cache_keys, labels, prototypes):
    width = queries.shape[1]
    own = lax.axis_index("cache")
    x, z = own // SIDE, own % SIDE
    low = lax.axis_index("cls") * (2 * CB)

    unit_queries = unit_small(queries)
    gathered = lax.all_gather(unit_queries, ("cache", "cls"), axis=0, tiled=True)

    order = lax.sort(labels * 16384 + lax.iota(jnp.int32, labels.shape[0]), is_stable=False)
    start = jnp.sum((labels < low).astype(jnp.int32))
    middle = jnp.sum((labels < low + CB).astype(jnp.int32))
    stop = jnp.sum((labels < low + 2 * CB).astype(jnp.int32))
    padded = jnp.concatenate([order, jnp.zeros((CAP,), jnp.int32)])
    picked = jnp.concatenate(
        [lax.dynamic_slice(padded, (start,), (CAP,)), lax.dynamic_slice(padded, (middle,), (CAP,))]
    )
    counts = jnp.stack([middle - start, stop - middle])
    place = lax.iota(jnp.int32, 2 * CAP)
    block = place // CAP
    valid = place - block * CAP < jnp.where(block == 0, counts[0], counts[1])
    local = jnp.where(valid, picked // 16384 - low - block * CB, -1)
    rows = jnp.take(cache_keys, picked % 16384, axis=0, mode="clip")
    text = text_scale * lax.dot_general(
        lax.all_gather(unit_queries, "cls", axis=0, tiled=True),
        prototypes,
        (((1,), (1,)), ((), ())),
        preferred_element_type=jnp.float32,
    )
    rows, text = lax.optimization_barrier((rows, text))
    tiles = jnp.maximum((counts + KT - 1) // KT, COMMON)
    facts = jnp.stack([x, z, tiles[0], tiles[1]]).astype(jnp.int32)
    keys, hots, facts = prepare(facts, rows, local)
    gathered, facts = lax.optimization_barrier((gathered, facts))
    q3 = gathered.reshape(SIDE * SIDE, QT, width)

    def run(facts, shifts, halves, coded, arrived=()):
        *parts, facts = sums(shifts, halves, coded, facts, q3, keys, hots, arrived)
        return parts, facts

    def send_all(parts):
        a_right, a_left, b_right, b_left = parts
        return send(a_right, 1, 0), send(a_left, -1, 0), send(b_right, 0, 1), send(b_left, 0, -1)

    far, facts = run(facts, (2, 2), (0, 1), True)
    far = send_all(far)
    free, facts = run(facts, (1, 3), (1, 0), True)
    free = send_all(free)
    full, facts = run(facts, (1, 3), (0, 1), True, far)
    full = send_all(full)
    a_low, a_high, b_low, b_high = run(
        facts, (0, 0), (0, 1), False, (free[1], free[0], free[3], free[2])
    )[0]

    own_a, a_plus, a_far, a_minus = turn(z[None], a_low, a_high, full[0], full[1])
    own_b, b_plus, b_far, b_minus = turn(x[None], b_low, b_high, full[2], full[3])
    a_msgs = send(a_far, 0, 2), send(a_plus, 0, 1), send(a_minus, 0, -1)
    b_msgs = send(b_far, 2, 0), send(b_plus, 1, 0), send(b_minus, -1, 0)

    logits, stats = close(text, own_a, a_msgs, own_b, b_msgs)
    return finish(logits, lax.all_gather(stats, "cls"))


def solution(mesh):
    placed = (P(("cache", "cls"), None), P("cache", None), P("cache"), P("cls", None))
    return jax.shard_map(
        per_device, mesh=mesh, in_specs=placed, out_specs=P("cache", "cls"), check_vma=False
    )
```

```python
import math

import jax
import jax.numpy as jnp
from jax import lax
from jax.experimental import pallas as pl
from jax.experimental.pallas import tpu as pltpu
from jax.sharding import PartitionSpec as P

text_scale = 100.0
epsilon = 1e-06
SIDE = 4
CB = 640
CAP = 1280
QT = 256
KT = 256
TAIL = 16


def params(mib=36):
    return pltpu.CompilerParams(vmem_limit_bytes=mib * 1024 * 1024)


def unit_rows(matrix):
    widened = matrix.astype(jnp.float32)
    return (widened / jnp.sqrt(jnp.sum(widened * widened, axis=1, keepdims=True) + epsilon)).astype(
        jnp.bfloat16
    )


def prepare_kernel(facts_ref, rows_ref, labels_ref, unit_ref, hot_ref, next_ref):
    for at in range(4):
        next_ref[at] = facts_ref[at]
    unit_ref[...] = unit_rows(rows_ref[...])
    classes = lax.broadcasted_iota(jnp.int32, (KT, CB), 1)
    labels = jnp.sum(jnp.where(diagonal(), labels_ref[0], 0), axis=1, keepdims=True)
    hot_ref[...] = jnp.where(labels == classes, 1.0, 0.0).astype(jnp.bfloat16)


def prepare(facts, rows, labels):
    count, width = rows.shape
    return pl.pallas_call(
        prepare_kernel,
        grid=(count // KT,),
        in_specs=[
            pl.BlockSpec(memory_space=pltpu.SMEM),
            pl.BlockSpec((KT, width), lambda i: (i, 0)),
            pl.BlockSpec((1, 1, KT), lambda i: (i, 0, 0)),
        ],
        out_specs=[
            pl.BlockSpec((KT, width), lambda i: (i, 0)),
            pl.BlockSpec((KT, CB), lambda i: (i, 0)),
            pl.BlockSpec(memory_space=pltpu.SMEM),
        ],
        out_shape=[
            jax.ShapeDtypeStruct((count, width), jnp.bfloat16),
            jax.ShapeDtypeStruct((count, CB), jnp.bfloat16),
            jax.ShapeDtypeStruct((4,), jnp.int32),
        ],
        compiler_params=params(),
        cost_estimate=pl.CostEstimate(flops=count * width * 4, bytes_accessed=count * width * 6, transcendentals=count),
        name="prepare",
    )(facts, rows, labels.reshape(count // KT, 1, KT))


def unit_kernel(rows_ref, unit_ref):
    unit_ref[...] = unit_rows(rows_ref[...])


def unit_small(rows):
    return pl.pallas_call(
        unit_kernel,
        out_shape=jax.ShapeDtypeStruct(rows.shape, jnp.bfloat16),
        compiler_params=params(),
        name="unit",
    )(rows)


def aligned(value):
    return pl.multiple_of(value, QT)


def diagonal():
    shape = (QT, QT)
    return lax.broadcasted_iota(jnp.int32, shape, 0) == lax.broadcasted_iota(jnp.int32, shape, 1)


def encode(values, message_ref, tile, tail_row):
    largest = jnp.maximum(jnp.max(values, axis=1, keepdims=True), 1e-30)
    exponent = jnp.ceil(jnp.log2(largest) - 14.99)
    codes = (values * jnp.exp2(-exponent) + 0.5).astype(jnp.int32)
    message_ref[pl.ds(aligned(tile * QT), QT), :] = codes.astype(jnp.int16)
    along = jnp.sum(jnp.where(diagonal(), exponent, 0.0), axis=0, keepdims=True)
    shape = (TAIL, QT)
    old = message_ref[tail_row : tail_row + TAIL, :QT].astype(jnp.int32)
    new = jnp.broadcast_to(along, shape).astype(jnp.int32)
    at = lax.broadcasted_iota(jnp.int32, shape, 0) == tile
    message_ref[tail_row : tail_row + TAIL, :QT] = jnp.where(at, new, old).astype(jnp.int16)


def clear_tail(message_ref, tail_row):
    message_ref[tail_row : tail_row + TAIL, :] = jnp.zeros((TAIL, CB), jnp.int16)


def decode(message_ref, tile, tail_row):
    shape = (TAIL, QT)
    tail = message_ref[tail_row : tail_row + TAIL, :QT].astype(jnp.float32)
    at = lax.broadcasted_iota(jnp.int32, shape, 0) == tile
    along = jnp.sum(jnp.where(at, tail, 0.0), axis=0, keepdims=True)
    exponent = jnp.sum(jnp.where(diagonal(), along, 0.0), axis=1, keepdims=True)
    codes = message_ref[pl.ds(aligned(tile * QT), QT), :].astype(jnp.float32)
    return codes * jnp.exp2(exponent)


HALF = 2 * QT
HALF_MSG = jax.ShapeDtypeStruct((HALF + TAIL, CB), jnp.int16)
TILE_MSG = jax.ShapeDtypeStruct((QT + TAIL, CB), jnp.int16)
HALF_RAW = jax.ShapeDtypeStruct((HALF, CB), jnp.float32)


SUPER = SIDE * QT
COMMON = 3


def super_sums(tiles, q_ref, keys_ref, hot_ref, scores_ref, total_ref):
    width = q_ref.shape[-1]
    sharpness = float(width) ** 0.5 * math.log2(math.e)
    queries = q_ref[...].reshape(SUPER, width)

    def scores(at):
        cosine = lax.dot_general(
            queries, keys_ref[at, :], (((1,), (1,)), ((), ())), preferred_element_type=jnp.float32
        )
        scores_ref[:, at] = jnp.exp2(sharpness * cosine).astype(jnp.bfloat16)

    cut = COMMON * KT
    for t in range(COMMON):
        scores(pl.ds(t * KT, KT))
    total_ref[...] = jnp.dot(
        scores_ref[:, :cut], hot_ref[:cut, :], preferred_element_type=jnp.float32
    )

    @pl.when(tiles > COMMON)
    def _():
        def step(t, carry):
            scores(pl.ds(aligned(t * KT), KT))
            return carry

        def rest(i, carry):
            rows = pl.ds(aligned(i * HALF), HALF)
            total_ref[rows, :] += jnp.dot(
                scores_ref[rows, cut:], hot_ref[cut:, :], preferred_element_type=jnp.float32
            )
            return carry

        lax.fori_loop(COMMON, tiles, step, 0)
        lax.fori_loop(0, 2, rest, 0)


def sums(shifts, halves, coded, facts, queries, keys, hots, arrived=()):
    width = keys.shape[1]
    joined = len(arrived)

    def kernel(facts_ref, q_hbm, keys_ref, hot_ref, *rest):
        came, outs, next_ref = rest[:joined], rest[joined : joined + 4], rest[joined + 4]
        scratch = rest[joined + 5 :]
        q_ref, scores_ref, total_ref, came_ref, msg_ref, q_sems, came_sems, out_sems = scratch
        for at in range(4):
            next_ref[at] = facts_ref[at]

        def copy_queries(block, part):
            away = shifts[part // 2]
            inner = halves[part // 2] * 2 + part % 2
            outer = lax.rem(facts_ref[block] + away, SIDE)
            chunk = jnp.where(block == 0, outer * SIDE + inner, inner * SIDE + outer)
            return pltpu.make_async_copy(q_hbm.at[chunk], q_ref.at[block, part], q_sems.at[block, part])

        def copy_came(at):
            return pltpu.make_async_copy(came[at], came_ref.at[at], came_sems.at[at])

        def copy_out(at):
            source = msg_ref.at[at] if coded else total_ref.at[at // 2, pl.ds(at % 2 * HALF, HALF), :]
            return pltpu.make_async_copy(source, outs[at], out_sems.at[at])

        for block in range(2):
            for part in range(SIDE):
                copy_queries(block, part).start()
        for at in range(joined):
            copy_came(at).start()
        scores_ref[:, COMMON * KT :] = jnp.zeros((SUPER, CAP - COMMON * KT), jnp.bfloat16)
        if coded:
            for at in range(4):
                clear_tail(msg_ref.at[at], HALF)

        def run(block, carry):
            for part in range(SIDE):
                copy_queries(block, part).wait()
            super_sums(
                facts_ref[2 + block],
                q_ref.at[block],
                keys_ref.at[pl.ds(aligned(block * CAP), CAP), :],
                hot_ref.at[pl.ds(aligned(block * CAP), CAP), :],
                scores_ref,
                total_ref.at[block],
            )
            if joined:
                @pl.when(block == 0)
                def _():
                    for at in range(joined):
                        copy_came(at).wait()

            if joined or coded:
                def body(t, carry):
                    rows = pl.ds(aligned(t * QT), QT)
                    at = 2 * block + t // 2
                    values = total_ref[block, rows, :]
                    if joined:
                        values += decode(came_ref.at[at], t % 2, HALF)
                    if coded:
                        encode(values, msg_ref.at[at], t % 2, HALF)
                    else:
                        total_ref[block, rows, :] = values
                    return carry

                lax.fori_loop(0, SIDE, body, 0)
            for at in range(4):
                @pl.when(block == at // 2)
                def _(at=at):
                    copy_out(at).start()
            return carry

        lax.fori_loop(0, 2, run, 0)
        for at in range(4):
            copy_out(at).wait()

    vmem, smem = pl.BlockSpec(memory_space=pltpu.VMEM), pl.BlockSpec(memory_space=pltpu.SMEM)
    anywhere = pl.BlockSpec(memory_space=pl.ANY)
    return pl.pallas_call(
        kernel,
        in_specs=[smem, anywhere, vmem, vmem] + [anywhere] * joined,
        out_specs=[anywhere] * 4 + [smem],
        out_shape=[HALF_MSG if coded else HALF_RAW] * 4 + [jax.ShapeDtypeStruct((4,), jnp.int32)],
        scratch_shapes=[
            pltpu.VMEM((2, SIDE, QT, width), jnp.bfloat16),
            pltpu.VMEM((SUPER, CAP), jnp.bfloat16),
            pltpu.VMEM((2, SUPER, CB), jnp.float32),
            pltpu.VMEM((4,) + HALF_MSG.shape, jnp.int16),
            pltpu.VMEM((4,) + HALF_MSG.shape, jnp.int16),
            pltpu.SemaphoreType.DMA((2, SIDE)),
            pltpu.SemaphoreType.DMA((4,)),
            pltpu.SemaphoreType.DMA((4,)),
        ],
        compiler_params=params(),
        cost_estimate=pl.CostEstimate(
            flops=2 * 4 * HALF * CAP * (width + CB),
            bytes_accessed=8 * HALF * width,
            transcendentals=2 * HALF * CAP,
        ),
        name="sums",
    )(facts, queries, keys, hots, *arrived)


def turn(place, low, high, low_came, high_came):
    def kernel(place_ref, low_hbm, high_hbm, low_msg, high_msg, own_hbm, plus_hbm, far_hbm, minus_hbm, *scratch):
        raw_ref, came_ref, msg_ref, own_ref, raw_sems, came_sems, out_sems = scratch

        def loads(half):
            raw, came = ((low_hbm, low_msg), (high_hbm, high_msg))[half]
            return (
                pltpu.make_async_copy(raw, raw_ref.at[half], raw_sems.at[half]),
                pltpu.make_async_copy(came, came_ref.at[half], came_sems.at[half]),
            )

        for half in range(2):
            for load in loads(half):
                load.start()
        for k in range(3):
            clear_tail(msg_ref.at[k], QT)
        for half in range(2):
            for load in loads(half):
                load.wait()

        def values(k):
            tile = lax.rem(place_ref[0] + k, SIDE)
            half, at = tile // 2, tile % 2
            return raw_ref[half, pl.ds(aligned(at * QT), QT), :] + decode(came_ref.at[half], at, HALF)

        def body(i, carry):
            k = jnp.where(i == 0, 2, jnp.where(i == 1, 1, 3))
            encode(values(k), msg_ref.at[i], 0, QT)
            return carry

        outs = [
            pltpu.make_async_copy(msg_ref.at[i], out, out_sems.at[i])
            for i, out in enumerate((far_hbm, plus_hbm, minus_hbm))
        ]
        outs.append(pltpu.make_async_copy(own_ref, own_hbm, out_sems.at[3]))
        lax.fori_loop(0, 3, body, 0)
        for out in outs[:3]:
            out.start()
        own_ref[...] = values(0)
        outs[3].start()
        for out in outs:
            out.wait()

    anywhere = pl.BlockSpec(memory_space=pl.ANY)
    return pl.pallas_call(
        kernel,
        in_specs=[pl.BlockSpec(memory_space=pltpu.SMEM)] + [anywhere] * 4,
        out_specs=[anywhere] * 4,
        out_shape=[jax.ShapeDtypeStruct((QT, CB), jnp.float32), TILE_MSG, TILE_MSG, TILE_MSG],
        scratch_shapes=[
            pltpu.VMEM((2, HALF, CB), jnp.float32),
            pltpu.VMEM((2,) + HALF_MSG.shape, jnp.int16),
            pltpu.VMEM((3,) + TILE_MSG.shape, jnp.int16),
            pltpu.VMEM((QT, CB), jnp.float32),
            pltpu.SemaphoreType.DMA((2,)),
            pltpu.SemaphoreType.DMA((2,)),
            pltpu.SemaphoreType.DMA((4,)),
        ],
        compiler_params=params(),
        cost_estimate=pl.CostEstimate(flops=40 * QT * CB, bytes_accessed=40 * QT * CB, transcendentals=0),
        name="turn",
    )(place, low, high, low_came, high_came)


def close(text, own_a, msgs_a, own_b, msgs_b):
    def kernel(text_ref, *rest):
        own, msgs = rest[0:2], (rest[2:5], rest[5:8])
        logits_ref, stats_ref = rest[8:]
        for block in range(2):
            total = own[block][...]
            for msg in msgs[block]:
                total += decode(msg, 0, QT)
            at = slice(block * CB, block * CB + CB)
            logits_ref[:, at] = text_ref[:, at] + total
        logits = logits_ref[...]
        largest = jnp.max(logits, axis=1, keepdims=True)
        total = jnp.sum(jnp.exp(logits - largest), axis=1, keepdims=True)
        eye = diagonal()
        stats_ref[0:1, :] = jnp.sum(jnp.where(eye, largest, 0.0), axis=0, keepdims=True)
        stats_ref[1:2, :] = jnp.sum(jnp.where(eye, total, 0.0), axis=0, keepdims=True)

    return pl.pallas_call(
        kernel,
        out_shape=[
            jax.ShapeDtypeStruct((QT, 2 * CB), jnp.float32),
            jax.ShapeDtypeStruct((2, QT), jnp.float32),
        ],
        compiler_params=params(),
        cost_estimate=pl.CostEstimate(flops=30 * QT * CB, bytes_accessed=40 * QT * CB, transcendentals=QT * CB),
        name="close",
    )(text, own_a, own_b, *msgs_a, *msgs_b)


def finish(logits, stats):
    def kernel(logits_ref, stats_ref, out_ref):
        largest = jnp.max(stats_ref[:, 0, :], axis=0, keepdims=True)
        total = jnp.sum(stats_ref[:, 1, :] * jnp.exp(stats_ref[:, 0, :] - largest), axis=0, keepdims=True)
        eye = diagonal()
        largest = jnp.sum(jnp.where(eye, largest, 0.0), axis=1, keepdims=True)
        shift = jnp.sum(jnp.where(eye, jnp.log(total), 0.0), axis=1, keepdims=True)
        out_ref[...] = logits_ref[...] - largest - shift

    return pl.pallas_call(
        kernel,
        out_shape=jax.ShapeDtypeStruct(logits.shape, jnp.float32),
        compiler_params=params(),
        name="finish",
    )(logits, stats)


def shifted(dx, dz):
    return [
        (x * SIDE + z, (x + dx) % SIDE * SIDE + (z + dz) % SIDE) for x in range(SIDE) for z in range(SIDE)
    ]


def send(message, dx, dz):
    return lax.ppermute(message, "cache", shifted(dx, dz))


def per_device(queries, cache_keys, labels, prototypes):
    width = queries.shape[1]
    own = lax.axis_index("cache")
    x, z = own // SIDE, own % SIDE
    low = lax.axis_index("cls") * (2 * CB)

    unit_queries = unit_small(queries)
    gathered = lax.all_gather(unit_queries, ("cache", "cls"), axis=0, tiled=True)

    order = lax.sort(labels * 16384 + lax.iota(jnp.int32, labels.shape[0]), is_stable=False)
    start = jnp.sum((labels < low).astype(jnp.int32))
    middle = jnp.sum((labels < low + CB).astype(jnp.int32))
    stop = jnp.sum((labels < low + 2 * CB).astype(jnp.int32))
    padded = jnp.concatenate([order, jnp.zeros((CAP,), jnp.int32)])
    picked = jnp.concatenate(
        [lax.dynamic_slice(padded, (start,), (CAP,)), lax.dynamic_slice(padded, (middle,), (CAP,))]
    )
    counts = jnp.stack([middle - start, stop - middle])
    place = lax.iota(jnp.int32, 2 * CAP)
    block = place // CAP
    valid = place - block * CAP < jnp.where(block == 0, counts[0], counts[1])
    local = jnp.where(valid, picked // 16384 - low - block * CB, -1)
    rows = jnp.take(cache_keys, picked % 16384, axis=0, mode="clip")
    text = text_scale * lax.dot_general(
        lax.all_gather(unit_queries, "cls", axis=0, tiled=True),
        prototypes,
        (((1,), (1,)), ((), ())),
        preferred_element_type=jnp.float32,
    )
    rows, text = lax.optimization_barrier((rows, text))
    tiles = jnp.maximum((counts + KT - 1) // KT, COMMON)
    facts = jnp.stack([x, z, tiles[0], tiles[1]]).astype(jnp.int32)
    keys, hots, facts = prepare(facts, rows, local)
    gathered, facts = lax.optimization_barrier((gathered, facts))
    q3 = gathered.reshape(SIDE * SIDE, QT, width)

    def run(facts, shifts, halves, coded, arrived=()):
        *parts, facts = sums(shifts, halves, coded, facts, q3, keys, hots, arrived)
        return parts, facts

    def send_all(parts):
        a_right, a_left, b_right, b_left = parts
        return send(a_right, 1, 0), send(a_left, -1, 0), send(b_right, 0, 1), send(b_left, 0, -1)

    far, facts = run(facts, (2, 2), (0, 1), True)
    far = send_all(far)
    free, facts = run(facts, (1, 3), (1, 0), True)
    free = send_all(free)
    full, facts = run(facts, (1, 3), (0, 1), True, far)
    full = send_all(full)
    a_low, a_high, b_low, b_high = run(
        facts, (0, 0), (0, 1), False, (free[1], free[0], free[3], free[2])
    )[0]

    own_a, a_plus, a_far, a_minus = turn(z[None], a_low, a_high, full[0], full[1])
    own_b, b_plus, b_far, b_minus = turn(x[None], b_low, b_high, full[2], full[3])
    a_msgs = send(a_far, 0, 2), send(a_plus, 0, 1), send(a_minus, 0, -1)
    b_msgs = send(b_far, 2, 0), send(b_plus, 1, 0), send(b_minus, -1, 0)

    logits, stats = close(text, own_a, a_msgs, own_b, b_msgs)
    return finish(logits, lax.all_gather(stats, "cls"))


def solution(mesh):
    placed = (P(("cache", "cls"), None), P("cache", None), P("cache"), P("cls", None))
    return jax.shard_map(
        per_device, mesh=mesh, in_specs=placed, out_specs=P("cache", "cls"), check_vma=False
    )
```

```python
import math

import jax
import jax.numpy as jnp
from jax import lax
from jax.experimental import pallas as pl
from jax.experimental.pallas import tpu as pltpu
from jax.sharding import PartitionSpec as P

text_scale = 100.0
epsilon = 1e-06
SIDE = 4
CB = 640
CAP = 1280
QT = 256
KT = 256
TAIL = 16


def params(mib=36):
    return pltpu.CompilerParams(vmem_limit_bytes=mib * 1024 * 1024)


def unit_rows(matrix):
    widened = matrix.astype(jnp.float32)
    return (widened / jnp.sqrt(jnp.sum(widened * widened, axis=1, keepdims=True) + epsilon)).astype(
        jnp.bfloat16
    )


def prepare_kernel(facts_ref, rows_ref, labels_ref, unit_ref, hot_ref, next_ref):
    for at in range(4):
        next_ref[at] = facts_ref[at]
    unit_ref[...] = unit_rows(rows_ref[...])
    classes = lax.broadcasted_iota(jnp.int32, (KT, CB), 1)
    labels = jnp.sum(jnp.where(diagonal(), labels_ref[0], 0), axis=1, keepdims=True)
    hot_ref[...] = jnp.where(labels == classes, 1.0, 0.0).astype(jnp.bfloat16)


def prepare(facts, rows, labels):
    count, width = rows.shape
    return pl.pallas_call(
        prepare_kernel,
        grid=(count // KT,),
        in_specs=[
            pl.BlockSpec(memory_space=pltpu.SMEM),
            pl.BlockSpec((KT, width), lambda i: (i, 0)),
            pl.BlockSpec((1, 1, KT), lambda i: (i, 0, 0)),
        ],
        out_specs=[
            pl.BlockSpec((KT, width), lambda i: (i, 0)),
            pl.BlockSpec((KT, CB), lambda i: (i, 0)),
            pl.BlockSpec(memory_space=pltpu.SMEM),
        ],
        out_shape=[
            jax.ShapeDtypeStruct((count, width), jnp.bfloat16),
            jax.ShapeDtypeStruct((count, CB), jnp.bfloat16),
            jax.ShapeDtypeStruct((4,), jnp.int32),
        ],
        compiler_params=params(),
        cost_estimate=pl.CostEstimate(flops=count * width * 4, bytes_accessed=count * width * 6, transcendentals=count),
        name="prepare",
    )(facts, rows, labels.reshape(count // KT, 1, KT))


def unit_kernel(rows_ref, unit_ref):
    unit_ref[...] = unit_rows(rows_ref[...])


def unit_small(rows):
    return pl.pallas_call(
        unit_kernel,
        out_shape=jax.ShapeDtypeStruct(rows.shape, jnp.bfloat16),
        compiler_params=params(),
        name="unit",
    )(rows)


def aligned(value):
    return pl.multiple_of(value, QT)


def diagonal():
    shape = (QT, QT)
    return lax.broadcasted_iota(jnp.int32, shape, 0) == lax.broadcasted_iota(jnp.int32, shape, 1)


def encode(values, message_ref, tile, tail_row):
    largest = jnp.maximum(jnp.max(values, axis=1, keepdims=True), 1e-30)
    exponent = jnp.ceil(jnp.log2(largest) - 14.99)
    codes = (values * jnp.exp2(-exponent) + 0.5).astype(jnp.int32)
    message_ref[pl.ds(aligned(tile * QT), QT), :] = codes.astype(jnp.int16)
    along = jnp.sum(jnp.where(diagonal(), exponent, 0.0), axis=0, keepdims=True)
    shape = (TAIL, QT)
    old = message_ref[tail_row : tail_row + TAIL, :QT].astype(jnp.int32)
    new = jnp.broadcast_to(along, shape).astype(jnp.int32)
    at = lax.broadcasted_iota(jnp.int32, shape, 0) == tile
    message_ref[tail_row : tail_row + TAIL, :QT] = jnp.where(at, new, old).astype(jnp.int16)


def clear_tail(message_ref, tail_row):
    message_ref[tail_row : tail_row + TAIL, :] = jnp.zeros((TAIL, CB), jnp.int16)


def decode(message_ref, tile, tail_row):
    shape = (TAIL, QT)
    tail = message_ref[tail_row : tail_row + TAIL, :QT].astype(jnp.float32)
    at = lax.broadcasted_iota(jnp.int32, shape, 0) == tile
    along = jnp.sum(jnp.where(at, tail, 0.0), axis=0, keepdims=True)
    exponent = jnp.sum(jnp.where(diagonal(), along, 0.0), axis=1, keepdims=True)
    codes = message_ref[pl.ds(aligned(tile * QT), QT), :].astype(jnp.float32)
    return codes * jnp.exp2(exponent)


HALF = 2 * QT
HALF_MSG = jax.ShapeDtypeStruct((HALF + TAIL, CB), jnp.int16)
TILE_MSG = jax.ShapeDtypeStruct((QT + TAIL, CB), jnp.int16)
HALF_RAW = jax.ShapeDtypeStruct((HALF, CB), jnp.float32)


SUPER = SIDE * QT
COMMON = 3


def super_sums(tiles, q_ref, keys_ref, hot_ref, scores_ref, total_ref):
    width = q_ref.shape[-1]
    sharpness = float(width) ** 0.5 * math.log2(math.e)
    queries = q_ref[...].reshape(SUPER, width)

    def step(t, carry):
        at = pl.ds(aligned(t * KT), KT)
        cosine = lax.dot_general(
            queries, keys_ref[at, :], (((1,), (1,)), ((), ())), preferred_element_type=jnp.float32
        )
        scores_ref[:, at] = jnp.exp2(sharpness * cosine).astype(jnp.bfloat16)
        return carry

    lax.fori_loop(0, tiles, step, 0)
    cut = COMMON * KT
    total_ref[...] = jnp.dot(
        scores_ref[:, :cut], hot_ref[:cut, :], preferred_element_type=jnp.float32
    )

    @pl.when(tiles > COMMON)
    def _():
        total_ref[...] += jnp.dot(
            scores_ref[:, cut:], hot_ref[cut:, :], preferred_element_type=jnp.float32
        )


def sums(shifts, halves, coded, facts, queries, keys, hots, arrived=()):
    width = keys.shape[1]
    joined = len(arrived)

    def kernel(facts_ref, q_hbm, keys_ref, hot_ref, *rest):
        came, outs, next_ref = rest[:joined], rest[joined : joined + 4], rest[joined + 4]
        scratch = rest[joined + 5 :]
        q_ref, scores_ref, total_ref, came_ref, msg_ref, q_sems, came_sems, out_sems = scratch
        for at in range(4):
            next_ref[at] = facts_ref[at]

        def copy_queries(block, part):
            away = shifts[part // 2]
            inner = halves[part // 2] * 2 + part % 2
            outer = lax.rem(facts_ref[block] + away, SIDE)
            chunk = jnp.where(block == 0, outer * SIDE + inner, inner * SIDE + outer)
            return pltpu.make_async_copy(q_hbm.at[chunk], q_ref.at[block, part], q_sems.at[block, part])

        def copy_came(at):
            return pltpu.make_async_copy(came[at], came_ref.at[at], came_sems.at[at])

        def copy_out(at):
            source = msg_ref.at[at] if coded else total_ref.at[at // 2, pl.ds(at % 2 * HALF, HALF), :]
            return pltpu.make_async_copy(source, outs[at], out_sems.at[at])

        for part in range(SIDE):
            copy_queries(0, part).start()
        scores_ref[:, COMMON * KT :] = jnp.zeros((SUPER, CAP - COMMON * KT), jnp.bfloat16)
        if coded:
            for at in range(4):
                clear_tail(msg_ref.at[at], HALF)

        def run(block, carry):
            for part in range(SIDE):
                copy_queries(block, part).wait()

            @pl.when(block == 0)
            def _():
                for part in range(SIDE):
                    copy_queries(1, part).start()
                for at in range(joined):
                    copy_came(at).start()

            super_sums(
                facts_ref[2 + block],
                q_ref.at[block],
                keys_ref.at[pl.ds(aligned(block * CAP), CAP), :],
                hot_ref.at[pl.ds(aligned(block * CAP), CAP), :],
                scores_ref,
                total_ref.at[block],
            )
            if joined:
                @pl.when(block == 0)
                def _():
                    for at in range(joined):
                        copy_came(at).wait()

            if joined or coded:
                def body(t, carry):
                    rows = pl.ds(aligned(t * QT), QT)
                    at = 2 * block + t // 2
                    values = total_ref[block, rows, :]
                    if joined:
                        values += decode(came_ref.at[at], t % 2, HALF)
                    if coded:
                        encode(values, msg_ref.at[at], t % 2, HALF)
                    else:
                        total_ref[block, rows, :] = values
                    return carry

                lax.fori_loop(0, SIDE, body, 0)
            for at in range(4):
                @pl.when(block == at // 2)
                def _(at=at):
                    copy_out(at).start()
            return carry

        lax.fori_loop(0, 2, run, 0)
        for at in range(4):
            copy_out(at).wait()

    vmem, smem = pl.BlockSpec(memory_space=pltpu.VMEM), pl.BlockSpec(memory_space=pltpu.SMEM)
    anywhere = pl.BlockSpec(memory_space=pl.ANY)
    return pl.pallas_call(
        kernel,
        in_specs=[smem, anywhere, vmem, vmem] + [anywhere] * joined,
        out_specs=[anywhere] * 4 + [smem],
        out_shape=[HALF_MSG if coded else HALF_RAW] * 4 + [jax.ShapeDtypeStruct((4,), jnp.int32)],
        scratch_shapes=[
            pltpu.VMEM((2, SIDE, QT, width), jnp.bfloat16),
            pltpu.VMEM((SUPER, CAP), jnp.bfloat16),
            pltpu.VMEM((2, SUPER, CB), jnp.float32),
            pltpu.VMEM((4,) + HALF_MSG.shape, jnp.int16),
            pltpu.VMEM((4,) + HALF_MSG.shape, jnp.int16),
            pltpu.SemaphoreType.DMA((2, SIDE)),
            pltpu.SemaphoreType.DMA((4,)),
            pltpu.SemaphoreType.DMA((4,)),
        ],
        compiler_params=params(),
        cost_estimate=pl.CostEstimate(
            flops=2 * 4 * HALF * CAP * (width + CB),
            bytes_accessed=8 * HALF * width,
            transcendentals=2 * HALF * CAP,
        ),
        name="sums",
    )(facts, queries, keys, hots, *arrived)


def turn(place, low, high, low_came, high_came):
    def kernel(place_ref, low_hbm, high_hbm, low_msg, high_msg, own_hbm, plus_hbm, far_hbm, minus_hbm, *scratch):
        raw_ref, came_ref, msg_ref, own_ref, raw_sems, came_sems, out_sems = scratch

        def loads(half):
            raw, came = ((low_hbm, low_msg), (high_hbm, high_msg))[half]
            return (
                pltpu.make_async_copy(raw, raw_ref.at[half], raw_sems.at[half]),
                pltpu.make_async_copy(came, came_ref.at[half], came_sems.at[half]),
            )

        for half in range(2):
            for load in loads(half):
                load.start()
        for k in range(3):
            clear_tail(msg_ref.at[k], QT)
        for half in range(2):
            for load in loads(half):
                load.wait()

        def values(k):
            tile = lax.rem(place_ref[0] + k, SIDE)
            half, at = tile // 2, tile % 2
            return raw_ref[half, pl.ds(aligned(at * QT), QT), :] + decode(came_ref.at[half], at, HALF)

        def body(i, carry):
            k = jnp.where(i == 0, 2, jnp.where(i == 1, 1, 3))
            encode(values(k), msg_ref.at[i], 0, QT)
            return carry

        outs = [
            pltpu.make_async_copy(msg_ref.at[i], out, out_sems.at[i])
            for i, out in enumerate((far_hbm, plus_hbm, minus_hbm))
        ]
        outs.append(pltpu.make_async_copy(own_ref, own_hbm, out_sems.at[3]))
        lax.fori_loop(0, 3, body, 0)
        for out in outs[:3]:
            out.start()
        own_ref[...] = values(0)
        outs[3].start()
        for out in outs:
            out.wait()

    anywhere = pl.BlockSpec(memory_space=pl.ANY)
    return pl.pallas_call(
        kernel,
        in_specs=[pl.BlockSpec(memory_space=pltpu.SMEM)] + [anywhere] * 4,
        out_specs=[anywhere] * 4,
        out_shape=[jax.ShapeDtypeStruct((QT, CB), jnp.float32), TILE_MSG, TILE_MSG, TILE_MSG],
        scratch_shapes=[
            pltpu.VMEM((2, HALF, CB), jnp.float32),
            pltpu.VMEM((2,) + HALF_MSG.shape, jnp.int16),
            pltpu.VMEM((3,) + TILE_MSG.shape, jnp.int16),
            pltpu.VMEM((QT, CB), jnp.float32),
            pltpu.SemaphoreType.DMA((2,)),
            pltpu.SemaphoreType.DMA((2,)),
            pltpu.SemaphoreType.DMA((4,)),
        ],
        compiler_params=params(),
        cost_estimate=pl.CostEstimate(flops=40 * QT * CB, bytes_accessed=40 * QT * CB, transcendentals=0),
        name="turn",
    )(place, low, high, low_came, high_came)


def close(text, own_a, msgs_a, own_b, msgs_b):
    def kernel(text_ref, *rest):
        own, msgs = rest[0:2], (rest[2:5], rest[5:8])
        logits_ref, stats_ref = rest[8:]
        for block in range(2):
            total = own[block][...]
            for msg in msgs[block]:
                total += decode(msg, 0, QT)
            at = slice(block * CB, block * CB + CB)
            logits_ref[:, at] = text_ref[:, at] + total
        logits = logits_ref[...]
        largest = jnp.max(logits, axis=1, keepdims=True)
        total = jnp.sum(jnp.exp(logits - largest), axis=1, keepdims=True)
        eye = diagonal()
        stats_ref[0:1, :] = jnp.sum(jnp.where(eye, largest, 0.0), axis=0, keepdims=True)
        stats_ref[1:2, :] = jnp.sum(jnp.where(eye, total, 0.0), axis=0, keepdims=True)

    return pl.pallas_call(
        kernel,
        out_shape=[
            jax.ShapeDtypeStruct((QT, 2 * CB), jnp.float32),
            jax.ShapeDtypeStruct((2, QT), jnp.float32),
        ],
        compiler_params=params(),
        cost_estimate=pl.CostEstimate(flops=30 * QT * CB, bytes_accessed=40 * QT * CB, transcendentals=QT * CB),
        name="close",
    )(text, own_a, own_b, *msgs_a, *msgs_b)


def finish(logits, stats):
    def kernel(logits_ref, stats_ref, out_ref):
        largest = jnp.max(stats_ref[:, 0, :], axis=0, keepdims=True)
        total = jnp.sum(stats_ref[:, 1, :] * jnp.exp(stats_ref[:, 0, :] - largest), axis=0, keepdims=True)
        eye = diagonal()
        largest = jnp.sum(jnp.where(eye, largest, 0.0), axis=1, keepdims=True)
        shift = jnp.sum(jnp.where(eye, jnp.log(total), 0.0), axis=1, keepdims=True)
        out_ref[...] = logits_ref[...] - largest - shift

    return pl.pallas_call(
        kernel,
        out_shape=jax.ShapeDtypeStruct(logits.shape, jnp.float32),
        compiler_params=params(),
        name="finish",
    )(logits, stats)


def shifted(dx, dz):
    return [
        (x * SIDE + z, (x + dx) % SIDE * SIDE + (z + dz) % SIDE) for x in range(SIDE) for z in range(SIDE)
    ]


def send(message, dx, dz):
    return lax.ppermute(message, "cache", shifted(dx, dz))


def per_device(queries, cache_keys, labels, prototypes):
    width = queries.shape[1]
    own = lax.axis_index("cache")
    x, z = own // SIDE, own % SIDE
    low = lax.axis_index("cls") * (2 * CB)

    unit_queries = unit_small(queries)
    gathered = lax.all_gather(unit_queries, ("cache", "cls"), axis=0, tiled=True)

    order = lax.sort(labels * 16384 + lax.iota(jnp.int32, labels.shape[0]), is_stable=False)
    start = jnp.sum((labels < low).astype(jnp.int32))
    middle = jnp.sum((labels < low + CB).astype(jnp.int32))
    stop = jnp.sum((labels < low + 2 * CB).astype(jnp.int32))
    padded = jnp.concatenate([order, jnp.zeros((CAP,), jnp.int32)])
    picked = jnp.concatenate(
        [lax.dynamic_slice(padded, (start,), (CAP,)), lax.dynamic_slice(padded, (middle,), (CAP,))]
    )
    counts = jnp.stack([middle - start, stop - middle])
    place = lax.iota(jnp.int32, 2 * CAP)
    block = place // CAP
    valid = place - block * CAP < jnp.where(block == 0, counts[0], counts[1])
    local = jnp.where(valid, picked // 16384 - low - block * CB, -1)
    rows = jnp.take(cache_keys, picked % 16384, axis=0, mode="clip")
    text = text_scale * lax.dot_general(
        lax.all_gather(unit_queries, "cls", axis=0, tiled=True),
        prototypes,
        (((1,), (1,)), ((), ())),
        preferred_element_type=jnp.float32,
    )
    rows, text = lax.optimization_barrier((rows, text))
    tiles = jnp.maximum((counts + KT - 1) // KT, COMMON)
    facts = jnp.stack([x, z, tiles[0], tiles[1]]).astype(jnp.int32)
    keys, hots, facts = prepare(facts, rows, local)
    gathered, facts = lax.optimization_barrier((gathered, facts))
    q3 = gathered.reshape(SIDE * SIDE, QT, width)

    def run(facts, shifts, halves, coded, arrived=()):
        *parts, facts = sums(shifts, halves, coded, facts, q3, keys, hots, arrived)
        return parts, facts

    def send_all(parts):
        a_right, a_left, b_right, b_left = parts
        return send(a_right, 1, 0), send(a_left, -1, 0), send(b_right, 0, 1), send(b_left, 0, -1)

    far, facts = run(facts, (2, 2), (0, 1), True)
    far = send_all(far)
    free, facts = run(facts, (1, 3), (1, 0), True)
    free = send_all(free)
    full, facts = run(facts, (1, 3), (0, 1), True, far)
    full = send_all(full)
    a_low, a_high, b_low, b_high = run(
        facts, (0, 0), (0, 1), False, (free[1], free[0], free[3], free[2])
    )[0]

    own_a, a_plus, a_far, a_minus = turn(z[None], a_low, a_high, full[0], full[1])
    own_b, b_plus, b_far, b_minus = turn(x[None], b_low, b_high, full[2], full[3])
    a_msgs = send(a_far, 0, 2), send(a_plus, 0, 1), send(a_minus, 0, -1)
    b_msgs = send(b_far, 2, 0), send(b_plus, 1, 0), send(b_minus, -1, 0)

    logits, stats = close(text, own_a, a_msgs, own_b, b_msgs)
    return finish(logits, lax.all_gather(stats, "cls"))


def solution(mesh):
    placed = (P(("cache", "cls"), None), P("cache", None), P("cache"), P("cls", None))
    return jax.shard_map(
        per_device, mesh=mesh, in_specs=placed, out_specs=P("cache", "cls"), check_vma=False
    )
```
